128 devices in a mesh: ctx: 16 (over y_hi, z, core), chan: 8 (over y_lo, x).
Axes of the slice: x: 4, y: 4 (y_hi: 2, y_lo: 2; y = y_hi * 2 + y_lo), z: 4, core: 2. Of those that a mesh axis runs over, the one named last changes fastest.
Arguments:
- frames: bfloat16 [2, 18432, 1536], P(None, 'ctx'), may hold values from -6 to 6
- ln_gain: float32 [1536], replicated, may hold values from 0.5 to 1.5
- ln_bias: float32 [1536], replicated, may hold values from -3 to 3
- w_in: bfloat16 [1536, 2, 1536], P('ctx', None, 'chan'), may hold values from -0.15625 to 0.15625
- w_depth: float32 [31, 1536], P(None, 'chan'), may hold values from -1 to 1
- bn_gain: float32 [1536], P('chan'), may hold values from 0.1 to 1.9
- bn_bias: float32 [1536], P('chan'), may hold values from -3 to 3
- w_out: bfloat16 [1536, 1536], P('ctx', 'chan'), may hold values from -0.15625 to 0.15625
- lengths: int32 [2], replicated, may hold values from 4608 to 18432, as said below
- grad_out: bfloat16 [2, 18432, 1536], P(None, 'ctx'), may hold values from -6 to 6
Outputs:
- block_out: bfloat16 [2, 18432, 1536], P(None, 'ctx', 'chan')
- grad_frames: bfloat16 [2, 18432, 1536], P(None, 'ctx', 'chan')
- grad_w_in: float32 [1536, 2, 1536], P('ctx', None, 'chan')
- grad_w_out: float32 [1536, 1536], P('ctx', 'chan')
- grad_w_depth: float32 [31, 1536], P(None, 'chan')
- grad_bn: float32 [2, 1536], P(None, 'chan')
- grad_ln: float32 [2, 1536], P(None, 'chan')
The draws below stay inside these ranges and needn't reach their ends.
Inputs may be any that keep to these rules, and one draw needn't show every extreme that they name: `lengths`: recording 0 always has all 18432 frames valid.
All inputs are finite; a program needn't handle non-finite values.
Results may differ from the reference program's by a relative error of at most 0.018.
Values may be sent and summed in bfloat16 or wider, within the bound.
No kernel may reach another device: no remote copies, remote signals or barrier semaphores. Data moves between devices by JAX's collectives and lax.ppermute only.
A program may use at most 192 MiB of HBM per device.

```python
import jax
import jax.numpy as jnp
from jax import lax

D = 1536
K = 31
B = 2
SEQ = 18432


def draw_lengths(key, part):
    others = jax.random.randint(key, (B,), SEQ // 4, SEQ + 1, dtype=jnp.int32)
    leading = jnp.arange(B, dtype=jnp.int32) == 0
    return jnp.where(leading, SEQ, others).astype(jnp.int32)


def level_of(key, shape, pieces, least, top_value):
    def one(dim, blocks):
        draws = jax.random.uniform(jax.random.fold_in(jax.random.fold_in(key, 6), dim), (blocks,), jnp.float32, least / len(pieces), top_value / len(pieces))
        return jnp.repeat(jnp.exp(draws), shape[dim] // blocks).reshape((-1,) + (1,) * (len(shape) - dim - 1))

    loudness = one(*pieces[0])
    for cut in pieces[1:]:
        loudness = loudness * one(*cut)
    return loudness


def bell_draw(own_key, dims, scale, most, cuts=(), held_as=jnp.bfloat16):
    gain = level_of(own_key, dims, cuts, -0.22, 0.18) if cuts else 1.0
    values = jax.random.normal(own_key, dims, jnp.float32) * scale * gain
    return jnp.minimum(jnp.maximum(values, -most), most).astype(held_as)


def setup_inputs(seed: int = 0) -> dict:
    splits = jax.random.split(jax.random.key(seed), 11)
    frames = bell_draw(splits[0], (B, SEQ, D), 1.0, 6.0, ((1, 16),))
    ln_gain = jnp.clip(1.0 + 0.1 * jax.random.normal(splits[1], (D,), jnp.float32), 0.5, 1.5)
    ln_bias = bell_draw(splits[2], (D,), 0.5, 3.0, (), jnp.float32)
    w_in = bell_draw(splits[3], (D, 2, D), D ** -0.5, 0.15625, ((0, 16), (2, 8)))
    w_depth = bell_draw(splits[4], (K, D), K ** -0.5, 1.0, ((1, 8),), jnp.float32)
    bn_gain = jnp.clip(1.0 + 0.18 * jax.random.normal(splits[5], (D,), jnp.float32), 0.1, 1.9)
    bn_bias = bell_draw(splits[6], (D,), 0.5, 3.0, ((0, 8),), jnp.float32)
    w_out = bell_draw(splits[7], (D, D), D ** -0.5, 0.15625, ((0, 16), (1, 8)))
    lengths = draw_lengths(jax.random.fold_in(splits[10], 71), 0)
    grad_out = bell_draw(splits[9], (B, SEQ, D), 1.0, 6.0, ((1, 16),))
    return dict(frames=frames, ln_gain=ln_gain, ln_bias=ln_bias, w_in=w_in, w_depth=w_depth, bn_gain=bn_gain, bn_bias=bn_bias, w_out=w_out, lengths=lengths, grad_out=grad_out)


epsilon = 1e-05

def frame_mask(lengths, length):
    position = jnp.arange(length, dtype=jnp.int32)
    return (position[None, :] < lengths[:, None]).astype(jnp.float32)[:, :, None]

def reference(frames, ln_gain, ln_bias, w_in, w_depth, bn_gain, bn_bias, w_out, lengths, grad_out):
    records, length, model_width = frames.shape
    tap_count = w_depth.shape[0]
    margin = (tap_count - 1) // 2
    total_rows = records * length
    valid_mask = frame_mask(lengths, length)
    frame_count = jnp.sum(lengths.astype(jnp.float32))
    inputs = frames.astype(jnp.float32)
    centred = inputs - lax.optimization_barrier(jnp.mean(inputs, axis=-1, keepdims=True))
    ln_rstd = lax.rsqrt(lax.optimization_barrier(jnp.mean(centred * centred, axis=-1, keepdims=True)) + epsilon)
    ln_hat = centred * ln_rstd
    normed = (ln_hat * ln_gain + ln_bias).astype(jnp.bfloat16)
    normed_rows = normed.reshape(total_rows, model_width)
    w_in_flat = w_in.reshape(model_width, 2 * model_width)
    projected = jnp.dot(normed_rows, w_in_flat, preferred_element_type=jnp.float32)
    projected = projected.reshape(records, length, 2, model_width)
    values = projected[:, :, 0]
    gate_vals = jax.nn.sigmoid(projected[:, :, 1])
    glu_out = (values * gate_vals * valid_mask).astype(jnp.bfloat16)
    padded = jnp.pad(glu_out.astype(jnp.float32), ((0, 0), (margin, margin), (0, 0)))
    depth_out = jnp.zeros((records, length, model_width), jnp.float32)
    for offset in range(tap_count):
        depth_out = depth_out + padded[:, offset:offset + length] * w_depth[offset]
    bn_mean = lax.optimization_barrier(jnp.sum(depth_out * valid_mask, axis=(0, 1))) / frame_count
    bn_cent = (depth_out - bn_mean) * valid_mask
    bn_rstd = lax.rsqrt(lax.optimization_barrier(jnp.sum(bn_cent * bn_cent, axis=(0, 1))) / frame_count + epsilon)
    bn_hat = (depth_out - bn_mean) * bn_rstd
    bn_out = bn_hat * bn_gain + bn_bias
    swish_gate = jax.nn.sigmoid(bn_out)
    activated = (bn_out * swish_gate * valid_mask).astype(jnp.bfloat16)
    act_rows = activated.reshape(total_rows, model_width)
    proj_out = lax.dot_general(act_rows, w_out, (((1,), (1,)), ((), ())), preferred_element_type=jnp.float32)
    block_out = (inputs.reshape(total_rows, model_width) + proj_out).astype(jnp.bfloat16)
    block_out = block_out.reshape(records, length, model_width)
    grad_rows = grad_out.reshape(total_rows, model_width)
    grad_w_out = lax.dot_general(grad_rows, act_rows, (((0,), (0,)), ((), ())), preferred_element_type=jnp.float32)
    grad_act = jnp.dot(grad_rows, w_out, preferred_element_type=jnp.float32).reshape(records, length, model_width)
    grad_bn_out = grad_act * valid_mask * (swish_gate * (1.0 + bn_out * (1.0 - swish_gate)))
    gain_sum = lax.optimization_barrier(jnp.sum(grad_bn_out * bn_hat, axis=(0, 1)))
    bias_sum = lax.optimization_barrier(jnp.sum(grad_bn_out, axis=(0, 1)))
    grad_depth = valid_mask * (bn_gain * bn_rstd) * (grad_bn_out - (bias_sum + bn_hat * gain_sum) / frame_count)
    grad_w_depth = jnp.stack([lax.optimization_barrier(jnp.sum(grad_depth * padded[:, offset:offset + length], axis=(0, 1))) for offset in range(tap_count)])
    grad_padded = jnp.pad(grad_depth, ((0, 0), (margin, margin), (0, 0)))
    grad_glu = jnp.zeros((records, length, model_width), jnp.float32)
    for offset in range(tap_count):
        begin_at = tap_count - 1 - offset
        grad_glu = grad_glu + grad_padded[:, begin_at:begin_at + length] * w_depth[offset]
    grad_glu = grad_glu * valid_mask
    grad_values = grad_glu * gate_vals
    grad_gates = grad_glu * values * gate_vals * (1.0 - gate_vals)
    grad_proj = jnp.stack([grad_values, grad_gates], axis=2).astype(jnp.bfloat16).reshape(total_rows, 2 * model_width)
    grad_w_in = lax.dot_general(normed_rows, grad_proj, (((0,), (0,)), ((), ())), preferred_element_type=jnp.float32)
    grad_w_in = grad_w_in.reshape(model_width, 2, model_width)
    grad_normed = lax.dot_general(grad_proj, w_in_flat, (((1,), (1,)), ((), ())), preferred_element_type=jnp.float32)
    grad_normed = grad_normed.reshape(records, length, model_width)
    grad_ln = jnp.stack([lax.optimization_barrier(jnp.sum(grad_normed * ln_hat, axis=(0, 1))), lax.optimization_barrier(jnp.sum(grad_normed, axis=(0, 1)))])
    scaled = grad_normed * ln_gain
    first_mean = lax.optimization_barrier(jnp.mean(scaled, axis=-1, keepdims=True))
    second_mean = lax.optimization_barrier(jnp.mean(scaled * ln_hat, axis=-1, keepdims=True))
    grad_frames = (ln_rstd * (scaled - first_mean - ln_hat * second_mean) + grad_out.astype(jnp.float32)).astype(jnp.bfloat16)
    grad_bn = jnp.stack([gain_sum, bias_sum])
    return (block_out, grad_frames, grad_w_in, grad_w_out, grad_w_depth, grad_bn, grad_ln)
```

```python
import functools

import jax
import jax.numpy as jnp
from jax import lax
from jax.experimental import pallas as pl
from jax.experimental.pallas import tpu as pltpu
from jax.sharding import Mesh
from jax.sharding import PartitionSpec as P

F32 = jnp.float32
BF16 = jnp.bfloat16
CTX = ("yh", "z", "c")
CHAN = ("yl", "x")
TIME = ("yh", "z", "c", "yl")
EPS = 1e-05
TAPS = 31
EDGE = 16
LIMIT = pltpu.CompilerParams(vmem_limit_bytes=50 * 1024 * 1024)

S_YL, S_X, S_PAIR, S_ODD, S_POS, S_LEN, S_Z, S_C, S_YH = 0, 1, 2, 3, 4, 5, 7, 8, 9

SMEM = pl.BlockSpec(memory_space=pltpu.SMEM)
VMEM = pl.BlockSpec(memory_space=pltpu.VMEM)
ANY = pl.BlockSpec(memory_space=pl.ANY)


def cost(flops, nbytes):
    return pl.CostEstimate(flops=flops // 50, bytes_accessed=nbytes // 50, transcendentals=0)


def sds(shape, dtype):
    return jax.ShapeDtypeStruct(shape, dtype)


def nt(a, b):
    return lax.dot_general(a, b, (((1,), (1,)), ((), ())), preferred_element_type=F32)


def ln_body(s, fr, gain, bias, normed, stat):
    v = fr[0].astype(F32)
    mean = jnp.mean(v, axis=-1, keepdims=True)
    cen = v - mean
    rstd = lax.rsqrt(jnp.mean(cen * cen, axis=-1, keepdims=True) + EPS)
    stat[0, :, 0:1] = mean
    stat[0, :, 1:2] = rstd

    @pl.when(pl.program_id(0) == 0)
    def _():
        normed[...] = (cen * rstd * gain[...] + bias[...]).astype(BF16)


def layer_norm(s, frames, gain, bias):
    recs, length, width = frames.shape
    blk = length // 4

    def rows(h, b, i, s):
        return (b, jnp.where(h == 0, s[S_YL], 1 - s[S_YL]) * 2 + i, 0)

    return pl.pallas_call(
        ln_body,
        grid_spec=pltpu.PrefetchScalarGridSpec(
            num_scalar_prefetch=1,
            grid=(2, recs, 2),
            in_specs=[
                pl.BlockSpec((1, blk, width), rows),
                pl.BlockSpec((1, width), lambda h, b, i, s: (0, 0)),
                pl.BlockSpec((1, width), lambda h, b, i, s: (0, 0)),
            ],
            out_specs=[
                pl.BlockSpec((blk, width), lambda h, b, i, s: (jnp.where(h == 0, b * 2 + i, 2 * recs - 1), 0)),
                pl.BlockSpec((1, blk, 2), rows),
            ],
        ),
        out_shape=[sds((recs * length // 2, width), BF16), sds((recs, length, 2), F32)],
        compiler_params=LIMIT,
        cost_estimate=cost(recs * length * width * 10, 4 * recs * length * width),
        name="layer_norm",
    )(s, frames, gain[None], bias[None])


def place(s, pieces, out, sem):
    z, c = s[S_Z], s[S_C]
    n = pieces[0].shape[1]
    copies = []
    for r in range(4):
        for k in range(2):
            for h in range(2):
                row = (h * 4 + lax.rem(z + r, 4)) * 2 + (c if k == 0 else 1 - c)
                cp = pltpu.make_async_copy(pieces[2 * r + k].at[h], out.at[pl.ds(pl.multiple_of(row * n, n), n)], sem.at[len(copies)])
                cp.start()
                copies.append(cp)
    for cp in copies:
        cp.wait()


def proj_body(s, normed, *refs, blk, half):
    pieces, (proj, glu, w, sem) = refs[:8], refs[8:]
    i = pl.program_id(0)

    @pl.when(i == 0)
    def _():
        place(s, pieces, w, sem)

    p = jnp.dot(normed[...], w[...], preferred_element_type=F32)
    proj[...] = p
    n = p.shape[1] // 2
    b = i // (half // blk)
    t = s[S_POS] + (i % (half // blk)) * blk + lax.broadcasted_iota(jnp.int32, (blk, 1), 0)
    valid = (t < s[S_LEN + b]).astype(F32)
    glu[...] = (p[:, :n] * jax.nn.sigmoid(p[:, n:]) * valid).astype(BF16)


def project(s, normed, pieces, half):
    rows, width = normed.shape
    _, shard, n2 = pieces[0].shape
    blk = half // 2
    return pl.pallas_call(
        functools.partial(proj_body, blk=blk, half=half),
        grid_spec=pltpu.PrefetchScalarGridSpec(
            num_scalar_prefetch=1,
            grid=(rows // blk,),
            in_specs=[pl.BlockSpec((blk, width), lambda i, s: (i, 0))] + [ANY] * 8,
            out_specs=[
                pl.BlockSpec((blk, n2), lambda i, s: (i, 0)),
                pl.BlockSpec((blk, n2 // 2), lambda i, s: (i, 0)),
                pl.BlockSpec((16 * shard, n2), lambda i, s: (0, 0)),
            ],
            scratch_shapes=[pltpu.SemaphoreType.DMA((16,))],
        ),
        out_shape=[sds((rows, n2), F32), sds((rows, n2 // 2), BF16), sds((16 * shard, n2), BF16)],
        compiler_params=LIMIT,
        cost_estimate=cost(2 * rows * width * n2, 2 * rows * width + 5 * rows * n2),
        name="project",
    )(s, normed, *pieces)


def gact_body(s, go, *refs):
    pieces, (out, w, sem) = refs[:8], refs[8:]

    @pl.when((pl.program_id(0) == 0) & (pl.program_id(1) == 0))
    def _():
        place(s, pieces, w, sem)

    out[0] = jnp.dot(go[0], w[...], preferred_element_type=F32)


def grad_act(s, grad_out, pieces):
    recs, length, width = grad_out.shape
    _, shard, n = pieces[0].shape
    blk = length // 4
    return pl.pallas_call(
        gact_body,
        grid_spec=pltpu.PrefetchScalarGridSpec(
            num_scalar_prefetch=1,
            grid=(recs, 2),
            in_specs=[pl.BlockSpec((1, blk, width), lambda b, i, s: (b, s[S_YL] * 2 + i, 0))] + [ANY] * 8,
            out_specs=[
                pl.BlockSpec((1, blk, n), lambda b, i, s: (b, i, 0)),
                pl.BlockSpec((16 * shard, n), lambda b, i, s: (0, 0)),
            ],
            scratch_shapes=[pltpu.SemaphoreType.DMA((16,))],
        ),
        out_shape=[sds((recs, length // 2, n), F32), sds((16 * shard, n), BF16)],
        compiler_params=LIMIT,
        cost_estimate=cost(recs * length * width * n, recs * length * (width + 2 * n)),
        name="grad_act",
    )(s, grad_out, *pieces)


def tn(a, b):
    return lax.dot_general(a, b, (((0,), (0,)), ((), ())), preferred_element_type=F32)


def wgrad_body(s, normed, gp, go, act, w, mine, theirs, tu, colsum):
    shard = mine.shape[1]
    n2 = gp.shape[1]

    @pl.when(pl.program_id(0) == 0)
    def _():
        colsum[...] = jnp.sum(gp[...].astype(F32), axis=0, keepdims=True)

    g_in = tn(normed[...], gp[...])
    wide = w[...].astype(F32)
    tu[:, 0:1] = jnp.sum(wide * g_in, axis=1, keepdims=True)
    tu[:, 1:2] = jnp.sum(wide * colsum[...], axis=1, keepdims=True)
    g_out = tn(go[...].reshape(-1, go.shape[2]), act[...])
    first = s[S_C] == 0
    for i in range(2):
        r0 = 2 * i * shard
        for g, cols in ((g_in, slice(0, n2)), (g_out, slice(n2, n2 + g_out.shape[1]))):
            top, low = g[r0 : r0 + shard], g[r0 + shard : r0 + 2 * shard]
            mine[i, :, cols] = jnp.where(first, top, low).astype(BF16)
            theirs[i, :, cols] = jnp.where(first, low, top).astype(BF16)


def weight_grads(s, normed, gp, grad_out, act, w):
    rows, width = normed.shape
    n2, n = gp.shape[1], act.shape[1]
    recs, length, _ = grad_out.shape
    blk = width // 4
    shard = width // 16
    part = pl.BlockSpec((2, shard, n2 + n), lambda k, s: (k, 0, 0))
    return pl.pallas_call(
        wgrad_body,
        grid_spec=pltpu.PrefetchScalarGridSpec(
            num_scalar_prefetch=1,
            grid=(4,),
            in_specs=[
                pl.BlockSpec((rows, blk), lambda k, s: (0, k)),
                pl.BlockSpec((rows, n2), lambda k, s: (0, 0)),
                pl.BlockSpec((recs, length // 2, blk), lambda k, s: (0, s[S_YL], k)),
                pl.BlockSpec((rows, n), lambda k, s: (0, 0)),
                pl.BlockSpec((blk, n2), lambda k, s: (k, 0)),
            ],
            out_specs=[part, part, pl.BlockSpec((blk, 2), lambda k, s: (k, 0))],
            scratch_shapes=[pltpu.VMEM((1, n2), F32)],
        ),
        out_shape=[sds((8, shard, n2 + n), BF16)] * 2 + [sds((width, 2), F32)],
        compiler_params=LIMIT,
        cost_estimate=cost(2 * rows * width * (n2 + n), 4 * rows * width),
        name="weight_grads",
    )(s, normed, gp, grad_out, act, w)


def core_body(s, mine, got, *outs):
    for r, out in enumerate(outs):
        q = lax.rem(s[S_Z] + r, 4)
        for h in range(2):
            out[h] = (mine[h * 4 + q].astype(F32) + got[h * 4 + q].astype(F32)).astype(BF16)


def core_sum(s, mine, got):
    _, shard, n = mine.shape
    return pl.pallas_call(
        core_body,
        in_specs=[SMEM, VMEM, VMEM],
        out_specs=[VMEM] * 4,
        out_shape=[sds((2, shard, n), BF16)] * 4,
        compiler_params=LIMIT,
        cost_estimate=cost(16 * shard * n, 48 * shard * n),
        name="core_sum",
    )(s, mine, got)


def ring_body(s, p0, p1, p2, p3, own, to_yl, to_yh, to_xx):
    n = own.shape[1] // 3

    def total(h):
        return p0[h].astype(F32) + p1[h].astype(F32) + p2[h].astype(F32) + p3[h].astype(F32)

    first = s[S_YL] == 0
    for v, here, there in ((total(s[S_YH]), own, to_yl), (total(1 - s[S_YH]), to_yh, to_xx)):
        for g in range(3):
            low, high = v[:, 2 * g * n : (2 * g + 1) * n], v[:, (2 * g + 1) * n : (2 * g + 2) * n]
            cols = slice(g * n, g * n + n)
            here[:, cols] = jnp.where(first, low, high).astype(here.dtype)
            there[:, cols] = jnp.where(first, high, low).astype(there.dtype)


def ring_sum(s, parts):
    _, shard, n = parts[0].shape
    return pl.pallas_call(
        ring_body,
        in_specs=[SMEM] + [VMEM] * 4,
        out_specs=[VMEM] * 4,
        out_shape=[sds((shard, n // 2), F32)] + [sds((shard, n // 2), BF16)] * 3,
        compiler_params=LIMIT,
        cost_estimate=cost(8 * shard * n, 24 * shard * n),
        name="ring_sum",
    )(s, *parts)


def fill(pad, mid, lo, hi):
    recs, half = mid.shape[0], mid.shape[1]
    for b in range(recs):
        for j in range(mid.shape[2] // 128):
            lanes = slice(128 * j, 128 * j + 128)
            pad[b, j, 0:EDGE, :] = lo[b, :, lanes].astype(F32)
            pad[b, j, EDGE : EDGE + half, :] = mid[b, :, lanes].astype(F32)
            pad[b, j, EDGE + half :, :] = hi[b, :, lanes].astype(F32)


def tile_mask(start, rows, length):
    t = start + lax.broadcasted_iota(jnp.int32, (rows, 128), 0)
    return ((t >= 0) & (t < length)).astype(F32)


def local_count(s, half):
    n = jnp.int32(0)
    for b in range(2):
        n = n + jnp.clip(s[S_LEN + b] - s[S_POS], 0, half)
    return jnp.maximum(n, 1).astype(F32)


def fold(v):
    return jnp.sum(v.reshape(-1, 8, v.shape[1]), axis=0)


TILE = 96


def conv_body(s, glu, lo, hi, w, depth, stat, pad):
    recs, half, chans = glu.shape
    fill(pad, glu, lo, hi)
    count = local_count(s, half)
    for j in range(chans // 128):
        lanes = slice(128 * j, 128 * j + 128)
        total = jnp.zeros((8, 128), F32)
        for b in range(recs):

            def step(i, total, b=b):
                r0 = pl.multiple_of(i * TILE, 8)
                acc = jnp.zeros((TILE, 128), F32)
                for o in range(TAPS):
                    acc = acc + pad[b, j, pl.ds(r0 + o + 1, TILE), :] * w[o : o + 1, lanes]
                depth[b, pl.ds(r0, TILE), lanes] = acc
                return total + fold(acc * tile_mask(s[S_POS] + r0, TILE, s[S_LEN + b]))

            total = lax.fori_loop(0, half // TILE, step, total)
        mean = jnp.sum(total, axis=0, keepdims=True) / count
        spread = jnp.zeros((8, 128), F32)
        for b in range(recs):

            def step2(i, spread, b=b):
                r0 = pl.multiple_of(i * TILE, 8)
                d = (depth[b, pl.ds(r0, TILE), lanes] - mean) * tile_mask(s[S_POS] + r0, TILE, s[S_LEN + b])
                return spread + fold(d * d)

            spread = lax.fori_loop(0, half // TILE, step2, spread)
        stat[0:1, lanes] = mean
        stat[0:1, slice(chans + 128 * j, chans + 128 * j + 128)] = jnp.sum(spread, axis=0, keepdims=True)


def conv(s, glu, lo, hi, w):
    recs, half, chans = glu.shape
    return pl.pallas_call(
        conv_body,
        in_specs=[SMEM, VMEM, VMEM, VMEM, VMEM],
        out_specs=[VMEM, VMEM],
        out_shape=[sds((recs, half, chans), F32), sds((1, 2 * chans), F32)],
        scratch_shapes=[pltpu.VMEM((recs, chans // 128, half + 2 * EDGE, 128), F32)],
        compiler_params=LIMIT,
        cost_estimate=cost(recs * half * chans * 62 * 50, recs * half * chans * 6),
        name="conv",
    )(s, glu, lo, hi, w)


def bn_stats(s, got, half, chans):
    dev = got.shape[0]
    start = half * lax.broadcasted_iota(jnp.int32, (dev, 1), 0)
    n = jnp.zeros((dev, 1), jnp.int32)
    for b in range(2):
        n = n + jnp.clip(s[S_LEN + b] - start, 0, half)
    n = n.astype(F32)
    count = (s[S_LEN].astype(F32)) + (s[S_LEN + 1].astype(F32))
    means, spread = got[:, :chans], got[:, chans:]
    mean = jnp.sum(n * means, axis=0, keepdims=True) / count
    var = jnp.sum(spread + n * (means - mean) ** 2, axis=0, keepdims=True) / count
    return mean, lax.rsqrt(var + EPS), count


def act_body(s, depth, gact, got, prm, act, gbo, sums, bn, *, half):
    b = pl.program_id(0)
    i = pl.program_id(1)
    rows, chans = depth.shape[1], depth.shape[2]

    @pl.when((b == 0) & (i == 0))
    def _():
        mean, rstd, _ = bn_stats(s, got, half, chans)
        bn[0:1, :] = mean
        bn[1:2, :] = rstd
        sums[...] = jnp.zeros_like(sums)

    for j in range(chans // 128):
        lanes = slice(128 * j, 128 * j + 128)
        high = slice(chans + 128 * j, chans + 128 * j + 128)
        mean, rstd = bn[0:1, lanes], bn[1:2, lanes]
        gain, bias = prm[31:32, lanes], prm[32:33, lanes]
        one = jnp.zeros((8, 128), F32)
        two = jnp.zeros((8, 128), F32)
        for k in range(rows // TILE):
            r = slice(k * TILE, k * TILE + TILE)
            hat = (depth[0, r, lanes] - mean) * rstd
            out = hat * gain + bias
            g = jax.nn.sigmoid(out)
            m = tile_mask(s[S_POS] + i * rows + k * TILE, TILE, s[S_LEN + b])
            act[0, r, lanes] = (out * g * m).astype(BF16)
            gb = gact[0, r, lanes] * m * (g * (1.0 + out * (1.0 - g)))
            gbo[0, r, lanes] = gb
            one = one + fold(gb * hat)
            two = two + fold(gb)
        sums[0:1, lanes] += jnp.sum(one, axis=0, keepdims=True)
        sums[0:1, high] += jnp.sum(two, axis=0, keepdims=True)


def activate(s, depth, gact, got, prm):
    recs, half, chans = depth.shape
    blk = half // 2
    block = pl.BlockSpec((1, blk, chans), lambda b, i, s: (b, i, 0))
    whole = lambda a: pl.BlockSpec(a.shape, lambda b, i, s: (0, 0))
    return pl.pallas_call(
        functools.partial(act_body, half=half),
        grid_spec=pltpu.PrefetchScalarGridSpec(
            num_scalar_prefetch=1,
            grid=(recs, 2),
            in_specs=[block, block, whole(got), whole(prm)],
            out_specs=[block, block, pl.BlockSpec((1, 2 * chans), lambda b, i, s: (0, 0)), pl.BlockSpec((8, chans), lambda b, i, s: (0, 0))],
        ),
        out_shape=[sds(depth.shape, BF16), sds(depth.shape, F32), sds((1, 2 * chans), F32), sds((8, chans), F32)],
        compiler_params=LIMIT,
        cost_estimate=cost(recs * half * chans * 200, recs * half * chans * 14),
        name="activate",
    )(s, depth, gact, got, prm)


def back_body(s, depth, gbo, lo, hi, sums, bn, prm, proj, gd_out, gp, pad):
    recs, half, chans = depth.shape
    total = jnp.sum(sums[...], axis=0, keepdims=True)
    count = (s[S_LEN].astype(F32)) + (s[S_LEN + 1].astype(F32))
    pos = s[S_POS]
    for j in range(chans // 128):
        lanes = slice(128 * j, 128 * j + 128)
        high = slice(chans + 128 * j, chans + 128 * j + 128)
        gsum, bsum = total[:, lanes], total[:, high]
        mean, rstd = bn[0:1, lanes], bn[1:2, lanes]
        scale = prm[31:32, lanes] * rstd

        def grad(dep, gb, start, length):
            m = tile_mask(start, dep.shape[0], length)
            hat = (dep - mean) * rstd
            return m * scale * (gb - (bsum + hat * gsum) / count)

        for b in range(recs):
            length = s[S_LEN + b]
            pad[b, j, 0:EDGE, :] = grad(lo[0, b, :, lanes], lo[1, b, :, lanes], pos - EDGE, length)
            pad[b, j, EDGE + half :, :] = grad(hi[0, b, :, lanes], hi[1, b, :, lanes], pos + half, length)

            def step(i, _, b=b, length=length):
                r0 = pl.multiple_of(i * TILE, 8)
                v = grad(depth[b, pl.ds(r0, TILE), lanes], gbo[b, pl.ds(r0, TILE), lanes], pos + r0, length)
                pad[b, j, pl.ds(pl.multiple_of(r0 + EDGE, 8), TILE), :] = v
                gd_out[b, pl.ds(r0, TILE), lanes] = v
                return 0

            lax.fori_loop(0, half // TILE, step, 0)

            def step2(i, _, b=b, length=length):
                r0 = pl.multiple_of(i * TILE, 16)
                acc = jnp.zeros((TILE, 128), F32)
                for o in range(TAPS):
                    acc = acc + pad[b, j, pl.ds(r0 + TAPS - o, TILE), :] * prm[o : o + 1, lanes]
                acc = acc * tile_mask(pos + r0, TILE, length)
                val = proj[b, pl.ds(r0, TILE), lanes]
                g = jax.nn.sigmoid(proj[b, pl.ds(r0, TILE), high])
                gp[b, pl.ds(r0, TILE), lanes] = (acc * g).astype(BF16)
                gp[b, pl.ds(r0, TILE), high] = (acc * val * g * (1.0 - g)).astype(BF16)
                return 0

            lax.fori_loop(0, half // TILE, step2, 0)


def backward(s, depth, gbo, lo, hi, sums, bn, prm, proj):
    recs, half, chans = depth.shape
    return pl.pallas_call(
        back_body,
        in_specs=[SMEM] + [VMEM] * 8,
        out_specs=[VMEM, VMEM],
        out_shape=[sds(depth.shape, F32), sds((recs, half, 2 * chans), BF16)],
        scratch_shapes=[pltpu.VMEM((recs, chans // 128, half + 2 * EDGE, 128), F32)],
        compiler_params=LIMIT,
        cost_estimate=cost(recs * half * chans * 62 * 50, recs * half * chans * 24),
        name="backward",
    )(s, depth, gbo, lo, hi, sums, bn, prm, proj)


def taps_body(gd, glu, lo, hi, gwd, pad):
    recs, half, chans = glu.shape
    fill(pad, glu, lo, hi)
    gwd[...] = jnp.zeros_like(gwd)
    for j in range(chans // 128):
        lanes = slice(128 * j, 128 * j + 128)
        accs = tuple(jnp.zeros((8, 128), F32) for _ in range(TAPS))
        for b in range(recs):

            def step(i, accs, b=b):
                r0 = pl.multiple_of(i * 16, 16)
                new = list(accs)
                for k in range(2):
                    g = gd[b, pl.ds(r0 + 8 * k, 8), lanes]
                    for o in range(TAPS):
                        new[o] = new[o] + g * pad[b, j, pl.ds(r0 + 8 * k + o + 1, 8), :]
                return tuple(new)

            accs = lax.fori_loop(0, half // 16, step, accs)
        for o in range(TAPS):
            gwd[o : o + 1, lanes] = jnp.sum(accs[o], axis=0, keepdims=True)


def taps_grad(gd, glu, lo, hi):
    recs, half, chans = glu.shape
    return pl.pallas_call(
        taps_body,
        in_specs=[VMEM] * 4,
        out_specs=VMEM,
        out_shape=sds((32, chans), F32),
        scratch_shapes=[pltpu.VMEM((recs, chans // 128, half + 2 * EDGE, 128), F32)],
        compiler_params=LIMIT,
        cost_estimate=cost(recs * half * chans * 62 * 50, recs * half * chans * 20),
        name="taps_grad",
    )(gd, glu, lo, hi)


def rows_body(gp, proj, gw, rs):
    recs, half, _ = gp.shape
    gsum = gw[0:1, :] + gw[1:2, :]
    shift = gw[2:3, :] + gw[3:4, :]
    for b in range(recs):

        def step2(i, _, b=b):
            r0 = pl.multiple_of(i * 48, 16)
            g = gp[b, pl.ds(r0, 48), :].astype(F32)
            rs[b, pl.ds(r0, 48), 0:1] = jnp.sum(g * gsum, axis=1, keepdims=True)
            rs[b, pl.ds(r0, 48), 1:2] = jnp.sum(g * (proj[b, pl.ds(r0, 48), :] - shift), axis=1, keepdims=True)
            return 0

        lax.fori_loop(0, half // 48, step2, 0)


def row_sums(gp, proj, gw):
    recs, half, n2 = gp.shape
    return pl.pallas_call(
        rows_body,
        in_specs=[VMEM] * 3,
        out_specs=VMEM,
        out_shape=sds((recs, half, 2), F32),
        compiler_params=LIMIT,
        cost_estimate=cost(recs * half * n2 * 8, recs * half * n2 * 6),
        name="row_sums",
    )(gp, proj, gw)


def through_body(gain, bias, w, out):
    def split(v):
        top = v.astype(BF16).astype(F32)
        return top, v - top

    g1, g2 = split(gain[...])
    b1, b2 = split(bias[...])
    row = lax.broadcasted_iota(jnp.int32, (16, gain.shape[1]), 0)
    v = jnp.where(row == 0, g1, jnp.where(row == 1, g2, jnp.where(row == 2, b1, jnp.where(row == 3, b2, 0.0))))
    out[...] = jnp.dot(v.astype(BF16), w[...], preferred_element_type=F32)


def through(gain, bias, w):
    return pl.pallas_call(
        through_body,
        in_specs=[VMEM] * 3,
        out_specs=VMEM,
        out_shape=sds((16, w.shape[1]), F32),
        compiler_params=LIMIT,
        cost_estimate=cost(32 * w.shape[0] * w.shape[1], 2 * w.shape[0] * w.shape[1]),
        name="through",
    )(gain[None], bias[None], w)


def blocks_body(s, lhs, w, *refs, jobs, adds):
    plus, outs, cat = refs[:adds], refs[adds:-1], refs[-1]
    n, half = w.shape[1], lhs.shape[1]
    last = None
    for rec, r, to, at in jobs:
        if r != last:
            dest = lax.rem(s[S_X] + r, 4)
            cat[0:n, :] = w[dest]
            cat[n:, :] = w[dest + 4]
            last = r
        v = nt(lhs[rec], cat[...])
        if adds:
            v = v + plus[to][0:half, :].astype(F32)
        outs[to][at * half : (at + 1) * half, :] = v.astype(BF16)


def blocks(s, lhs, w8, jobs, plus=()):
    recs, half, depth = lhs.shape
    n = w8.shape[1]
    each = len(jobs) // 2
    return pl.pallas_call(
        functools.partial(blocks_body, jobs=jobs, adds=len(plus)),
        in_specs=[SMEM] + [VMEM] * (2 + len(plus)),
        out_specs=[VMEM] * 2,
        out_shape=[sds((each * half, 2 * n), BF16)] * 2,
        scratch_shapes=[pltpu.VMEM((2 * n, depth), BF16)],
        compiler_params=LIMIT,
        cost_estimate=cost(4 * half * depth * n * len(jobs), 4 * half * depth + 16 * n * depth),
        name="blocks",
    )(s, lhs, w8, *plus)


def finish_body(s, lhs, w, up, down, last_a, last_b, keep, give, cat):
    n, half = w.shape[1], lhs.shape[1]
    cat[0:n, :] = w[s[S_X]]
    cat[n:, :] = w[s[S_X] + 4]
    first = s[S_YL] == 0
    for rec, (one, two) in enumerate(((last_a, down), (last_b, up))):
        v = nt(lhs[rec], cat[...]) + one[...].astype(F32) + two[half:, :].astype(F32)
        low, high = v[:, :n], v[:, n:]
        keep[rec] = jnp.where(first, low, high)
        give[:, rec * n : (rec + 1) * n] = jnp.where(first, high, low).astype(BF16)


def finish(s, lhs, w8, parts):
    recs, half, depth = lhs.shape
    n = w8.shape[1]
    return pl.pallas_call(
        finish_body,
        in_specs=[SMEM] + [VMEM] * 6,
        out_specs=[VMEM] * 2,
        out_shape=[sds((recs, half, n), F32), sds((half, recs * n), BF16)],
        scratch_shapes=[pltpu.VMEM((2 * n, depth), BF16)],
        compiler_params=LIMIT,
        cost_estimate=cost(8 * half * depth * n, 4 * half * depth + 16 * n * depth),
        name="finish",
    )(s, lhs, w8, *parts)


def hop(v, axis, by):
    n = lax.axis_size(axis)
    return lax.ppermute(v, axis, [(i, (i + by) % n) for i in range(n)])


def sum_start(s, lhs, w8):
    sent = blocks(s, lhs, w8, ((0, 2, 0, 0), (1, 2, 1, 0), (1, 1, 0, 1), (0, 3, 1, 1)))
    return (hop(sent[0], "x", 1), hop(sent[1], "x", -1)), sent[0]


def sum_middle(s, lhs, w8, got):
    sent = blocks(s, lhs, w8, ((0, 1, 0, 0), (1, 3, 1, 0)), got)
    return (hop(sent[0], "x", 1), hop(sent[1], "x", -1)), sent[0]


def sum_end(s, lhs, w8, got, last):
    keep, give = finish(s, lhs, w8, (*got, *last))
    return keep, hop(give, "yl", 1)


def after(values, *first):
    return lax.optimization_barrier((*values, *first))[: len(values)]


def pick(block, odd):
    n = block.shape[1] // 2
    return jnp.where(odd == 1, block[:, n:].astype(F32), block[:, :n].astype(F32))


def halves(s, keep, got):
    n = keep.shape[2]
    mine = keep[0]
    theirs = jnp.where(pl.program_id(0) == 0, got[:, :n].astype(F32), got[:, n:].astype(F32))
    first = s[S_YL] == 0
    return jnp.where(first, mine, theirs), jnp.where(first, theirs, mine)


def out_body(s, keep, got, fr, out):
    half = keep.shape[1]
    for h, v in enumerate(halves(s, keep, got)):
        rows = slice(h * half, h * half + half)
        out[0, rows, :] = (pick(fr[0, rows, :], s[S_ODD]) + v).astype(BF16)


def frames_body(s, keep, got, fr, go, stat, rs, gain, out):
    half = keep.shape[1]
    width = 8 * out.shape[2]
    for h, v in enumerate(halves(s, keep, got)):
        rows = slice(h * half, h * half + half)
        g = v * gain[...]
        mean, rstd = stat[0, rows, 0:1], stat[0, rows, 1:2]
        first, second = rs[h, 0, :, 0:1], rs[h, 0, :, 1:2]
        hat = (pick(fr[0, rows, :], s[S_ODD]) - mean) * rstd
        v = rstd * (g - first / width - hat * (second / width)) + pick(go[0, rows, :], s[S_ODD])
        out[0, rows, :] = v.astype(BF16)


def last_call(body, s, keep, got, wide, extra, extra_specs, name):
    recs, half, n = keep.shape
    cols = pl.BlockSpec((1, 2 * half, 2 * n), lambda b, s: (b, 0, s[S_PAIR]))
    return pl.pallas_call(
        body,
        grid_spec=pltpu.PrefetchScalarGridSpec(
            num_scalar_prefetch=1,
            grid=(recs,),
            in_specs=[
                pl.BlockSpec((1, half, n), lambda b, s: (b, 0, 0)),
                pl.BlockSpec((half, recs * n), lambda b, s: (0, 0)),
            ]
            + [cols] * len(wide)
            + extra_specs,
            out_specs=pl.BlockSpec((1, 2 * half, n), lambda b, s: (b, 0, 0)),
        ),
        out_shape=sds((recs, 2 * half, n), BF16),
        compiler_params=LIMIT,
        cost_estimate=cost(recs * half * n * 20, recs * half * n * 20),
        name=name,
    )(s, keep, got, *wide, *extra)


def spread(v, axes):
    n = lax.axis_size(axes)
    return lax.all_to_all(jnp.broadcast_to(v[None], (n, *v.shape)), axes, 0, 0, tiled=True)


def on_device(frames, ln_gain, ln_bias, w_in, w_depth, bn_gain, bn_bias, w_out, lengths, grad_out):
    recs, length, width = frames.shape
    shard, _, own = w_in.shape
    half = length // 2
    chans = 2 * own
    yh, z, c, yl, x = (lax.axis_index(a) for a in ("yh", "z", "c", "yl", "x"))
    ctx = (yh * 4 + z) * 2 + c
    chan = yl * 4 + x
    time = ctx * 2 + yl
    s = jnp.stack([yl, x, chan // 2, chan % 2, time * half, lengths[0], lengths[1], z, c, yh]).astype(jnp.int32)

    w3 = jnp.concatenate([w_in.reshape(shard, 2 * own), w_out], axis=1)
    w_yl = hop(w3, "yl", 1)
    w_yh = hop(w3, "yh", 1)
    w_xx = lax.ppermute(w3, ("yh", "yl"), [(i, 3 - i) for i in range(4)])

    def paired(a, b, g0, g1):
        lo, hi = jnp.where(yl == 0, a, b), jnp.where(yl == 0, b, a)
        cols = []
        for g in range(g0, g1):
            cols += [lo[:, g * own : (g + 1) * own], hi[:, g * own : (g + 1) * own]]
        return jnp.concatenate(cols, axis=1)

    def rows_two(g0, g1):
        same, other = paired(w3, w_yl, g0, g1), paired(w_yh, w_xx, g0, g1)
        return jnp.where(yh == 0, jnp.stack([same, other]), jnp.stack([other, same]))

    def gathered(v, first):
        pieces = []
        for r in range(4):
            p = v if r == 0 else hop(v, "z", -r)
            if first is not None:
                (p,) = after([p], first)
            pieces += [p, hop(p, "c", 1)]
        return pieces

    in_two = rows_two(0, 2)
    normed, stat = layer_norm(s, *after([frames, ln_gain, ln_bias], in_two))
    in_pieces = gathered(in_two, normed)
    out_pieces = gathered(*after([rows_two(2, 3)], *in_pieces), None)
    prm1 = jnp.concatenate([w_depth, bn_gain[None], bn_bias[None], jnp.zeros((7, own), F32)], axis=0)
    prm2 = hop(prm1, "yl", 1)
    prm = jnp.where(yl == 0, jnp.concatenate([prm1, prm2], axis=1), jnp.concatenate([prm2, prm1], axis=1))

    proj, glu, w_in_all = project(s, normed, in_pieces, half)
    w_in_8 = w_in_all.reshape(8, own, 2 * chans)
    glu = glu.reshape(recs, half, chans)
    proj = proj.reshape(recs, half, 2 * chans)
    devices = lax.axis_size(TIME)
    up = [(i, i + 1) for i in range(devices - 1)]
    down = [(i + 1, i) for i in range(devices - 1)]
    g_lo = lax.ppermute(glu[:, half - EDGE :], TIME, up)
    g_hi = lax.ppermute(glu[:, :EDGE], TIME, down)
    depth, bn_own = conv(s, glu, g_lo, g_hi, prm)
    bn_all = spread(bn_own, TIME).reshape(devices, 2 * chans)
    gact, w_out_all = grad_act(s, grad_out, out_pieces)
    w_out_8 = w_out_all.reshape(8, own, chans)
    act, gbo, sums_own, bn = activate(s, depth, gact, bn_all, prm)
    sums = spread(sums_own, TIME).reshape(devices, 2 * chans)
    e_lo = lax.ppermute(jnp.stack([depth[:, half - EDGE :], gbo[:, half - EDGE :]]), TIME, up)
    e_hi = lax.ppermute(jnp.stack([depth[:, :EDGE], gbo[:, :EDGE]]), TIME, down)

    out_first, sent = sum_start(s, act, w_out_8)
    g_w = through(*after([ln_gain, ln_bias, w_in_all], sent))
    depth, gbo = after([depth, gbo], sent, g_w)
    gd, gp = backward(s, depth, gbo, e_lo, e_hi, sums, bn, prm, proj)
    gn_first, sent = sum_start(s, gp, w_in_8)
    (act_m,) = after([act], sent)
    out_last, sent = sum_middle(s, act_m, w_out_8, out_first)
    (gp_a,) = after([gp], sent)
    rs = row_sums(gp_a, proj, g_w)
    (gp_a,) = after([gp_a], rs)
    mine, theirs, tu = weight_grads(
        s,
        normed,
        gp_a.reshape(recs * half, 2 * chans),
        grad_out,
        act.reshape(recs * half, chans),
        w_in_all,
    )
    (gp_m,) = after([gp], mine)
    gn_last, sent = sum_middle(s, gp_m, w_in_8, gn_first)
    (mine, rs) = after([mine, rs], sent)
    rs_all = spread(rs.transpose(2, 0, 1), CHAN).reshape(2, 4, 2, recs, half)
    rs_all = jnp.sum(rs_all, axis=1).transpose(0, 2, 3, 1)
    parts = core_sum(s, mine, hop(theirs, "c", 1))
    (act_e,) = after([act], parts[0])
    out_keep, out_got = sum_end(s, act_e, w_out_8, out_first, out_last)
    gd, glu = after([gd, glu], out_keep)
    gwd = taps_grad(gd, glu, g_lo, g_hi)
    block_out = last_call(out_body, s, out_keep, out_got, [frames], [], [], "block_out")
    (gp_e,) = after([gp], gwd)
    gn_keep, gn_got = sum_end(s, gp_e, w_in_8, gn_first, gn_last)

    own_gain = lax.dynamic_slice_in_dim(ln_gain, chan * own, own, 0)
    own_bias = lax.dynamic_slice_in_dim(ln_bias, chan * own, own, 0)
    grad_frames = last_call(
        frames_body,
        s,
        gn_keep,
        gn_got,
        [frames, grad_out],
        [stat, rs_all, own_gain[None]],
        [
            pl.BlockSpec((1, length, 2), lambda b, s: (b, 0, 0)),
            pl.BlockSpec((2, 1, half, 2), lambda b, s: (0, b, 0, 0)),
            pl.BlockSpec((1, own), lambda b, s: (0, 0)),
        ],
        "grad_frames",
    )

    parts = [parts[0]] + [hop(parts[r], "z", r) for r in range(1, 4)]
    g_fin, to_yl, to_yh, to_xx = ring_sum(s, parts)
    g_fin = g_fin + hop(to_yl, "yl", 1).astype(F32) + hop(to_yh, "yh", 1).astype(F32)
    g_fin = g_fin + lax.ppermute(to_xx, ("yh", "yl"), [(i, 3 - i) for i in range(4)]).astype(F32)
    grad_w_in = g_fin[:, : 2 * own].reshape(shard, 2, own)
    grad_w_out = g_fin[:, 2 * own :]

    tu = tu.T.reshape(2, 2, 4, own).transpose(1, 2, 0, 3)
    mine_x = (jnp.arange(4) == x).astype(F32)[None, :, None, None]
    taps4 = gwd[:TAPS].reshape(TAPS, 2, own).transpose(1, 0, 2)[:, None] * mine_x
    small = jnp.concatenate([taps4, tu], axis=2).reshape(8, TAPS + 2, own)
    small = jnp.sum(lax.all_to_all(small, CHAN, 0, 0, tiled=True), axis=0)
    small = jnp.sum(spread(small, CTX), axis=0)
    grad_w_depth = small[:TAPS]
    t, u = small[TAPS], small[TAPS + 1]
    grad_ln = jnp.stack([(t - own_bias * u) / own_gain, u])
    grad_bn = lax.dynamic_index_in_dim(jnp.sum(sums, axis=0).reshape(2, 2, own), yl, 1, False)
    return (block_out, grad_frames, grad_w_in, grad_w_out, grad_w_depth, grad_bn, grad_ln)


def solution(mesh):
    split = Mesh(mesh.devices.reshape(2, 4, 2, 2, 4), ("yh", "z", "c", "yl", "x"))
    placed = (
        P(None, CTX, None),
        P(),
        P(),
        P(CTX, None, CHAN),
        P(None, CHAN),
        P(CHAN),
        P(CHAN),
        P(CTX, CHAN),
        P(),
        P(None, CTX, None),
    )
    return jax.shard_map(
        on_device,
        mesh=split,
        in_specs=placed,
        out_specs=(
            P(None, CTX, CHAN),
            P(None, CTX, CHAN),
            P(CTX, None, CHAN),
            P(CTX, CHAN),
            P(None, CHAN),
            P(None, CHAN),
            P(None, CHAN),
        ),
        check_vma=False,
    )
```

```python
import functools

import jax
import jax.numpy as jnp
from jax import lax
from jax.experimental import pallas as pl
from jax.experimental.pallas import tpu as pltpu
from jax.sharding import Mesh
from jax.sharding import PartitionSpec as P

F32 = jnp.float32
BF16 = jnp.bfloat16
CTX = ("yh", "z", "c")
CHAN = ("yl", "x")
TIME = ("yh", "z", "c", "yl")
EPS = 1e-05
TAPS = 31
EDGE = 16
LIMIT = pltpu.CompilerParams(vmem_limit_bytes=50 * 1024 * 1024)

S_YL, S_X, S_PAIR, S_ODD, S_POS, S_LEN, S_Z, S_C, S_YH = 0, 1, 2, 3, 4, 5, 7, 8, 9

SMEM = pl.BlockSpec(memory_space=pltpu.SMEM)
VMEM = pl.BlockSpec(memory_space=pltpu.VMEM)
ANY = pl.BlockSpec(memory_space=pl.ANY)


def cost(flops, nbytes):
    return pl.CostEstimate(flops=flops // 50, bytes_accessed=nbytes // 50, transcendentals=0)


LONG = pl.CostEstimate(flops=0, bytes_accessed=100 * 1024 * 1024, transcendentals=0)


def sds(shape, dtype):
    return jax.ShapeDtypeStruct(shape, dtype)


def nt(a, b):
    return lax.dot_general(a, b, (((1,), (1,)), ((), ())), preferred_element_type=F32)


def ln_body(s, fr, gain, bias, normed, stat):
    v = fr[0].astype(F32)
    mean = jnp.mean(v, axis=-1, keepdims=True)
    cen = v - mean
    rstd = lax.rsqrt(jnp.mean(cen * cen, axis=-1, keepdims=True) + EPS)
    stat[0, :, 0:1] = mean
    stat[0, :, 1:2] = rstd

    @pl.when(pl.program_id(0) == 0)
    def _():
        normed[...] = (cen * rstd * gain[...] + bias[...]).astype(BF16)


def layer_norm(s, frames, gain, bias):
    recs, length, width = frames.shape
    blk = length // 4

    def rows(h, b, i, s):
        return (b, jnp.where(h == 0, s[S_YL], 1 - s[S_YL]) * 2 + i, 0)

    return pl.pallas_call(
        ln_body,
        grid_spec=pltpu.PrefetchScalarGridSpec(
            num_scalar_prefetch=1,
            grid=(2, recs, 2),
            in_specs=[
                pl.BlockSpec((1, blk, width), rows),
                pl.BlockSpec((1, width), lambda h, b, i, s: (0, 0)),
                pl.BlockSpec((1, width), lambda h, b, i, s: (0, 0)),
            ],
            out_specs=[
                pl.BlockSpec((blk, width), lambda h, b, i, s: (jnp.where(h == 0, b * 2 + i, 2 * recs - 1), 0)),
                pl.BlockSpec((1, blk, 2), rows),
            ],
        ),
        out_shape=[sds((recs * length // 2, width), BF16), sds((recs, length, 2), F32)],
        compiler_params=LIMIT,
        cost_estimate=cost(recs * length * width * 10, 4 * recs * length * width),
        name="layer_norm",
    )(s, frames, gain[None], bias[None])


def place(s, pieces, out):
    z, c = s[S_Z], s[S_C]
    n = pieces[0].shape[1]
    for r in range(4):
        for k in range(2):
            for h in range(2):
                row = (h * 4 + lax.rem(z + r, 4)) * 2 + (c if k == 0 else 1 - c)
                out[pl.ds(pl.multiple_of(row * n, n), n), :] = pieces[2 * r + k][h]


def proj_body(s, normed, *refs, blk, half):
    pieces, (proj, glu, w) = refs[:8], refs[8:]
    i = pl.program_id(0)

    @pl.when(i == 0)
    def _():
        place(s, pieces, w)

    p = jnp.dot(normed[...], w[...], preferred_element_type=F32)
    proj[...] = p
    n = p.shape[1] // 2
    b = i // (half // blk)
    t = s[S_POS] + (i % (half // blk)) * blk + lax.broadcasted_iota(jnp.int32, (blk, 1), 0)
    valid = (t < s[S_LEN + b]).astype(F32)
    glu[...] = (p[:, :n] * jax.nn.sigmoid(p[:, n:]) * valid).astype(BF16)


def project(s, normed, pieces, half):
    rows, width = normed.shape
    _, shard, n2 = pieces[0].shape
    blk = half // 2
    return pl.pallas_call(
        functools.partial(proj_body, blk=blk, half=half),
        grid_spec=pltpu.PrefetchScalarGridSpec(
            num_scalar_prefetch=1,
            grid=(rows // blk,),
            in_specs=[pl.BlockSpec((blk, width), lambda i, s: (i, 0))] + [VMEM] * 8,
            out_specs=[
                pl.BlockSpec((blk, n2), lambda i, s: (i, 0)),
                pl.BlockSpec((blk, n2 // 2), lambda i, s: (i, 0)),
                pl.BlockSpec((16 * shard, n2), lambda i, s: (0, 0)),
            ],
        ),
        out_shape=[sds((rows, n2), F32), sds((rows, n2 // 2), BF16), sds((16 * shard, n2), BF16)],
        compiler_params=LIMIT,
        cost_estimate=cost(2 * rows * width * n2, 2 * rows * width + 5 * rows * n2),
        name="project",
    )(s, normed, *pieces)


def gact_body(s, go, *refs):
    pieces, (out, w) = refs[:8], refs[8:]

    @pl.when((pl.program_id(0) == 0) & (pl.program_id(1) == 0))
    def _():
        place(s, pieces, w)

    out[0] = jnp.dot(go[0], w[...], preferred_element_type=F32)


def grad_act(s, grad_out, pieces):
    recs, length, width = grad_out.shape
    _, shard, n = pieces[0].shape
    blk = length // 4
    return pl.pallas_call(
        gact_body,
        grid_spec=pltpu.PrefetchScalarGridSpec(
            num_scalar_prefetch=1,
            grid=(recs, 2),
            in_specs=[pl.BlockSpec((1, blk, width), lambda b, i, s: (b, s[S_YL] * 2 + i, 0))] + [VMEM] * 8,
            out_specs=[
                pl.BlockSpec((1, blk, n), lambda b, i, s: (b, i, 0)),
                pl.BlockSpec((16 * shard, n), lambda b, i, s: (0, 0)),
            ],
        ),
        out_shape=[sds((recs, length // 2, n), F32), sds((16 * shard, n), BF16)],
        compiler_params=LIMIT,
        cost_estimate=cost(recs * length * width * n, recs * length * (width + 2 * n)),
        name="grad_act",
    )(s, grad_out, *pieces)


def tn(a, b):
    return lax.dot_general(a, b, (((0,), (0,)), ((), ())), preferred_element_type=F32)


def wgrad_body(s, normed, gp, go, act, w, mine, theirs, tu, colsum):
    shard = mine.shape[1]
    n2 = gp.shape[1]

    @pl.when(pl.program_id(0) == 0)
    def _():
        colsum[...] = jnp.sum(gp[...].astype(F32), axis=0, keepdims=True)

    g_in = tn(normed[...], gp[...])
    wide = w[...].astype(F32)
    tu[:, 0:1] = jnp.sum(wide * g_in, axis=1, keepdims=True)
    tu[:, 1:2] = jnp.sum(wide * colsum[...], axis=1, keepdims=True)
    g_out = tn(go[...].reshape(-1, go.shape[2]), act[...])
    first = s[S_C] == 0
    for i in range(2):
        r0 = 2 * i * shard
        for g, cols in ((g_in, slice(0, n2)), (g_out, slice(n2, n2 + g_out.shape[1]))):
            top, low = g[r0 : r0 + shard], g[r0 + shard : r0 + 2 * shard]
            mine[i, :, cols] = jnp.where(first, top, low).astype(BF16)
            theirs[i, :, cols] = jnp.where(first, low, top).astype(BF16)


def weight_grads(s, normed, gp, grad_out, act, w):
    rows, width = normed.shape
    n2, n = gp.shape[1], act.shape[1]
    recs, length, _ = grad_out.shape
    blk = width // 4
    shard = width // 16
    part = pl.BlockSpec((2, shard, n2 + n), lambda k, s: (k, 0, 0))
    return pl.pallas_call(
        wgrad_body,
        grid_spec=pltpu.PrefetchScalarGridSpec(
            num_scalar_prefetch=1,
            grid=(4,),
            in_specs=[
                pl.BlockSpec((rows, blk), lambda k, s: (0, k)),
                pl.BlockSpec((rows, n2), lambda k, s: (0, 0)),
                pl.BlockSpec((recs, length // 2, blk), lambda k, s: (0, s[S_YL], k)),
                pl.BlockSpec((rows, n), lambda k, s: (0, 0)),
                pl.BlockSpec((blk, n2), lambda k, s: (k, 0)),
            ],
            out_specs=[part, part, pl.BlockSpec((blk, 2), lambda k, s: (k, 0))],
            scratch_shapes=[pltpu.VMEM((1, n2), F32)],
        ),
        out_shape=[sds((8, shard, n2 + n), BF16)] * 2 + [sds((width, 2), F32)],
        compiler_params=LIMIT,
        cost_estimate=cost(2 * rows * width * (n2 + n), 4 * rows * width),
        name="weight_grads",
    )(s, normed, gp, grad_out, act, w)


def core_body(s, mine, got, *outs):
    for r, out in enumerate(outs):
        q = lax.rem(s[S_Z] + r, 4)
        for h in range(2):
            out[h] = (mine[h * 4 + q].astype(F32) + got[h * 4 + q].astype(F32)).astype(BF16)


def core_sum(s, mine, got):
    _, shard, n = mine.shape
    return pl.pallas_call(
        core_body,
        in_specs=[SMEM, VMEM, VMEM],
        out_specs=[VMEM] * 4,
        out_shape=[sds((2, shard, n), BF16)] * 4,
        compiler_params=LIMIT,
        cost_estimate=cost(16 * shard * n, 48 * shard * n),
        name="core_sum",
    )(s, mine, got)


def ring_body(s, p0, p1, p2, p3, own, to_yl, to_yh, to_xx):
    n = own.shape[1] // 3

    def total(h):
        return p0[h].astype(F32) + p1[h].astype(F32) + p2[h].astype(F32) + p3[h].astype(F32)

    first = s[S_YL] == 0
    for v, here, there in ((total(s[S_YH]), own, to_yl), (total(1 - s[S_YH]), to_yh, to_xx)):
        for g in range(3):
            low, high = v[:, 2 * g * n : (2 * g + 1) * n], v[:, (2 * g + 1) * n : (2 * g + 2) * n]
            cols = slice(g * n, g * n + n)
            here[:, cols] = jnp.where(first, low, high).astype(here.dtype)
            there[:, cols] = jnp.where(first, high, low).astype(there.dtype)


def ring_sum(s, parts):
    _, shard, n = parts[0].shape
    return pl.pallas_call(
        ring_body,
        in_specs=[SMEM] + [VMEM] * 4,
        out_specs=[VMEM] * 4,
        out_shape=[sds((shard, n // 2), F32)] + [sds((shard, n // 2), BF16)] * 3,
        compiler_params=LIMIT,
        cost_estimate=cost(8 * shard * n, 24 * shard * n),
        name="ring_sum",
    )(s, *parts)


def fill(pad, mid, lo, hi):
    recs, half = mid.shape[0], mid.shape[1]
    for b in range(recs):
        for j in range(mid.shape[2] // 128):
            lanes = slice(128 * j, 128 * j + 128)
            pad[b, j, 0:EDGE, :] = lo[b, :, lanes].astype(F32)
            pad[b, j, EDGE : EDGE + half, :] = mid[b, :, lanes].astype(F32)
            pad[b, j, EDGE + half :, :] = hi[b, :, lanes].astype(F32)


def tile_mask(start, rows, length):
    t = start + lax.broadcasted_iota(jnp.int32, (rows, 128), 0)
    return ((t >= 0) & (t < length)).astype(F32)


def local_count(s, half):
    n = jnp.int32(0)
    for b in range(2):
        n = n + jnp.clip(s[S_LEN + b] - s[S_POS], 0, half)
    return jnp.maximum(n, 1).astype(F32)


def fold(v):
    return jnp.sum(v.reshape(-1, 8, v.shape[1]), axis=0)


TILE = 96


def conv_body(s, glu, lo, hi, w, depth, stat, pad):
    recs, half, chans = glu.shape
    fill(pad, glu, lo, hi)
    count = local_count(s, half)
    for j in range(chans // 128):
        lanes = slice(128 * j, 128 * j + 128)
        total = jnp.zeros((8, 128), F32)
        for b in range(recs):

            def step(i, total, b=b):
                r0 = pl.multiple_of(i * TILE, 8)
                acc = jnp.zeros((TILE, 128), F32)
                for o in range(TAPS):
                    acc = acc + pad[b, j, pl.ds(r0 + o + 1, TILE), :] * w[o : o + 1, lanes]
                depth[b, pl.ds(r0, TILE), lanes] = acc
                return total + fold(acc * tile_mask(s[S_POS] + r0, TILE, s[S_LEN + b]))

            total = lax.fori_loop(0, half // TILE, step, total)
        mean = jnp.sum(total, axis=0, keepdims=True) / count
        spread = jnp.zeros((8, 128), F32)
        for b in range(recs):

            def step2(i, spread, b=b):
                r0 = pl.multiple_of(i * TILE, 8)
                d = (depth[b, pl.ds(r0, TILE), lanes] - mean) * tile_mask(s[S_POS] + r0, TILE, s[S_LEN + b])
                return spread + fold(d * d)

            spread = lax.fori_loop(0, half // TILE, step2, spread)
        stat[0:1, lanes] = mean
        stat[0:1, slice(chans + 128 * j, chans + 128 * j + 128)] = jnp.sum(spread, axis=0, keepdims=True)


def conv(s, glu, lo, hi, w):
    recs, half, chans = glu.shape
    return pl.pallas_call(
        conv_body,
        in_specs=[SMEM, VMEM, VMEM, VMEM, VMEM],
        out_specs=[VMEM, VMEM],
        out_shape=[sds((recs, half, chans), F32), sds((1, 2 * chans), F32)],
        scratch_shapes=[pltpu.VMEM((recs, chans // 128, half + 2 * EDGE, 128), F32)],
        compiler_params=LIMIT,
        cost_estimate=cost(recs * half * chans * 62 * 50, recs * half * chans * 6),
        name="conv",
    )(s, glu, lo, hi, w)


def bn_stats(s, got, half, chans):
    dev = got.shape[0]
    start = half * lax.broadcasted_iota(jnp.int32, (dev, 1), 0)
    n = jnp.zeros((dev, 1), jnp.int32)
    for b in range(2):
        n = n + jnp.clip(s[S_LEN + b] - start, 0, half)
    n = n.astype(F32)
    count = (s[S_LEN].astype(F32)) + (s[S_LEN + 1].astype(F32))
    means, spread = got[:, :chans], got[:, chans:]
    mean = jnp.sum(n * means, axis=0, keepdims=True) / count
    var = jnp.sum(spread + n * (means - mean) ** 2, axis=0, keepdims=True) / count
    return mean, lax.rsqrt(var + EPS), count


def act_body(s, depth, gact, got, prm, act, gbo, sums, bn, *, half):
    b = pl.program_id(0)
    i = pl.program_id(1)
    rows, chans = depth.shape[1], depth.shape[2]

    @pl.when((b == 0) & (i == 0))
    def _():
        mean, rstd, _ = bn_stats(s, got, half, chans)
        bn[0:1, :] = mean
        bn[1:2, :] = rstd
        sums[...] = jnp.zeros_like(sums)

    for j in range(chans // 128):
        lanes = slice(128 * j, 128 * j + 128)
        high = slice(chans + 128 * j, chans + 128 * j + 128)
        mean, rstd = bn[0:1, lanes], bn[1:2, lanes]
        gain, bias = prm[31:32, lanes], prm[32:33, lanes]
        one = jnp.zeros((8, 128), F32)
        two = jnp.zeros((8, 128), F32)
        for k in range(rows // TILE):
            r = slice(k * TILE, k * TILE + TILE)
            hat = (depth[0, r, lanes] - mean) * rstd
            out = hat * gain + bias
            g = jax.nn.sigmoid(out)
            m = tile_mask(s[S_POS] + i * rows + k * TILE, TILE, s[S_LEN + b])
            act[0, r, lanes] = (out * g * m).astype(BF16)
            gb = gact[0, r, lanes] * m * (g * (1.0 + out * (1.0 - g)))
            gbo[0, r, lanes] = gb
            one = one + fold(gb * hat)
            two = two + fold(gb)
        sums[0:1, lanes] += jnp.sum(one, axis=0, keepdims=True)
        sums[0:1, high] += jnp.sum(two, axis=0, keepdims=True)


def activate(s, depth, gact, got, prm):
    recs, half, chans = depth.shape
    blk = half // 2
    block = pl.BlockSpec((1, blk, chans), lambda b, i, s: (b, i, 0))
    whole = lambda a: pl.BlockSpec(a.shape, lambda b, i, s: (0, 0))
    return pl.pallas_call(
        functools.partial(act_body, half=half),
        grid_spec=pltpu.PrefetchScalarGridSpec(
            num_scalar_prefetch=1,
            grid=(recs, 2),
            in_specs=[block, block, whole(got), whole(prm)],
            out_specs=[block, block, pl.BlockSpec((1, 2 * chans), lambda b, i, s: (0, 0)), pl.BlockSpec((8, chans), lambda b, i, s: (0, 0))],
        ),
        out_shape=[sds(depth.shape, BF16), sds(depth.shape, F32), sds((1, 2 * chans), F32), sds((8, chans), F32)],
        compiler_params=LIMIT,
        cost_estimate=cost(recs * half * chans * 200, recs * half * chans * 14),
        name="activate",
    )(s, depth, gact, got, prm)


def back_body(s, depth, gbo, lo, hi, sums, bn, prm, proj, gd_out, gp, pad):
    recs, half, chans = depth.shape
    total = jnp.sum(sums[...], axis=0, keepdims=True)
    count = (s[S_LEN].astype(F32)) + (s[S_LEN + 1].astype(F32))
    pos = s[S_POS]
    for j in range(chans // 128):
        lanes = slice(128 * j, 128 * j + 128)
        high = slice(chans + 128 * j, chans + 128 * j + 128)
        gsum, bsum = total[:, lanes], total[:, high]
        mean, rstd = bn[0:1, lanes], bn[1:2, lanes]
        scale = prm[31:32, lanes] * rstd

        def grad(dep, gb, start, length):
            m = tile_mask(start, dep.shape[0], length)
            hat = (dep - mean) * rstd
            return m * scale * (gb - (bsum + hat * gsum) / count)

        for b in range(recs):
            length = s[S_LEN + b]
            pad[b, j, 0:EDGE, :] = grad(lo[0, b, :, lanes], lo[1, b, :, lanes], pos - EDGE, length)
            pad[b, j, EDGE + half :, :] = grad(hi[0, b, :, lanes], hi[1, b, :, lanes], pos + half, length)

            def step(i, _, b=b, length=length):
                r0 = pl.multiple_of(i * TILE, 8)
                v = grad(depth[b, pl.ds(r0, TILE), lanes], gbo[b, pl.ds(r0, TILE), lanes], pos + r0, length)
                pad[b, j, pl.ds(pl.multiple_of(r0 + EDGE, 8), TILE), :] = v
                gd_out[b, pl.ds(r0, TILE), lanes] = v
                return 0

            lax.fori_loop(0, half // TILE, step, 0)

            def step2(i, _, b=b, length=length):
                r0 = pl.multiple_of(i * TILE, 16)
                acc = jnp.zeros((TILE, 128), F32)
                for o in range(TAPS):
                    acc = acc + pad[b, j, pl.ds(r0 + TAPS - o, TILE), :] * prm[o : o + 1, lanes]
                acc = acc * tile_mask(pos + r0, TILE, length)
                val = proj[b, pl.ds(r0, TILE), lanes]
                g = jax.nn.sigmoid(proj[b, pl.ds(r0, TILE), high])
                gp[b, pl.ds(r0, TILE), lanes] = (acc * g).astype(BF16)
                gp[b, pl.ds(r0, TILE), high] = (acc * val * g * (1.0 - g)).astype(BF16)
                return 0

            lax.fori_loop(0, half // TILE, step2, 0)


def backward(s, depth, gbo, lo, hi, sums, bn, prm, proj):
    recs, half, chans = depth.shape
    return pl.pallas_call(
        back_body,
        in_specs=[SMEM] + [VMEM] * 8,
        out_specs=[VMEM, VMEM],
        out_shape=[sds(depth.shape, F32), sds((recs, half, 2 * chans), BF16)],
        scratch_shapes=[pltpu.VMEM((recs, chans // 128, half + 2 * EDGE, 128), F32)],
        compiler_params=LIMIT,
        cost_estimate=LONG,
        name="backward",
    )(s, depth, gbo, lo, hi, sums, bn, prm, proj)


def taps_body(gd, glu, lo, hi, gwd, pad):
    recs, half, chans = glu.shape
    fill(pad, glu, lo, hi)
    gwd[...] = jnp.zeros_like(gwd)
    for j in range(chans // 128):
        lanes = slice(128 * j, 128 * j + 128)
        accs = tuple(jnp.zeros((8, 128), F32) for _ in range(TAPS))
        for b in range(recs):

            def step(i, accs, b=b):
                r0 = pl.multiple_of(i * 16, 16)
                new = list(accs)
                for k in range(2):
                    g = gd[b, pl.ds(r0 + 8 * k, 8), lanes]
                    for o in range(TAPS):
                        new[o] = new[o] + g * pad[b, j, pl.ds(r0 + 8 * k + o + 1, 8), :]
                return tuple(new)

            accs = lax.fori_loop(0, half // 16, step, accs)
        for o in range(TAPS):
            gwd[o : o + 1, lanes] = jnp.sum(accs[o], axis=0, keepdims=True)


def taps_grad(gd, glu, lo, hi):
    recs, half, chans = glu.shape
    return pl.pallas_call(
        taps_body,
        in_specs=[VMEM] * 4,
        out_specs=VMEM,
        out_shape=sds((32, chans), F32),
        scratch_shapes=[pltpu.VMEM((recs, chans // 128, half + 2 * EDGE, 128), F32)],
        compiler_params=LIMIT,
        cost_estimate=cost(recs * half * chans * 62 * 50, recs * half * chans * 20),
        name="taps_grad",
    )(gd, glu, lo, hi)


def rows_body(gp, proj, gw, rs):
    recs, half, _ = gp.shape
    gsum = gw[0:1, :] + gw[1:2, :]
    shift = gw[2:3, :] + gw[3:4, :]
    for b in range(recs):

        def step2(i, _, b=b):
            r0 = pl.multiple_of(i * 48, 16)
            g = gp[b, pl.ds(r0, 48), :].astype(F32)
            rs[b, pl.ds(r0, 48), 0:1] = jnp.sum(g * gsum, axis=1, keepdims=True)
            rs[b, pl.ds(r0, 48), 1:2] = jnp.sum(g * (proj[b, pl.ds(r0, 48), :] - shift), axis=1, keepdims=True)
            return 0

        lax.fori_loop(0, half // 48, step2, 0)


def row_sums(gp, proj, gw):
    recs, half, n2 = gp.shape
    return pl.pallas_call(
        rows_body,
        in_specs=[VMEM] * 3,
        out_specs=VMEM,
        out_shape=sds((recs, half, 2), F32),
        compiler_params=LIMIT,
        cost_estimate=cost(recs * half * n2 * 8, recs * half * n2 * 6),
        name="row_sums",
    )(gp, proj, gw)


def through_body(gain, bias, w, out):
    def split(v):
        top = v.astype(BF16).astype(F32)
        return top, v - top

    g1, g2 = split(gain[...])
    b1, b2 = split(bias[...])
    row = lax.broadcasted_iota(jnp.int32, (16, gain.shape[1]), 0)
    v = jnp.where(row == 0, g1, jnp.where(row == 1, g2, jnp.where(row == 2, b1, jnp.where(row == 3, b2, 0.0))))
    out[...] = jnp.dot(v.astype(BF16), w[...], preferred_element_type=F32)


def through(gain, bias, w):
    return pl.pallas_call(
        through_body,
        in_specs=[VMEM] * 3,
        out_specs=VMEM,
        out_shape=sds((16, w.shape[1]), F32),
        compiler_params=LIMIT,
        cost_estimate=cost(32 * w.shape[0] * w.shape[1], 2 * w.shape[0] * w.shape[1]),
        name="through",
    )(gain[None], bias[None], w)


def turn_body(w, out, cat):
    n = w.shape[1]
    for d in range(4):
        cat[0:n, :] = w[d]
        cat[n:, :] = w[d + 4]
        out[d] = cat[...].T


def turned(w):
    n, depth = w.shape[0] // 8, w.shape[1]
    return pl.pallas_call(
        turn_body,
        in_specs=[VMEM],
        out_specs=VMEM,
        out_shape=sds((4, depth, 2 * n), BF16),
        scratch_shapes=[pltpu.VMEM((2 * n, depth), BF16)],
        compiler_params=LIMIT,
        cost_estimate=cost(32 * n * depth, 32 * n * depth),
        name="turned",
    )(w.reshape(8, n, depth))


def blocks_body(s, lhs, w, *refs, jobs, adds):
    plus, outs = refs[:adds], refs[adds:]
    half = lhs.shape[1]
    for rec, r, to, at in jobs:
        v = jnp.dot(lhs[rec], w[lax.rem(s[S_X] + r, 4)], preferred_element_type=F32)
        if adds:
            v = v + plus[to][0:half, :].astype(F32)
        outs[to][at * half : (at + 1) * half, :] = v.astype(BF16)


def blocks(s, lhs, w4, jobs, plus=()):
    recs, half, depth = lhs.shape
    n = w4.shape[2]
    each = len(jobs) // 2
    return pl.pallas_call(
        functools.partial(blocks_body, jobs=jobs, adds=len(plus)),
        in_specs=[SMEM] + [VMEM] * (2 + len(plus)),
        out_specs=[VMEM] * 2,
        out_shape=[sds((each * half, n), BF16)] * 2,
        compiler_params=LIMIT,
        cost_estimate=cost(2 * half * depth * n * len(jobs), 4 * half * depth + 8 * n * depth),
        name="blocks",
    )(s, lhs, w4, *plus)


def finish_body(s, lhs, w, up, down, last_a, last_b, keep, give):
    half = lhs.shape[1]
    n = w.shape[2] // 2
    first = s[S_YL] == 0
    for rec, (one, two) in enumerate(((last_a, down), (last_b, up))):
        v = jnp.dot(lhs[rec], w[s[S_X]], preferred_element_type=F32)
        v = v + one[...].astype(F32) + two[half:, :].astype(F32)
        low, high = v[:, :n], v[:, n:]
        keep[:, rec * n : (rec + 1) * n] = jnp.where(first, low, high)
        give[:, rec * n : (rec + 1) * n] = jnp.where(first, high, low).astype(BF16)


def finish(s, lhs, w4, parts):
    recs, half, depth = lhs.shape
    n = w4.shape[2] // 2
    return pl.pallas_call(
        finish_body,
        in_specs=[SMEM] + [VMEM] * 6,
        out_specs=[VMEM] * 2,
        out_shape=[sds((half, recs * n), F32), sds((half, recs * n), BF16)],
        compiler_params=LIMIT,
        cost_estimate=LONG,
        name="finish",
    )(s, lhs, w4, *parts)


def hop(v, axis, by):
    n = lax.axis_size(axis)
    return lax.ppermute(v, axis, [(i, (i + by) % n) for i in range(n)])


def sum_start(s, lhs, w8):
    sent = blocks(s, lhs, w8, ((0, 2, 0, 0), (1, 2, 1, 0), (1, 1, 0, 1), (0, 3, 1, 1)))
    return (hop(sent[0], "x", 1), hop(sent[1], "x", -1)), sent[0]


def sum_middle(s, lhs, w8, got):
    sent = blocks(s, lhs, w8, ((0, 1, 0, 0), (1, 3, 1, 0)), got)
    return (hop(sent[0], "x", 1), hop(sent[1], "x", -1)), sent[0]


def sum_end(s, lhs, w8, got, last):
    keep, give = finish(s, lhs, w8, (*got, *last))
    return keep, hop(give, "yl", 1)


def after(values, *first):
    return lax.optimization_barrier((*values, *first))[: len(values)]


def pick(block, odd):
    n = block.shape[1] // 2
    return jnp.where(odd == 1, block[:, n:].astype(F32), block[:, :n].astype(F32))


def halves(s, keep, got):
    n = keep.shape[1] // 2
    early = pl.program_id(0) == 0
    mine = jnp.where(early, keep[:, :n], keep[:, n:])
    theirs = jnp.where(early, got[:, :n].astype(F32), got[:, n:].astype(F32))
    first = s[S_YL] == 0
    return jnp.where(first, mine, theirs), jnp.where(first, theirs, mine)


def out_body(s, keep, got, fr, out):
    half = keep.shape[0]
    for h, v in enumerate(halves(s, keep, got)):
        rows = slice(h * half, h * half + half)
        out[0, :, rows] = (pick(fr[0, rows, :], s[S_ODD]) + v).T.astype(BF16)


def frames_body(s, keep, got, fr, go, stat, rs, gain, out):
    half = keep.shape[0]
    width = 8 * out.shape[1]
    for h, v in enumerate(halves(s, keep, got)):
        rows = slice(h * half, h * half + half)
        g = v * gain[...]
        mean, rstd = stat[0, rows, 0:1], stat[0, rows, 1:2]
        first, second = rs[h, 0, :, 0:1], rs[h, 0, :, 1:2]
        hat = (pick(fr[0, rows, :], s[S_ODD]) - mean) * rstd
        v = rstd * (g - first / width - hat * (second / width)) + pick(go[0, rows, :], s[S_ODD])
        out[0, :, rows] = v.T.astype(BF16)


def last_call(body, s, keep, got, wide, extra, extra_specs, name):
    recs, length, _ = wide[0].shape
    half, n = length // 2, keep.shape[1] // 2
    cols = pl.BlockSpec((1, 2 * half, 2 * n), lambda b, s: (b, 0, s[S_PAIR]))
    return pl.pallas_call(
        body,
        grid_spec=pltpu.PrefetchScalarGridSpec(
            num_scalar_prefetch=1,
            grid=(recs,),
            in_specs=[
                pl.BlockSpec((half, recs * n), lambda b, s: (0, 0)),
                pl.BlockSpec((half, recs * n), lambda b, s: (0, 0)),
            ]
            + [cols] * len(wide)
            + extra_specs,
            out_specs=pl.BlockSpec((1, n, 2 * half), lambda b, s: (b, 0, 0)),
        ),
        out_shape=sds((recs, n, 2 * half), BF16),
        compiler_params=LIMIT,
        cost_estimate=cost(recs * half * n * 20, recs * half * n * 20),
        name=name,
    )(s, keep, got, *wide, *extra).transpose(0, 2, 1)


def spread(v, axes):
    n = lax.axis_size(axes)
    return lax.all_to_all(jnp.broadcast_to(v[None], (n, *v.shape)), axes, 0, 0, tiled=True)


def on_device(frames, ln_gain, ln_bias, w_in, w_depth, bn_gain, bn_bias, w_out, lengths, grad_out):
    recs, length, width = frames.shape
    shard, _, own = w_in.shape
    half = length // 2
    chans = 2 * own
    yh, z, c, yl, x = (lax.axis_index(a) for a in ("yh", "z", "c", "yl", "x"))
    ctx = (yh * 4 + z) * 2 + c
    chan = yl * 4 + x
    time = ctx * 2 + yl
    s = jnp.stack([yl, x, chan // 2, chan % 2, time * half, lengths[0], lengths[1], z, c, yh]).astype(jnp.int32)

    w3 = jnp.concatenate([w_in.reshape(shard, 2 * own), w_out], axis=1)
    w_yl = hop(w3, "yl", 1)
    w_yh = hop(w3, "yh", 1)
    w_xx = lax.ppermute(w3, ("yh", "yl"), [(i, 3 - i) for i in range(4)])

    def paired(a, b, g0, g1):
        lo, hi = jnp.where(yl == 0, a, b), jnp.where(yl == 0, b, a)
        cols = []
        for g in range(g0, g1):
            cols += [lo[:, g * own : (g + 1) * own], hi[:, g * own : (g + 1) * own]]
        return jnp.concatenate(cols, axis=1)

    def rows_two(g0, g1):
        same, other = paired(w3, w_yl, g0, g1), paired(w_yh, w_xx, g0, g1)
        return jnp.where(yh == 0, jnp.stack([same, other]), jnp.stack([other, same]))

    def gathered(v, first):
        pieces = []
        for r in range(4):
            p = v if r == 0 else hop(v, "z", -r)
            if first is not None:
                (p,) = after([p], first)
            pieces += [p, hop(p, "c", 1)]
        return pieces

    in_two = rows_two(0, 2)
    normed, stat = layer_norm(s, *after([frames, ln_gain, ln_bias], in_two))
    in_pieces = gathered(in_two, normed)
    out_pieces = gathered(*after([rows_two(2, 3)], *in_pieces), None)
    prm1 = jnp.concatenate([w_depth, bn_gain[None], bn_bias[None], jnp.zeros((7, own), F32)], axis=0)
    prm2 = hop(prm1, "yl", 1)
    prm = jnp.where(yl == 0, jnp.concatenate([prm1, prm2], axis=1), jnp.concatenate([prm2, prm1], axis=1))

    proj, glu, w_in_all = project(s, normed, in_pieces, half)
    glu = glu.reshape(recs, half, chans)
    proj = proj.reshape(recs, half, 2 * chans)
    devices = lax.axis_size(TIME)
    up = [(i, i + 1) for i in range(devices - 1)]
    down = [(i + 1, i) for i in range(devices - 1)]
    g_lo = lax.ppermute(glu[:, half - EDGE :], TIME, up)
    g_hi = lax.ppermute(glu[:, :EDGE], TIME, down)
    gact, w_out_all = grad_act(s, grad_out, out_pieces)
    (glu_c,) = after([glu], gact)
    depth, bn_own = conv(s, glu_c, g_lo, g_hi, prm)
    bn_all = spread(bn_own, TIME).reshape(devices, 2 * chans)
    w_out_4 = turned(*after([w_out_all], bn_own))
    w_in_4 = turned(*after([w_in_all], bn_own))
    g_w = through(*after([ln_gain, ln_bias, w_in_all], bn_own))
    (gact,) = after([gact], w_out_4, w_in_4, g_w)
    act, gbo, sums_own, bn = activate(s, depth, gact, bn_all, prm)
    sums = spread(sums_own, TIME).reshape(devices, 2 * chans)
    e_lo = lax.ppermute(jnp.stack([depth[:, half - EDGE :], gbo[:, half - EDGE :]]), TIME, up)
    e_hi = lax.ppermute(jnp.stack([depth[:, :EDGE], gbo[:, :EDGE]]), TIME, down)

    out_first, sent = sum_start(s, act, w_out_4)
    depth, gbo = after([depth, gbo], sent)
    gd, gp = backward(s, depth, gbo, e_lo, e_hi, sums, bn, prm, proj)
    gn_first, sent = sum_start(s, gp, w_in_4)
    (act_m,) = after([act], sent)
    out_last, sent = sum_middle(s, act_m, w_out_4, out_first)
    gd, glu = after([gd, glu], sent)
    gwd = taps_grad(gd, glu, g_lo, g_hi)
    (gp_r,) = after([gp], gwd)
    rs = row_sums(gp_r, proj, g_w)
    (gp_m,) = after([gp], rs)
    gn_last, sent = sum_middle(s, gp_m, w_in_4, gn_first)
    (gp_w,) = after([gp], sent)
    mine, theirs, tu = weight_grads(
        s,
        normed,
        gp_w.reshape(recs * half, 2 * chans),
        grad_out,
        act.reshape(recs * half, chans),
        w_in_all,
    )

    tu = tu.T.reshape(2, 2, 4, own).transpose(1, 2, 0, 3)
    mine_x = (jnp.arange(4) == x).astype(F32)[None, :, None, None]
    taps4 = gwd[:TAPS].reshape(TAPS, 2, own).transpose(1, 0, 2)[:, None] * mine_x
    rs_rows = recs * 2 * half // own
    rs8 = jnp.broadcast_to(rs.transpose(2, 0, 1).reshape(1, 1, rs_rows, own), (2, 4, rs_rows, own))
    small = jnp.concatenate([taps4, tu, rs8], axis=2).reshape(8, TAPS + 2 + rs_rows, own)

    (gp_e,) = after([gp], mine)
    gn_keep, gn_got = sum_end(s, gp_e, w_in_4, gn_first, gn_last)
    mine, theirs = after([mine, theirs], gn_keep)
    parts = core_sum(s, mine, hop(theirs, "c", 1))
    (small,) = after([small], gn_keep)
    small = lax.all_to_all(small, CHAN, 0, 0, tiled=True)
    rs_all = jnp.sum(small[:, TAPS + 2 :].reshape(2, 4, 2, recs, half), axis=1).transpose(0, 2, 3, 1)
    small = jnp.sum(small[:, : TAPS + 2], axis=0)
    (act_e,) = after([act], gn_keep)
    out_keep, out_got = sum_end(s, act_e, w_out_4, out_first, out_last)
    block_out = last_call(out_body, s, out_keep, out_got, [frames], [], [], "block_out")
    small = jnp.sum(spread(small, CTX), axis=0)

    own_gain = lax.dynamic_slice_in_dim(ln_gain, chan * own, own, 0)
    own_bias = lax.dynamic_slice_in_dim(ln_bias, chan * own, own, 0)
    grad_frames = last_call(
        frames_body,
        s,
        gn_keep,
        gn_got,
        [frames, grad_out],
        [stat, rs_all, own_gain[None]],
        [
            pl.BlockSpec((1, length, 2), lambda b, s: (b, 0, 0)),
            pl.BlockSpec((2, 1, half, 2), lambda b, s: (0, b, 0, 0)),
            pl.BlockSpec((1, own), lambda b, s: (0, 0)),
        ],
        "grad_frames",
    )

    parts = [parts[0]] + [hop(parts[r], "z", r) for r in range(1, 4)]
    g_fin, to_yl, to_yh, to_xx = ring_sum(s, parts)
    g_fin = g_fin + hop(to_yl, "yl", 1).astype(F32) + hop(to_yh, "yh", 1).astype(F32)
    g_fin = g_fin + lax.ppermute(to_xx, ("yh", "yl"), [(i, 3 - i) for i in range(4)]).astype(F32)
    grad_w_in = g_fin[:, : 2 * own].reshape(shard, 2, own)
    grad_w_out = g_fin[:, 2 * own :]

    grad_w_depth = small[:TAPS]
    t, u = small[TAPS], small[TAPS + 1]
    grad_ln = jnp.stack([(t - own_bias * u) / own_gain, u])
    grad_bn = lax.dynamic_index_in_dim(jnp.sum(sums, axis=0).reshape(2, 2, own), yl, 1, False)
    return (block_out, grad_frames, grad_w_in, grad_w_out, grad_w_depth, grad_bn, grad_ln)


def solution(mesh):
    split = Mesh(mesh.devices.reshape(2, 4, 2, 2, 4), ("yh", "z", "c", "yl", "x"))
    placed = (
        P(None, CTX, None),
        P(),
        P(),
        P(CTX, None, CHAN),
        P(None, CHAN),
        P(CHAN),
        P(CHAN),
        P(CTX, CHAN),
        P(),
        P(None, CTX, None),
    )
    return jax.shard_map(
        on_device,
        mesh=split,
        in_specs=placed,
        out_specs=(
            P(None, CTX, CHAN),
            P(None, CTX, CHAN),
            P(CTX, None, CHAN),
            P(CTX, CHAN),
            P(None, CHAN),
            P(None, CHAN),
            P(None, CHAN),
        ),
        check_vma=False,
    )
```

```python
import functools

import jax
import jax.numpy as jnp
from jax import lax
from jax.experimental import pallas as pl
from jax.experimental.pallas import tpu as pltpu
from jax.sharding import Mesh
from jax.sharding import PartitionSpec as P

F32 = jnp.float32
BF16 = jnp.bfloat16
CTX = ("yh", "z", "c")
CHAN = ("yl", "x")
TIME = ("yh", "z", "c", "yl")
EPS = 1e-05
TAPS = 31
EDGE = 16
LIMIT = pltpu.CompilerParams(vmem_limit_bytes=50 * 1024 * 1024)

S_YL, S_X, S_PAIR, S_ODD, S_POS, S_LEN, S_Z, S_C, S_YH = 0, 1, 2, 3, 4, 5, 7, 8, 9

SMEM = pl.BlockSpec(memory_space=pltpu.SMEM)
VMEM = pl.BlockSpec(memory_space=pltpu.VMEM)
ANY = pl.BlockSpec(memory_space=pl.ANY)


def cost(flops, nbytes):
    return pl.CostEstimate(flops=flops // 50, bytes_accessed=nbytes // 50, transcendentals=0)


LONG = pl.CostEstimate(flops=0, bytes_accessed=100 * 1024 * 1024, transcendentals=0)


def sds(shape, dtype):
    return jax.ShapeDtypeStruct(shape, dtype)


def nt(a, b):
    return lax.dot_general(a, b, (((1,), (1,)), ((), ())), preferred_element_type=F32)


def ln_body(s, fr, gain, bias, normed, stat):
    v = fr[0].astype(F32)
    mean = jnp.mean(v, axis=-1, keepdims=True)
    cen = v - mean
    rstd = lax.rsqrt(jnp.mean(cen * cen, axis=-1, keepdims=True) + EPS)
    stat[0, :, 0:1] = mean
    stat[0, :, 1:2] = rstd

    @pl.when(pl.program_id(0) == 0)
    def _():
        normed[...] = (cen * rstd * gain[...] + bias[...]).astype(BF16)


def layer_norm(s, frames, gain, bias):
    recs, length, width = frames.shape
    blk = length // 4

    def rows(h, b, i, s):
        return (b, jnp.where(h == 0, s[S_YL], 1 - s[S_YL]) * 2 + i, 0)

    return pl.pallas_call(
        ln_body,
        grid_spec=pltpu.PrefetchScalarGridSpec(
            num_scalar_prefetch=1,
            grid=(2, recs, 2),
            in_specs=[
                pl.BlockSpec((1, blk, width), rows),
                pl.BlockSpec((1, width), lambda h, b, i, s: (0, 0)),
                pl.BlockSpec((1, width), lambda h, b, i, s: (0, 0)),
            ],
            out_specs=[
                pl.BlockSpec((blk, width), lambda h, b, i, s: (jnp.where(h == 0, b * 2 + i, 2 * recs - 1), 0)),
                pl.BlockSpec((1, blk, 2), rows),
            ],
        ),
        out_shape=[sds((recs * length // 2, width), BF16), sds((recs, length, 2), F32)],
        compiler_params=LIMIT,
        cost_estimate=cost(recs * length * width * 10, 4 * recs * length * width),
        name="layer_norm",
    )(s, frames, gain[None], bias[None])


def place(s, pieces, out):
    z, c = s[S_Z], s[S_C]
    n = pieces[0].shape[1]
    for r in range(4):
        for k in range(2):
            for h in range(2):
                row = (h * 4 + lax.rem(z + r, 4)) * 2 + (c if k == 0 else 1 - c)
                out[pl.ds(pl.multiple_of(row * n, n), n), :] = pieces[2 * r + k][h]


def proj_body(s, normed, *refs, blk, half):
    pieces, (proj, glu, w) = refs[:8], refs[8:]
    i = pl.program_id(0)

    @pl.when(i == 0)
    def _():
        place(s, pieces, w)

    p = jnp.dot(normed[...], w[...], preferred_element_type=F32)
    proj[...] = p
    n = p.shape[1] // 2
    b = i // (half // blk)
    t = s[S_POS] + (i % (half // blk)) * blk + lax.broadcasted_iota(jnp.int32, (blk, 1), 0)
    valid = (t < s[S_LEN + b]).astype(F32)
    glu[...] = (p[:, :n] * jax.nn.sigmoid(p[:, n:]) * valid).astype(BF16)


def project(s, normed, pieces, half):
    rows, width = normed.shape
    _, shard, n2 = pieces[0].shape
    blk = half
    return pl.pallas_call(
        functools.partial(proj_body, blk=blk, half=half),
        grid_spec=pltpu.PrefetchScalarGridSpec(
            num_scalar_prefetch=1,
            grid=(rows // blk,),
            in_specs=[pl.BlockSpec((blk, width), lambda i, s: (i, 0))] + [VMEM] * 8,
            out_specs=[
                pl.BlockSpec((blk, n2), lambda i, s: (i, 0)),
                pl.BlockSpec((blk, n2 // 2), lambda i, s: (i, 0)),
                pl.BlockSpec((16 * shard, n2), lambda i, s: (0, 0)),
            ],
        ),
        out_shape=[sds((rows, n2), F32), sds((rows, n2 // 2), BF16), sds((16 * shard, n2), BF16)],
        compiler_params=LIMIT,
        cost_estimate=cost(2 * rows * width * n2, 2 * rows * width + 5 * rows * n2),
        name="project",
    )(s, normed, *pieces)


def gact_body(s, go, *refs):
    pieces, (out, w) = refs[:8], refs[8:]

    @pl.when((pl.program_id(0) == 0) & (pl.program_id(1) == 0))
    def _():
        place(s, pieces, w)

    out[0] = jnp.dot(go[0], w[...], preferred_element_type=F32)


def grad_act(s, grad_out, pieces):
    recs, length, width = grad_out.shape
    _, shard, n = pieces[0].shape
    blk = length // 2
    return pl.pallas_call(
        gact_body,
        grid_spec=pltpu.PrefetchScalarGridSpec(
            num_scalar_prefetch=1,
            grid=(recs, 1),
            in_specs=[pl.BlockSpec((1, blk, width), lambda b, i, s: (b, s[S_YL] + i, 0))] + [VMEM] * 8,
            out_specs=[
                pl.BlockSpec((1, blk, n), lambda b, i, s: (b, i, 0)),
                pl.BlockSpec((16 * shard, n), lambda b, i, s: (0, 0)),
            ],
        ),
        out_shape=[sds((recs, length // 2, n), F32), sds((16 * shard, n), BF16)],
        compiler_params=LIMIT,
        cost_estimate=cost(recs * length * width * n, recs * length * (width + 2 * n)),
        name="grad_act",
    )(s, grad_out, *pieces)


def tn(a, b):
    return lax.dot_general(a, b, (((0,), (0,)), ((), ())), preferred_element_type=F32)


def wgrad_body(s, normed, gp, go, act, w, mine, theirs, tu, colsum):
    shard = mine.shape[1]
    n2 = gp.shape[1]

    @pl.when(pl.program_id(0) == 0)
    def _():
        colsum[...] = jnp.sum(gp[...].astype(F32), axis=0, keepdims=True)

    g_in = tn(normed[...], gp[...])
    wide = w[...].astype(F32)
    tu[:, 0:1] = jnp.sum(wide * g_in, axis=1, keepdims=True)
    tu[:, 1:2] = jnp.sum(wide * colsum[...], axis=1, keepdims=True)
    g_out = tn(go[...].reshape(-1, go.shape[2]), act[...])
    first = s[S_C] == 0
    for i in range(2):
        r0 = 2 * i * shard
        for g, cols in ((g_in, slice(0, n2)), (g_out, slice(n2, n2 + g_out.shape[1]))):
            top, low = g[r0 : r0 + shard], g[r0 + shard : r0 + 2 * shard]
            mine[i, :, cols] = jnp.where(first, top, low).astype(BF16)
            theirs[i, :, cols] = jnp.where(first, low, top).astype(BF16)


def weight_grads(s, normed, gp, grad_out, act, w):
    rows, width = normed.shape
    n2, n = gp.shape[1], act.shape[1]
    recs, length, _ = grad_out.shape
    blk = width // 4
    shard = width // 16
    part = pl.BlockSpec((2, shard, n2 + n), lambda k, s: (k, 0, 0))
    return pl.pallas_call(
        wgrad_body,
        grid_spec=pltpu.PrefetchScalarGridSpec(
            num_scalar_prefetch=1,
            grid=(4,),
            in_specs=[
                pl.BlockSpec((rows, blk), lambda k, s: (0, k)),
                pl.BlockSpec((rows, n2), lambda k, s: (0, 0)),
                pl.BlockSpec((recs, length // 2, blk), lambda k, s: (0, s[S_YL], k)),
                pl.BlockSpec((rows, n), lambda k, s: (0, 0)),
                pl.BlockSpec((blk, n2), lambda k, s: (k, 0)),
            ],
            out_specs=[part, part, pl.BlockSpec((blk, 2), lambda k, s: (k, 0))],
            scratch_shapes=[pltpu.VMEM((1, n2), F32)],
        ),
        out_shape=[sds((8, shard, n2 + n), BF16)] * 2 + [sds((width, 2), F32)],
        compiler_params=LIMIT,
        cost_estimate=LONG,
        name="weight_grads",
    )(s, normed, gp, grad_out, act, w)


def core_body(s, mine, got, *outs):
    for r, out in enumerate(outs):
        q = lax.rem(s[S_Z] + r, 4)
        for h in range(2):
            out[h] = (mine[h * 4 + q].astype(F32) + got[h * 4 + q].astype(F32)).astype(BF16)


def core_sum(s, mine, got):
    _, shard, n = mine.shape
    return pl.pallas_call(
        core_body,
        in_specs=[SMEM, VMEM, VMEM],
        out_specs=[VMEM] * 4,
        out_shape=[sds((2, shard, n), BF16)] * 4,
        compiler_params=LIMIT,
        cost_estimate=cost(16 * shard * n, 48 * shard * n),
        name="core_sum",
    )(s, mine, got)


def ring_body(s, p0, p1, p2, p3, own, to_yl, to_yh, to_xx):
    n = own.shape[1] // 3

    def total(h):
        return p0[h].astype(F32) + p1[h].astype(F32) + p2[h].astype(F32) + p3[h].astype(F32)

    first = s[S_YL] == 0
    for v, here, there in ((total(s[S_YH]), own, to_yl), (total(1 - s[S_YH]), to_yh, to_xx)):
        for g in range(3):
            low, high = v[:, 2 * g * n : (2 * g + 1) * n], v[:, (2 * g + 1) * n : (2 * g + 2) * n]
            cols = slice(g * n, g * n + n)
            here[:, cols] = jnp.where(first, low, high).astype(here.dtype)
            there[:, cols] = jnp.where(first, high, low).astype(there.dtype)


def ring_sum(s, parts):
    _, shard, n = parts[0].shape
    return pl.pallas_call(
        ring_body,
        in_specs=[SMEM] + [VMEM] * 4,
        out_specs=[VMEM] * 4,
        out_shape=[sds((shard, n // 2), F32)] + [sds((shard, n // 2), BF16)] * 3,
        compiler_params=LIMIT,
        cost_estimate=cost(8 * shard * n, 24 * shard * n),
        name="ring_sum",
    )(s, *parts)


def fill(pad, mid, lo, hi):
    recs, half = mid.shape[0], mid.shape[1]
    for b in range(recs):
        for j in range(mid.shape[2] // 128):
            lanes = slice(128 * j, 128 * j + 128)
            pad[b, j, 0:EDGE, :] = lo[b, :, lanes].astype(F32)
            pad[b, j, EDGE : EDGE + half, :] = mid[b, :, lanes].astype(F32)
            pad[b, j, EDGE + half :, :] = hi[b, :, lanes].astype(F32)


def tile_mask(start, rows, length):
    t = start + lax.broadcasted_iota(jnp.int32, (rows, 128), 0)
    return ((t >= 0) & (t < length)).astype(F32)


def local_count(s, half):
    n = jnp.int32(0)
    for b in range(2):
        n = n + jnp.clip(s[S_LEN + b] - s[S_POS], 0, half)
    return jnp.maximum(n, 1).astype(F32)


def fold(v):
    return jnp.sum(v.reshape(-1, 8, v.shape[1]), axis=0)


TILE = 96


def conv_body(s, glu, lo, hi, w, depth, stat, pad):
    recs, half, chans = glu.shape
    fill(pad, glu, lo, hi)
    count = local_count(s, half)
    for j in range(chans // 128):
        lanes = slice(128 * j, 128 * j + 128)
        total = jnp.zeros((8, 128), F32)
        for b in range(recs):

            def step(i, total, b=b):
                r0 = pl.multiple_of(i * TILE, 8)
                acc = jnp.zeros((TILE, 128), F32)
                for o in range(TAPS):
                    acc = acc + pad[b, j, pl.ds(r0 + o + 1, TILE), :] * w[o : o + 1, lanes]
                depth[b, pl.ds(r0, TILE), lanes] = acc
                return total + fold(acc * tile_mask(s[S_POS] + r0, TILE, s[S_LEN + b]))

            total = lax.fori_loop(0, half // TILE, step, total)
        mean = jnp.sum(total, axis=0, keepdims=True) / count
        spread = jnp.zeros((8, 128), F32)
        for b in range(recs):

            def step2(i, spread, b=b):
                r0 = pl.multiple_of(i * TILE, 8)
                d = (depth[b, pl.ds(r0, TILE), lanes] - mean) * tile_mask(s[S_POS] + r0, TILE, s[S_LEN + b])
                return spread + fold(d * d)

            spread = lax.fori_loop(0, half // TILE, step2, spread)
        stat[0:1, lanes] = mean
        stat[0:1, slice(chans + 128 * j, chans + 128 * j + 128)] = jnp.sum(spread, axis=0, keepdims=True)


def conv(s, glu, lo, hi, w):
    recs, half, chans = glu.shape
    return pl.pallas_call(
        conv_body,
        in_specs=[SMEM, VMEM, VMEM, VMEM, VMEM],
        out_specs=[VMEM, VMEM],
        out_shape=[sds((recs, half, chans), F32), sds((1, 2 * chans), F32)],
        scratch_shapes=[pltpu.VMEM((recs, chans // 128, half + 2 * EDGE, 128), F32)],
        compiler_params=LIMIT,
        cost_estimate=cost(recs * half * chans * 62 * 50, recs * half * chans * 6),
        name="conv",
    )(s, glu, lo, hi, w)


def bn_stats(s, got, half, chans):
    dev = got.shape[0]
    start = half * lax.broadcasted_iota(jnp.int32, (dev, 1), 0)
    n = jnp.zeros((dev, 1), jnp.int32)
    for b in range(2):
        n = n + jnp.clip(s[S_LEN + b] - start, 0, half)
    n = n.astype(F32)
    count = (s[S_LEN].astype(F32)) + (s[S_LEN + 1].astype(F32))
    means, spread = got[:, :chans], got[:, chans:]
    mean = jnp.sum(n * means, axis=0, keepdims=True) / count
    var = jnp.sum(spread + n * (means - mean) ** 2, axis=0, keepdims=True) / count
    return mean, lax.rsqrt(var + EPS), count


def act_body(s, depth, gact, got, prm, act, gbo, sums, bn, *, half):
    b = pl.program_id(0)
    i = pl.program_id(1)
    rows, chans = depth.shape[1], depth.shape[2]

    @pl.when((b == 0) & (i == 0))
    def _():
        mean, rstd, _ = bn_stats(s, got, half, chans)
        bn[0:1, :] = mean
        bn[1:2, :] = rstd
        sums[...] = jnp.zeros_like(sums)

    for j in range(chans // 128):
        lanes = slice(128 * j, 128 * j + 128)
        high = slice(chans + 128 * j, chans + 128 * j + 128)
        mean, rstd = bn[0:1, lanes], bn[1:2, lanes]
        gain, bias = prm[31:32, lanes], prm[32:33, lanes]
        one = jnp.zeros((8, 128), F32)
        two = jnp.zeros((8, 128), F32)
        for k in range(rows // TILE):
            r = slice(k * TILE, k * TILE + TILE)
            hat = (depth[0, r, lanes] - mean) * rstd
            out = hat * gain + bias
            g = jax.nn.sigmoid(out)
            m = tile_mask(s[S_POS] + i * rows + k * TILE, TILE, s[S_LEN + b])
            act[0, r, lanes] = (out * g * m).astype(BF16)
            gb = gact[0, r, lanes] * m * (g * (1.0 + out * (1.0 - g)))
            gbo[0, r, lanes] = gb
            one = one + fold(gb * hat)
            two = two + fold(gb)
        sums[0:1, lanes] += jnp.sum(one, axis=0, keepdims=True)
        sums[0:1, high] += jnp.sum(two, axis=0, keepdims=True)


def activate(s, depth, gact, got, prm):
    recs, half, chans = depth.shape
    blk = half // 2
    block = pl.BlockSpec((1, blk, chans), lambda b, i, s: (b, i, 0))
    whole = lambda a: pl.BlockSpec(a.shape, lambda b, i, s: (0, 0))
    return pl.pallas_call(
        functools.partial(act_body, half=half),
        grid_spec=pltpu.PrefetchScalarGridSpec(
            num_scalar_prefetch=1,
            grid=(recs, 2),
            in_specs=[block, block, whole(got), whole(prm)],
            out_specs=[block, block, pl.BlockSpec((1, 2 * chans), lambda b, i, s: (0, 0)), pl.BlockSpec((8, chans), lambda b, i, s: (0, 0))],
        ),
        out_shape=[sds(depth.shape, BF16), sds(depth.shape, F32), sds((1, 2 * chans), F32), sds((8, chans), F32)],
        compiler_params=LIMIT,
        cost_estimate=cost(recs * half * chans * 200, recs * half * chans * 14),
        name="activate",
    )(s, depth, gact, got, prm)


def back_body(s, depth, gbo, lo, hi, sums, bn, prm, proj, gd_out, gp, pad):
    recs, half, chans = depth.shape
    total = jnp.sum(sums[...], axis=0, keepdims=True)
    count = (s[S_LEN].astype(F32)) + (s[S_LEN + 1].astype(F32))
    pos = s[S_POS]
    for j in range(chans // 128):
        lanes = slice(128 * j, 128 * j + 128)
        high = slice(chans + 128 * j, chans + 128 * j + 128)
        gsum, bsum = total[:, lanes], total[:, high]
        mean, rstd = bn[0:1, lanes], bn[1:2, lanes]
        scale = prm[31:32, lanes] * rstd

        def grad(dep, gb, start, length):
            m = tile_mask(start, dep.shape[0], length)
            hat = (dep - mean) * rstd
            return m * scale * (gb - (bsum + hat * gsum) / count)

        for b in range(recs):
            length = s[S_LEN + b]
            pad[b, j, 0:EDGE, :] = grad(lo[0, b, :, lanes], lo[1, b, :, lanes], pos - EDGE, length)
            pad[b, j, EDGE + half :, :] = grad(hi[0, b, :, lanes], hi[1, b, :, lanes], pos + half, length)

            def step(i, _, b=b, length=length):
                r0 = pl.multiple_of(i * TILE, 8)
                v = grad(depth[b, pl.ds(r0, TILE), lanes], gbo[b, pl.ds(r0, TILE), lanes], pos + r0, length)
                pad[b, j, pl.ds(pl.multiple_of(r0 + EDGE, 8), TILE), :] = v
                gd_out[b, pl.ds(r0, TILE), lanes] = v
                return 0

            lax.fori_loop(0, half // TILE, step, 0)

            def step2(i, _, b=b, length=length):
                r0 = pl.multiple_of(i * TILE, 16)
                acc = jnp.zeros((TILE, 128), F32)
                for o in range(TAPS):
                    acc = acc + pad[b, j, pl.ds(r0 + TAPS - o, TILE), :] * prm[o : o + 1, lanes]
                acc = acc * tile_mask(pos + r0, TILE, length)
                val = proj[b, pl.ds(r0, TILE), lanes]
                g = jax.nn.sigmoid(proj[b, pl.ds(r0, TILE), high])
                gp[b, pl.ds(r0, TILE), lanes] = (acc * g).astype(BF16)
                gp[b, pl.ds(r0, TILE), high] = (acc * val * g * (1.0 - g)).astype(BF16)
                return 0

            lax.fori_loop(0, half // TILE, step2, 0)


def backward(s, depth, gbo, lo, hi, sums, bn, prm, proj):
    recs, half, chans = depth.shape
    return pl.pallas_call(
        back_body,
        in_specs=[SMEM] + [VMEM] * 8,
        out_specs=[VMEM, VMEM],
        out_shape=[sds(depth.shape, F32), sds((recs, half, 2 * chans), BF16)],
        scratch_shapes=[pltpu.VMEM((recs, chans // 128, half + 2 * EDGE, 128), F32)],
        compiler_params=LIMIT,
        cost_estimate=LONG,
        name="backward",
    )(s, depth, gbo, lo, hi, sums, bn, prm, proj)


def taps_body(gd, glu, lo, hi, gwd, pad):
    recs, half, chans = glu.shape
    fill(pad, glu, lo, hi)
    gwd[...] = jnp.zeros_like(gwd)
    for j in range(chans // 128):
        lanes = slice(128 * j, 128 * j + 128)
        accs = tuple(jnp.zeros((8, 128), F32) for _ in range(TAPS))
        for b in range(recs):

            def step(i, accs, b=b):
                r0 = pl.multiple_of(i * 16, 16)
                new = list(accs)
                for k in range(2):
                    g = gd[b, pl.ds(r0 + 8 * k, 8), lanes]
                    for o in range(TAPS):
                        new[o] = new[o] + g * pad[b, j, pl.ds(r0 + 8 * k + o + 1, 8), :]
                return tuple(new)

            accs = lax.fori_loop(0, half // 16, step, accs)
        for o in range(TAPS):
            gwd[o : o + 1, lanes] = jnp.sum(accs[o], axis=0, keepdims=True)


def taps_grad(gd, glu, lo, hi):
    recs, half, chans = glu.shape
    return pl.pallas_call(
        taps_body,
        in_specs=[VMEM] * 4,
        out_specs=VMEM,
        out_shape=sds((32, chans), F32),
        scratch_shapes=[pltpu.VMEM((recs, chans // 128, half + 2 * EDGE, 128), F32)],
        compiler_params=LIMIT,
        cost_estimate=LONG,
        name="taps_grad",
    )(gd, glu, lo, hi)


def rows_body(gp, proj, gw, rs):
    recs, half, _ = gp.shape
    gsum = gw[0:1, :] + gw[1:2, :]
    shift = gw[2:3, :] + gw[3:4, :]
    for b in range(recs):

        def step2(i, _, b=b):
            r0 = pl.multiple_of(i * 48, 16)
            g = gp[b, pl.ds(r0, 48), :].astype(F32)
            rs[b, pl.ds(r0, 48), 0:1] = jnp.sum(g * gsum, axis=1, keepdims=True)
            rs[b, pl.ds(r0, 48), 1:2] = jnp.sum(g * (proj[b, pl.ds(r0, 48), :] - shift), axis=1, keepdims=True)
            return 0

        lax.fori_loop(0, half // 48, step2, 0)


def row_sums(gp, proj, gw):
    recs, half, n2 = gp.shape
    return pl.pallas_call(
        rows_body,
        in_specs=[VMEM] * 3,
        out_specs=VMEM,
        out_shape=sds((recs, half, 2), F32),
        compiler_params=LIMIT,
        cost_estimate=cost(recs * half * n2 * 8, recs * half * n2 * 6),
        name="row_sums",
    )(gp, proj, gw)


def through_body(gain, bias, w, out):
    def split(v):
        top = v.astype(BF16).astype(F32)
        return top, v - top

    g1, g2 = split(gain[...])
    b1, b2 = split(bias[...])
    row = lax.broadcasted_iota(jnp.int32, (16, gain.shape[1]), 0)
    v = jnp.where(row == 0, g1, jnp.where(row == 1, g2, jnp.where(row == 2, b1, jnp.where(row == 3, b2, 0.0))))
    out[...] = jnp.dot(v.astype(BF16), w[...], preferred_element_type=F32)


def through(gain, bias, w):
    return pl.pallas_call(
        through_body,
        in_specs=[VMEM] * 3,
        out_specs=VMEM,
        out_shape=sds((16, w.shape[1]), F32),
        compiler_params=LIMIT,
        cost_estimate=cost(32 * w.shape[0] * w.shape[1], 2 * w.shape[0] * w.shape[1]),
        name="through",
    )(gain[None], bias[None], w)


def turn_body(w, out, cat):
    n = w.shape[1]
    for d in range(4):
        cat[0:n, :] = w[d]
        cat[n:, :] = w[d + 4]
        out[d] = cat[...].T


def turned(w):
    n, depth = w.shape[0] // 8, w.shape[1]
    return pl.pallas_call(
        turn_body,
        in_specs=[VMEM],
        out_specs=VMEM,
        out_shape=sds((4, depth, 2 * n), BF16),
        scratch_shapes=[pltpu.VMEM((2 * n, depth), BF16)],
        compiler_params=LIMIT,
        cost_estimate=cost(32 * n * depth, 32 * n * depth),
        name="turned",
    )(w.reshape(8, n, depth))


def blocks_body(s, lhs, w, *refs, jobs, adds):
    plus, outs = refs[:adds], refs[adds:]
    half = lhs.shape[1]
    for rec, r, to, at in jobs:
        v = jnp.dot(lhs[rec], w[lax.rem(s[S_X] + r, 4)], preferred_element_type=F32)
        if adds:
            v = v + plus[to][0:half, :].astype(F32)
        outs[to][at * half : (at + 1) * half, :] = v.astype(BF16)


def blocks(s, lhs, w4, jobs, plus=()):
    recs, half, depth = lhs.shape
    n = w4.shape[2]
    each = len(jobs) // 2
    return pl.pallas_call(
        functools.partial(blocks_body, jobs=jobs, adds=len(plus)),
        in_specs=[SMEM] + [VMEM] * (2 + len(plus)),
        out_specs=[VMEM] * 2,
        out_shape=[sds((each * half, n), BF16)] * 2,
        compiler_params=LIMIT,
        cost_estimate=cost(2 * half * depth * n * len(jobs), 4 * half * depth + 8 * n * depth),
        name="blocks",
    )(s, lhs, w4, *plus)


def finish_body(s, lhs, w, up, down, last_a, last_b, keep, give):
    half = lhs.shape[1]
    n = w.shape[2] // 2
    first = s[S_YL] == 0
    for rec, (one, two) in enumerate(((last_a, down), (last_b, up))):
        v = jnp.dot(lhs[rec], w[s[S_X]], preferred_element_type=F32)
        v = v + one[...].astype(F32) + two[half:, :].astype(F32)
        low, high = v[:, :n], v[:, n:]
        keep[:, rec * n : (rec + 1) * n] = jnp.where(first, low, high)
        give[:, rec * n : (rec + 1) * n] = jnp.where(first, high, low).astype(BF16)


def finish(s, lhs, w4, parts):
    recs, half, depth = lhs.shape
    n = w4.shape[2] // 2
    return pl.pallas_call(
        finish_body,
        in_specs=[SMEM] + [VMEM] * 6,
        out_specs=[VMEM] * 2,
        out_shape=[sds((half, recs * n), F32), sds((half, recs * n), BF16)],
        compiler_params=LIMIT,
        cost_estimate=LONG,
        name="finish",
    )(s, lhs, w4, *parts)


def hop(v, axis, by):
    n = lax.axis_size(axis)
    return lax.ppermute(v, axis, [(i, (i + by) % n) for i in range(n)])


def sum_start(s, lhs, w8):
    sent = blocks(s, lhs, w8, ((0, 2, 0, 0), (1, 2, 1, 0), (1, 1, 0, 1), (0, 3, 1, 1)))
    return (hop(sent[0], "x", 1), hop(sent[1], "x", -1)), sent[0]


def sum_middle(s, lhs, w8, got):
    sent = blocks(s, lhs, w8, ((0, 1, 0, 0), (1, 3, 1, 0)), got)
    return (hop(sent[0], "x", 1), hop(sent[1], "x", -1)), sent[0]


def sum_end(s, lhs, w8, got, last):
    keep, give = finish(s, lhs, w8, (*got, *last))
    return keep, hop(give, "yl", 1)


def after(values, *first):
    return lax.optimization_barrier((*values, *first))[: len(values)]


def pick(block, odd):
    n = block.shape[1] // 2
    return jnp.where(odd == 1, block[:, n:].astype(F32), block[:, :n].astype(F32))


def halves(s, keep, got):
    n = keep.shape[1] // 2
    early = pl.program_id(0) == 0
    mine = jnp.where(early, keep[:, :n], keep[:, n:])
    theirs = jnp.where(early, got[:, :n].astype(F32), got[:, n:].astype(F32))
    first = s[S_YL] == 0
    return jnp.where(first, mine, theirs), jnp.where(first, theirs, mine)


def out_body(s, keep, got, fr, out):
    half = keep.shape[0]
    for h, v in enumerate(halves(s, keep, got)):
        rows = slice(h * half, h * half + half)
        out[0, :, rows] = (pick(fr[0, rows, :], s[S_ODD]) + v).T.astype(BF16)


def frames_body(s, keep, got, fr, go, stat, rs, gain, out):
    half = keep.shape[0]
    width = 8 * out.shape[1]
    for h, v in enumerate(halves(s, keep, got)):
        rows = slice(h * half, h * half + half)
        g = v * gain[...]
        mean, rstd = stat[0, rows, 0:1], stat[0, rows, 1:2]
        first, second = rs[h, 0, :, 0:1], rs[h, 0, :, 1:2]
        hat = (pick(fr[0, rows, :], s[S_ODD]) - mean) * rstd
        v = rstd * (g - first / width - hat * (second / width)) + pick(go[0, rows, :], s[S_ODD])
        out[0, :, rows] = v.T.astype(BF16)


def last_call(body, s, keep, got, wide, extra, extra_specs, name):
    recs, length, _ = wide[0].shape
    half, n = length // 2, keep.shape[1] // 2
    cols = pl.BlockSpec((1, 2 * half, 2 * n), lambda b, s: (b, 0, s[S_PAIR]))
    return pl.pallas_call(
        body,
        grid_spec=pltpu.PrefetchScalarGridSpec(
            num_scalar_prefetch=1,
            grid=(recs,),
            in_specs=[
                pl.BlockSpec((half, recs * n), lambda b, s: (0, 0)),
                pl.BlockSpec((half, recs * n), lambda b, s: (0, 0)),
            ]
            + [cols] * len(wide)
            + extra_specs,
            out_specs=pl.BlockSpec((1, n, 2 * half), lambda b, s: (b, 0, 0)),
        ),
        out_shape=sds((recs, n, 2 * half), BF16),
        compiler_params=LIMIT,
        cost_estimate=LONG,
        name=name,
    )(s, keep, got, *wide, *extra).transpose(0, 2, 1)


def spread(v, axes):
    n = lax.axis_size(axes)
    return lax.all_to_all(jnp.broadcast_to(v[None], (n, *v.shape)), axes, 0, 0, tiled=True)


def on_device(frames, ln_gain, ln_bias, w_in, w_depth, bn_gain, bn_bias, w_out, lengths, grad_out):
    recs, length, width = frames.shape
    shard, _, own = w_in.shape
    half = length // 2
    chans = 2 * own
    yh, z, c, yl, x = (lax.axis_index(a) for a in ("yh", "z", "c", "yl", "x"))
    ctx = (yh * 4 + z) * 2 + c
    chan = yl * 4 + x
    time = ctx * 2 + yl
    s = jnp.stack([yl, x, chan // 2, chan % 2, time * half, lengths[0], lengths[1], z, c, yh]).astype(jnp.int32)

    w3 = jnp.concatenate([w_in.reshape(shard, 2 * own), w_out], axis=1)
    w_yl = hop(w3, "yl", 1)
    w_yh = hop(w3, "yh", 1)
    w_xx = lax.ppermute(w3, ("yh", "yl"), [(i, 3 - i) for i in range(4)])

    def paired(a, b, g0, g1):
        lo, hi = jnp.where(yl == 0, a, b), jnp.where(yl == 0, b, a)
        cols = []
        for g in range(g0, g1):
            cols += [lo[:, g * own : (g + 1) * own], hi[:, g * own : (g + 1) * own]]
        return jnp.concatenate(cols, axis=1)

    def rows_two(g0, g1):
        same, other = paired(w3, w_yl, g0, g1), paired(w_yh, w_xx, g0, g1)
        return jnp.where(yh == 0, jnp.stack([same, other]), jnp.stack([other, same]))

    def gathered(v, first):
        pieces = []
        for r in range(4):
            p = v if r == 0 else hop(v, "z", -r)
            if first is not None:
                (p,) = after([p], first)
            pieces += [p, hop(p, "c", 1)]
        return pieces

    prm1 = jnp.concatenate([w_depth, bn_gain[None], bn_bias[None], jnp.zeros((7, own), F32)], axis=0)
    prm2 = hop(prm1, "yl", 1)
    prm = jnp.where(yl == 0, jnp.concatenate([prm1, prm2], axis=1), jnp.concatenate([prm2, prm1], axis=1))
    (in_two,) = after([rows_two(0, 2)], prm2)
    normed, stat = layer_norm(s, *after([frames, ln_gain, ln_bias], in_two))
    in_pieces = gathered(in_two, normed)
    out_pieces = gathered(*after([rows_two(2, 3)], *in_pieces), None)
    proj, glu, w_in_all = project(s, normed, in_pieces, half)
    glu = glu.reshape(recs, half, chans)
    proj = proj.reshape(recs, half, 2 * chans)
    devices = lax.axis_size(TIME)
    up = [(i, i + 1) for i in range(devices - 1)]
    down = [(i + 1, i) for i in range(devices - 1)]
    g_lo = lax.ppermute(glu[:, half - EDGE :], TIME, up)
    g_hi = lax.ppermute(glu[:, :EDGE], TIME, down)
    gact, w_out_all = grad_act(s, grad_out, out_pieces)
    (glu_c,) = after([glu], gact)
    depth, bn_own = conv(s, glu_c, g_lo, g_hi, prm)
    bn_all = spread(bn_own, TIME).reshape(devices, 2 * chans)
    w_out_4 = turned(*after([w_out_all], bn_own))
    w_in_4 = turned(*after([w_in_all], bn_own))
    g_w = through(*after([ln_gain, ln_bias, w_in_all], bn_own))
    (gact,) = after([gact], w_out_4, w_in_4, g_w)
    act, gbo, sums_own, bn = activate(s, depth, gact, bn_all, prm)
    sums = spread(sums_own, TIME).reshape(devices, 2 * chans)
    e_lo = lax.ppermute(jnp.stack([depth[:, half - EDGE :], gbo[:, half - EDGE :]]), TIME, up)
    e_hi = lax.ppermute(jnp.stack([depth[:, :EDGE], gbo[:, :EDGE]]), TIME, down)

    out_first, sent = sum_start(s, *after([act], e_lo, e_hi), w_out_4)
    depth, gbo = after([depth, gbo], sent)
    gd, gp = backward(s, depth, gbo, e_lo, e_hi, sums, bn, prm, proj)
    gn_first, sent = sum_start(s, gp, w_in_4)
    (act_m,) = after([act], sent)
    out_last, sent = sum_middle(s, act_m, w_out_4, out_first)
    gd, glu = after([gd, glu], sent)
    gwd = taps_grad(gd, glu, g_lo, g_hi)
    (gp_r,) = after([gp], gwd)
    rs = row_sums(gp_r, proj, g_w)
    (act_e,) = after([act], rs)
    out_keep, out_got = sum_end(s, act_e, w_out_4, out_first, out_last)
    (gp_m,) = after([gp], out_keep)
    gn_last, sent = sum_middle(s, gp_m, w_in_4, gn_first)
    (gp_w,) = after([gp], sent)
    mine, theirs, tu = weight_grads(
        s,
        normed,
        gp_w.reshape(recs * half, 2 * chans),
        grad_out,
        act.reshape(recs * half, chans),
        w_in_all,
    )

    tu = tu.T.reshape(2, 2, 4, own).transpose(1, 2, 0, 3)
    mine_x = (jnp.arange(4) == x).astype(F32)[None, :, None, None]
    taps4 = gwd[:TAPS].reshape(TAPS, 2, own).transpose(1, 0, 2)[:, None] * mine_x
    rs_rows = recs * 2 * half // own
    rs8 = jnp.broadcast_to(rs.transpose(2, 0, 1).reshape(1, 1, rs_rows, own), (2, 4, rs_rows, own))
    small = jnp.concatenate([taps4, tu, rs8], axis=2).reshape(8, TAPS + 2 + rs_rows, own)

    (gp_e,) = after([gp], mine)
    gn_keep, gn_got = sum_end(s, gp_e, w_in_4, gn_first, gn_last)
    mine, theirs, out_keep = after([mine, theirs, out_keep], gn_keep)
    parts = core_sum(s, mine, hop(theirs, "c", 1))
    (small,) = after([small], gn_keep)
    small = lax.all_to_all(small, CHAN, 0, 0, tiled=True)
    rs_all = jnp.sum(small[:, TAPS + 2 :].reshape(2, 4, 2, recs, half), axis=1).transpose(0, 2, 3, 1)
    small = jnp.sum(small[:, : TAPS + 2], axis=0)
    block_out = last_call(out_body, s, out_keep, out_got, [frames], [], [], "block_out")
    (small,) = after([small], parts[0])
    small = jnp.sum(spread(small, CTX), axis=0)

    own_gain = lax.dynamic_slice_in_dim(ln_gain, chan * own, own, 0)
    own_bias = lax.dynamic_slice_in_dim(ln_bias, chan * own, own, 0)
    grad_frames = last_call(
        frames_body,
        s,
        gn_keep,
        gn_got,
        [frames, grad_out],
        [stat, rs_all, own_gain[None]],
        [
            pl.BlockSpec((1, length, 2), lambda b, s: (b, 0, 0)),
            pl.BlockSpec((2, 1, half, 2), lambda b, s: (0, b, 0, 0)),
            pl.BlockSpec((1, own), lambda b, s: (0, 0)),
        ],
        "grad_frames",
    )

    parts = [parts[0]] + [hop(parts[r], "z", r) for r in range(1, 4)]
    g_fin, to_yl, to_yh, to_xx = ring_sum(s, parts)
    g_fin = g_fin + hop(to_yl, "yl", 1).astype(F32) + hop(to_yh, "yh", 1).astype(F32)
    g_fin = g_fin + lax.ppermute(to_xx, ("yh", "yl"), [(i, 3 - i) for i in range(4)]).astype(F32)
    grad_w_in = g_fin[:, : 2 * own].reshape(shard, 2, own)
    grad_w_out = g_fin[:, 2 * own :]

    grad_w_depth = small[:TAPS]
    t, u = small[TAPS], small[TAPS + 1]
    grad_ln = jnp.stack([(t - own_bias * u) / own_gain, u])
    grad_bn = lax.dynamic_index_in_dim(jnp.sum(sums, axis=0).reshape(2, 2, own), yl, 1, False)
    return (block_out, grad_frames, grad_w_in, grad_w_out, grad_w_depth, grad_bn, grad_ln)


def solution(mesh):
    split = Mesh(mesh.devices.reshape(2, 4, 2, 2, 4), ("yh", "z", "c", "yl", "x"))
    placed = (
        P(None, CTX, None),
        P(),
        P(),
        P(CTX, None, CHAN),
        P(None, CHAN),
        P(CHAN),
        P(CHAN),
        P(CTX, CHAN),
        P(),
        P(None, CTX, None),
    )
    return jax.shard_map(
        on_device,
        mesh=split,
        in_specs=placed,
        out_specs=(
            P(None, CTX, CHAN),
            P(None, CTX, CHAN),
            P(CTX, None, CHAN),
            P(CTX, CHAN),
            P(None, CHAN),
            P(None, CHAN),
            P(None, CHAN),
        ),
        check_vma=False,
    )
```

```python
import functools

import jax
import jax.numpy as jnp
from jax import lax
from jax.experimental import pallas as pl
from jax.experimental.pallas import tpu as pltpu
from jax.sharding import Mesh
from jax.sharding import PartitionSpec as P

F32 = jnp.float32
BF16 = jnp.bfloat16
CTX = ("yh", "z", "c")
CHAN = ("yl", "x")
TIME = ("yh", "z", "c", "yl")
EPS = 1e-05
TAPS = 31
EDGE = 16
LIMIT = pltpu.CompilerParams(vmem_limit_bytes=50 * 1024 * 1024)

S_YL, S_X, S_PAIR, S_ODD, S_POS, S_LEN, S_Z, S_C, S_YH = 0, 1, 2, 3, 4, 5, 7, 8, 9

SMEM = pl.BlockSpec(memory_space=pltpu.SMEM)
VMEM = pl.BlockSpec(memory_space=pltpu.VMEM)
ANY = pl.BlockSpec(memory_space=pl.ANY)


def cost(flops, nbytes):
    return pl.CostEstimate(flops=flops // 50, bytes_accessed=nbytes // 50, transcendentals=0)


LONG = pl.CostEstimate(flops=0, bytes_accessed=100 * 1024 * 1024, transcendentals=0)


def sds(shape, dtype):
    return jax.ShapeDtypeStruct(shape, dtype)


def nt(a, b):
    return lax.dot_general(a, b, (((1,), (1,)), ((), ())), preferred_element_type=F32)


def ln_body(s, fr, gain, bias, normed, stat):
    v = fr[0].astype(F32)
    mean = jnp.mean(v, axis=-1, keepdims=True)
    cen = v - mean
    rstd = lax.rsqrt(jnp.mean(cen * cen, axis=-1, keepdims=True) + EPS)
    stat[0, :, 0:1] = mean
    stat[0, :, 1:2] = rstd

    @pl.when(pl.program_id(0) == 0)
    def _():
        normed[...] = (cen * rstd * gain[...] + bias[...]).astype(BF16)


def layer_norm(s, frames, gain, bias):
    recs, length, width = frames.shape
    blk = length // 4

    def rows(h, b, i, s):
        return (b, jnp.where(h == 0, s[S_YL], 1 - s[S_YL]) * 2 + i, 0)

    return pl.pallas_call(
        ln_body,
        grid_spec=pltpu.PrefetchScalarGridSpec(
            num_scalar_prefetch=1,
            grid=(2, recs, 2),
            in_specs=[
                pl.BlockSpec((1, blk, width), rows),
                pl.BlockSpec((1, width), lambda h, b, i, s: (0, 0)),
                pl.BlockSpec((1, width), lambda h, b, i, s: (0, 0)),
            ],
            out_specs=[
                pl.BlockSpec((blk, width), lambda h, b, i, s: (jnp.where(h == 0, b * 2 + i, 2 * recs - 1), 0)),
                pl.BlockSpec((1, blk, 2), rows),
            ],
        ),
        out_shape=[sds((recs * length // 2, width), BF16), sds((recs, length, 2), F32)],
        compiler_params=LIMIT,
        cost_estimate=cost(recs * length * width * 10, 4 * recs * length * width),
        name="layer_norm",
    )(s, frames, gain[None], bias[None])


def place(s, pieces, out):
    z, c = s[S_Z], s[S_C]
    n = pieces[0].shape[1]
    for r in range(4):
        for k in range(2):
            for h in range(2):
                row = (h * 4 + lax.rem(z + r, 4)) * 2 + (c if k == 0 else 1 - c)
                out[pl.ds(pl.multiple_of(row * n, n), n), :] = pieces[2 * r + k][h]


def proj_body(s, normed, *refs, blk, half):
    pieces, (proj, glu, w) = refs[:8], refs[8:]
    i = pl.program_id(0)

    @pl.when(i == 0)
    def _():
        place(s, pieces, w)

    p = jnp.dot(normed[...], w[...], preferred_element_type=F32)
    proj[...] = p
    n = p.shape[1] // 2
    b = i // (half // blk)
    t = s[S_POS] + (i % (half // blk)) * blk + lax.broadcasted_iota(jnp.int32, (blk, 1), 0)
    valid = (t < s[S_LEN + b]).astype(F32)
    glu[...] = (p[:, :n] * jax.nn.sigmoid(p[:, n:]) * valid).astype(BF16)


def project(s, normed, pieces, half):
    rows, width = normed.shape
    _, shard, n2 = pieces[0].shape
    blk = half
    return pl.pallas_call(
        functools.partial(proj_body, blk=blk, half=half),
        grid_spec=pltpu.PrefetchScalarGridSpec(
            num_scalar_prefetch=1,
            grid=(rows // blk,),
            in_specs=[pl.BlockSpec((blk, width), lambda i, s: (i, 0))] + [VMEM] * 8,
            out_specs=[
                pl.BlockSpec((blk, n2), lambda i, s: (i, 0)),
                pl.BlockSpec((blk, n2 // 2), lambda i, s: (i, 0)),
                pl.BlockSpec((16 * shard, n2), lambda i, s: (0, 0)),
            ],
        ),
        out_shape=[sds((rows, n2), F32), sds((rows, n2 // 2), BF16), sds((16 * shard, n2), BF16)],
        compiler_params=LIMIT,
        cost_estimate=cost(2 * rows * width * n2, 2 * rows * width + 5 * rows * n2),
        name="project",
    )(s, normed, *pieces)


def gact_body(s, go, *refs):
    pieces, (out, w) = refs[:8], refs[8:]

    @pl.when((pl.program_id(0) == 0) & (pl.program_id(1) == 0))
    def _():
        place(s, pieces, w)

    out[0] = jnp.dot(go[0], w[...], preferred_element_type=F32)


def grad_act(s, grad_out, pieces):
    recs, length, width = grad_out.shape
    _, shard, n = pieces[0].shape
    blk = length // 2
    return pl.pallas_call(
        gact_body,
        grid_spec=pltpu.PrefetchScalarGridSpec(
            num_scalar_prefetch=1,
            grid=(recs, 1),
            in_specs=[pl.BlockSpec((1, blk, width), lambda b, i, s: (b, s[S_YL] + i, 0))] + [VMEM] * 8,
            out_specs=[
                pl.BlockSpec((1, blk, n), lambda b, i, s: (b, i, 0)),
                pl.BlockSpec((16 * shard, n), lambda b, i, s: (0, 0)),
            ],
        ),
        out_shape=[sds((recs, length // 2, n), F32), sds((16 * shard, n), BF16)],
        compiler_params=LIMIT,
        cost_estimate=cost(recs * length * width * n, recs * length * (width + 2 * n)),
        name="grad_act",
    )(s, grad_out, *pieces)


def tn(a, b):
    return lax.dot_general(a, b, (((0,), (0,)), ((), ())), preferred_element_type=F32)


def wgrad_body(s, normed, gp, go, act, w, mine, theirs, tu, colsum):
    shard = mine.shape[1]
    n2 = gp.shape[1]

    @pl.when(pl.program_id(0) == 0)
    def _():
        colsum[...] = jnp.sum(gp[...].astype(F32), axis=0, keepdims=True)

    g_in = tn(normed[...], gp[...])
    wide = w[...].astype(F32)
    tu[:, 0:1] = jnp.sum(wide * g_in, axis=1, keepdims=True)
    tu[:, 1:2] = jnp.sum(wide * colsum[...], axis=1, keepdims=True)
    g_out = tn(go[...].reshape(-1, go.shape[2]), act[...])
    first = s[S_C] == 0
    for i in range(2):
        r0 = 2 * i * shard
        for g, cols in ((g_in, slice(0, n2)), (g_out, slice(n2, n2 + g_out.shape[1]))):
            top, low = g[r0 : r0 + shard], g[r0 + shard : r0 + 2 * shard]
            mine[i, :, cols] = jnp.where(first, top, low).astype(BF16)
            theirs[i, :, cols] = jnp.where(first, low, top).astype(BF16)


def weight_grads(s, normed, gp, grad_out, act, w):
    rows, width = normed.shape
    n2, n = gp.shape[1], act.shape[1]
    recs, length, _ = grad_out.shape
    blk = width // 4
    shard = width // 16
    part = pl.BlockSpec((2, shard, n2 + n), lambda k, s: (k, 0, 0))
    return pl.pallas_call(
        wgrad_body,
        grid_spec=pltpu.PrefetchScalarGridSpec(
            num_scalar_prefetch=1,
            grid=(4,),
            in_specs=[
                pl.BlockSpec((rows, blk), lambda k, s: (0, k)),
                pl.BlockSpec((rows, n2), lambda k, s: (0, 0)),
                pl.BlockSpec((recs, length // 2, blk), lambda k, s: (0, s[S_YL], k)),
                pl.BlockSpec((rows, n), lambda k, s: (0, 0)),
                pl.BlockSpec((blk, n2), lambda k, s: (k, 0)),
            ],
            out_specs=[part, part, pl.BlockSpec((blk, 2), lambda k, s: (k, 0))],
            scratch_shapes=[pltpu.VMEM((1, n2), F32)],
        ),
        out_shape=[sds((8, shard, n2 + n), BF16)] * 2 + [sds((width, 2), F32)],
        compiler_params=LIMIT,
        cost_estimate=cost(2 * rows * width * (n2 + n), 4 * rows * width),
        name="weight_grads",
    )(s, normed, gp, grad_out, act, w)


def core_body(s, mine, got, *outs):
    for r, out in enumerate(outs):
        q = lax.rem(s[S_Z] + r, 4)
        for h in range(2):
            out[h] = (mine[h * 4 + q].astype(F32) + got[h * 4 + q].astype(F32)).astype(BF16)


def core_sum(s, mine, got):
    _, shard, n = mine.shape
    return pl.pallas_call(
        core_body,
        in_specs=[SMEM, VMEM, VMEM],
        out_specs=[VMEM] * 4,
        out_shape=[sds((2, shard, n), BF16)] * 4,
        compiler_params=LIMIT,
        cost_estimate=cost(16 * shard * n, 48 * shard * n),
        name="core_sum",
    )(s, mine, got)


def ring_body(s, p0, p1, p2, p3, own, to_yl, to_yh, to_xx):
    n = own.shape[1] // 3

    def total(h):
        return p0[h].astype(F32) + p1[h].astype(F32) + p2[h].astype(F32) + p3[h].astype(F32)

    first = s[S_YL] == 0
    for v, here, there in ((total(s[S_YH]), own, to_yl), (total(1 - s[S_YH]), to_yh, to_xx)):
        for g in range(3):
            low, high = v[:, 2 * g * n : (2 * g + 1) * n], v[:, (2 * g + 1) * n : (2 * g + 2) * n]
            cols = slice(g * n, g * n + n)
            here[:, cols] = jnp.where(first, low, high).astype(here.dtype)
            there[:, cols] = jnp.where(first, high, low).astype(there.dtype)


def ring_sum(s, parts):
    _, shard, n = parts[0].shape
    return pl.pallas_call(
        ring_body,
        in_specs=[SMEM] + [VMEM] * 4,
        out_specs=[VMEM] * 4,
        out_shape=[sds((shard, n // 2), F32)] + [sds((shard, n // 2), BF16)] * 3,
        compiler_params=LIMIT,
        cost_estimate=cost(8 * shard * n, 24 * shard * n),
        name="ring_sum",
    )(s, *parts)


def fill(pad, mid, lo, hi):
    recs, half = mid.shape[0], mid.shape[1]
    for b in range(recs):
        for j in range(mid.shape[2] // 128):
            lanes = slice(128 * j, 128 * j + 128)
            pad[b, j, 0:EDGE, :] = lo[b, :, lanes].astype(F32)
            pad[b, j, EDGE : EDGE + half, :] = mid[b, :, lanes].astype(F32)
            pad[b, j, EDGE + half :, :] = hi[b, :, lanes].astype(F32)


def tile_mask(start, rows, length):
    t = start + lax.broadcasted_iota(jnp.int32, (rows, 128), 0)
    return ((t >= 0) & (t < length)).astype(F32)


def local_count(s, half):
    n = jnp.int32(0)
    for b in range(2):
        n = n + jnp.clip(s[S_LEN + b] - s[S_POS], 0, half)
    return jnp.maximum(n, 1).astype(F32)


def fold(v):
    return jnp.sum(v.reshape(-1, 8, v.shape[1]), axis=0)


TILE = 96


def conv_body(s, glu, lo, hi, w, depth, stat, pad):
    recs, half, chans = glu.shape
    fill(pad, glu, lo, hi)
    count = local_count(s, half)
    for j in range(chans // 128):
        lanes = slice(128 * j, 128 * j + 128)
        total = jnp.zeros((8, 128), F32)
        for b in range(recs):

            def step(i, total, b=b):
                r0 = pl.multiple_of(i * TILE, 8)
                acc = jnp.zeros((TILE, 128), F32)
                for o in range(TAPS):
                    acc = acc + pad[b, j, pl.ds(r0 + o + 1, TILE), :] * w[o : o + 1, lanes]
                depth[b, pl.ds(r0, TILE), lanes] = acc
                return total + fold(acc * tile_mask(s[S_POS] + r0, TILE, s[S_LEN + b]))

            total = lax.fori_loop(0, half // TILE, step, total)
        mean = jnp.sum(total, axis=0, keepdims=True) / count
        spread = jnp.zeros((8, 128), F32)
        for b in range(recs):

            def step2(i, spread, b=b):
                r0 = pl.multiple_of(i * TILE, 8)
                d = (depth[b, pl.ds(r0, TILE), lanes] - mean) * tile_mask(s[S_POS] + r0, TILE, s[S_LEN + b])
                return spread + fold(d * d)

            spread = lax.fori_loop(0, half // TILE, step2, spread)
        stat[0:1, lanes] = mean
        stat[0:1, slice(chans + 128 * j, chans + 128 * j + 128)] = jnp.sum(spread, axis=0, keepdims=True)


def conv(s, glu, lo, hi, w):
    recs, half, chans = glu.shape
    return pl.pallas_call(
        conv_body,
        in_specs=[SMEM, VMEM, VMEM, VMEM, VMEM],
        out_specs=[VMEM, VMEM],
        out_shape=[sds((recs, half, chans), F32), sds((1, 2 * chans), F32)],
        scratch_shapes=[pltpu.VMEM((recs, chans // 128, half + 2 * EDGE, 128), F32)],
        compiler_params=LIMIT,
        cost_estimate=cost(recs * half * chans * 62 * 50, recs * half * chans * 6),
        name="conv",
    )(s, glu, lo, hi, w)


def bn_stats(s, got, half, chans):
    dev = got.shape[0]
    start = half * lax.broadcasted_iota(jnp.int32, (dev, 1), 0)
    n = jnp.zeros((dev, 1), jnp.int32)
    for b in range(2):
        n = n + jnp.clip(s[S_LEN + b] - start, 0, half)
    n = n.astype(F32)
    count = (s[S_LEN].astype(F32)) + (s[S_LEN + 1].astype(F32))
    means, spread = got[:, :chans], got[:, chans:]
    mean = jnp.sum(n * means, axis=0, keepdims=True) / count
    var = jnp.sum(spread + n * (means - mean) ** 2, axis=0, keepdims=True) / count
    return mean, lax.rsqrt(var + EPS), count


def act_body(s, depth, gact, got, prm, act, gbo, sums, bn, *, half):
    b = pl.program_id(0)
    i = pl.program_id(1)
    rows, chans = depth.shape[1], depth.shape[2]

    @pl.when((b == 0) & (i == 0))
    def _():
        mean, rstd, _ = bn_stats(s, got, half, chans)
        bn[0:1, :] = mean
        bn[1:2, :] = rstd
        sums[...] = jnp.zeros_like(sums)

    for j in range(chans // 128):
        lanes = slice(128 * j, 128 * j + 128)
        high = slice(chans + 128 * j, chans + 128 * j + 128)
        mean, rstd = bn[0:1, lanes], bn[1:2, lanes]
        gain, bias = prm[31:32, lanes], prm[32:33, lanes]
        one = jnp.zeros((8, 128), F32)
        two = jnp.zeros((8, 128), F32)
        for k in range(rows // TILE):
            r = slice(k * TILE, k * TILE + TILE)
            hat = (depth[0, r, lanes] - mean) * rstd
            out = hat * gain + bias
            g = jax.nn.sigmoid(out)
            m = tile_mask(s[S_POS] + i * rows + k * TILE, TILE, s[S_LEN + b])
            act[0, r, lanes] = (out * g * m).astype(BF16)
            gb = gact[0, r, lanes] * m * (g * (1.0 + out * (1.0 - g)))
            gbo[0, r, lanes] = gb
            one = one + fold(gb * hat)
            two = two + fold(gb)
        sums[0:1, lanes] += jnp.sum(one, axis=0, keepdims=True)
        sums[0:1, high] += jnp.sum(two, axis=0, keepdims=True)


def activate(s, depth, gact, got, prm):
    recs, half, chans = depth.shape
    blk = half // 2
    block = pl.BlockSpec((1, blk, chans), lambda b, i, s: (b, i, 0))
    whole = lambda a: pl.BlockSpec(a.shape, lambda b, i, s: (0, 0))
    return pl.pallas_call(
        functools.partial(act_body, half=half),
        grid_spec=pltpu.PrefetchScalarGridSpec(
            num_scalar_prefetch=1,
            grid=(recs, 2),
            in_specs=[block, block, whole(got), whole(prm)],
            out_specs=[block, block, pl.BlockSpec((1, 2 * chans), lambda b, i, s: (0, 0)), pl.BlockSpec((8, chans), lambda b, i, s: (0, 0))],
        ),
        out_shape=[sds(depth.shape, BF16), sds(depth.shape, F32), sds((1, 2 * chans), F32), sds((8, chans), F32)],
        compiler_params=LIMIT,
        cost_estimate=cost(recs * half * chans * 200, recs * half * chans * 14),
        name="activate",
    )(s, depth, gact, got, prm)


def back_body(s, depth, gbo, lo, hi, sums, bn, prm, proj, gd_out, gp, pad):
    recs, half, chans = depth.shape
    total = jnp.sum(sums[...], axis=0, keepdims=True)
    count = (s[S_LEN].astype(F32)) + (s[S_LEN + 1].astype(F32))
    pos = s[S_POS]
    for j in range(chans // 128):
        lanes = slice(128 * j, 128 * j + 128)
        high = slice(chans + 128 * j, chans + 128 * j + 128)
        gsum, bsum = total[:, lanes], total[:, high]
        mean, rstd = bn[0:1, lanes], bn[1:2, lanes]
        scale = prm[31:32, lanes] * rstd

        def grad(dep, gb, start, length):
            m = tile_mask(start, dep.shape[0], length)
            hat = (dep - mean) * rstd
            return m * scale * (gb - (bsum + hat * gsum) / count)

        for b in range(recs):
            length = s[S_LEN + b]
            pad[b, j, 0:EDGE, :] = grad(lo[0, b, :, lanes], lo[1, b, :, lanes], pos - EDGE, length)
            pad[b, j, EDGE + half :, :] = grad(hi[0, b, :, lanes], hi[1, b, :, lanes], pos + half, length)

            def step(i, _, b=b, length=length):
                r0 = pl.multiple_of(i * TILE, 8)
                v = grad(depth[b, pl.ds(r0, TILE), lanes], gbo[b, pl.ds(r0, TILE), lanes], pos + r0, length)
                pad[b, j, pl.ds(pl.multiple_of(r0 + EDGE, 8), TILE), :] = v
                gd_out[b, pl.ds(r0, TILE), lanes] = v
                return 0

            lax.fori_loop(0, half // TILE, step, 0)

            def step2(i, _, b=b, length=length):
                r0 = pl.multiple_of(i * TILE, 16)
                acc = jnp.zeros((TILE, 128), F32)
                for o in range(TAPS):
                    acc = acc + pad[b, j, pl.ds(r0 + TAPS - o, TILE), :] * prm[o : o + 1, lanes]
                acc = acc * tile_mask(pos + r0, TILE, length)
                val = proj[b, pl.ds(r0, TILE), lanes]
                g = jax.nn.sigmoid(proj[b, pl.ds(r0, TILE), high])
                gp[b, pl.ds(r0, TILE), lanes] = (acc * g).astype(BF16)
                gp[b, pl.ds(r0, TILE), high] = (acc * val * g * (1.0 - g)).astype(BF16)
                return 0

            lax.fori_loop(0, half // TILE, step2, 0)


def backward(s, depth, gbo, lo, hi, sums, bn, prm, proj):
    recs, half, chans = depth.shape
    return pl.pallas_call(
        back_body,
        in_specs=[SMEM] + [VMEM] * 8,
        out_specs=[VMEM, VMEM],
        out_shape=[sds(depth.shape, F32), sds((recs, half, 2 * chans), BF16)],
        scratch_shapes=[pltpu.VMEM((recs, chans // 128, half + 2 * EDGE, 128), F32)],
        compiler_params=LIMIT,
        cost_estimate=LONG,
        name="backward",
    )(s, depth, gbo, lo, hi, sums, bn, prm, proj)


def taps_body(gd, glu, lo, hi, gwd, pad):
    recs, half, chans = glu.shape
    fill(pad, glu, lo, hi)
    gwd[...] = jnp.zeros_like(gwd)
    for j in range(chans // 128):
        lanes = slice(128 * j, 128 * j + 128)
        accs = tuple(jnp.zeros((8, 128), F32) for _ in range(TAPS))
        for b in range(recs):

            def step(i, accs, b=b):
                r0 = pl.multiple_of(i * 16, 16)
                new = list(accs)
                for k in range(2):
                    g = gd[b, pl.ds(r0 + 8 * k, 8), lanes]
                    for o in range(TAPS):
                        new[o] = new[o] + g * pad[b, j, pl.ds(r0 + 8 * k + o + 1, 8), :]
                return tuple(new)

            accs = lax.fori_loop(0, half // 16, step, accs)
        for o in range(TAPS):
            gwd[o : o + 1, lanes] = jnp.sum(accs[o], axis=0, keepdims=True)


def taps_grad(gd, glu, lo, hi):
    recs, half, chans = glu.shape
    return pl.pallas_call(
        taps_body,
        in_specs=[VMEM] * 4,
        out_specs=VMEM,
        out_shape=sds((32, chans), F32),
        scratch_shapes=[pltpu.VMEM((recs, chans // 128, half + 2 * EDGE, 128), F32)],
        compiler_params=LIMIT,
        cost_estimate=cost(recs * half * chans * 62 * 50, recs * half * chans * 20),
        name="taps_grad",
    )(gd, glu, lo, hi)


def rows_body(gp, proj, gw, rs):
    recs, half, _ = gp.shape
    gsum = gw[0:1, :] + gw[1:2, :]
    shift = gw[2:3, :] + gw[3:4, :]
    for b in range(recs):

        def step2(i, _, b=b):
            r0 = pl.multiple_of(i * 48, 16)
            g = gp[b, pl.ds(r0, 48), :].astype(F32)
            rs[b, pl.ds(r0, 48), 0:1] = jnp.sum(g * gsum, axis=1, keepdims=True)
            rs[b, pl.ds(r0, 48), 1:2] = jnp.sum(g * (proj[b, pl.ds(r0, 48), :] - shift), axis=1, keepdims=True)
            return 0

        lax.fori_loop(0, half // 48, step2, 0)


def row_sums(gp, proj, gw):
    recs, half, n2 = gp.shape
    return pl.pallas_call(
        rows_body,
        in_specs=[VMEM] * 3,
        out_specs=VMEM,
        out_shape=sds((recs, half, 2), F32),
        compiler_params=LIMIT,
        cost_estimate=cost(recs * half * n2 * 8, recs * half * n2 * 6),
        name="row_sums",
    )(gp, proj, gw)


def through_body(gain, bias, w, out):
    def split(v):
        top = v.astype(BF16).astype(F32)
        return top, v - top

    g1, g2 = split(gain[...])
    b1, b2 = split(bias[...])
    row = lax.broadcasted_iota(jnp.int32, (16, gain.shape[1]), 0)
    v = jnp.where(row == 0, g1, jnp.where(row == 1, g2, jnp.where(row == 2, b1, jnp.where(row == 3, b2, 0.0))))
    out[...] = jnp.dot(v.astype(BF16), w[...], preferred_element_type=F32)


def through(gain, bias, w):
    return pl.pallas_call(
        through_body,
        in_specs=[VMEM] * 3,
        out_specs=VMEM,
        out_shape=sds((16, w.shape[1]), F32),
        compiler_params=LIMIT,
        cost_estimate=cost(32 * w.shape[0] * w.shape[1], 2 * w.shape[0] * w.shape[1]),
        name="through",
    )(gain[None], bias[None], w)


def turn_body(w, out, cat):
    n = w.shape[1]
    for d in range(4):
        cat[0:n, :] = w[d]
        cat[n:, :] = w[d + 4]
        out[d] = cat[...].T


def turned(w):
    n, depth = w.shape[0] // 8, w.shape[1]
    return pl.pallas_call(
        turn_body,
        in_specs=[VMEM],
        out_specs=VMEM,
        out_shape=sds((4, depth, 2 * n), BF16),
        scratch_shapes=[pltpu.VMEM((2 * n, depth), BF16)],
        compiler_params=LIMIT,
        cost_estimate=cost(32 * n * depth, 32 * n * depth),
        name="turned",
    )(w.reshape(8, n, depth))


def blocks_body(s, lhs, w, *refs, jobs, adds):
    plus, outs = refs[:adds], refs[adds:]
    half = lhs.shape[1]
    for rec, r, to, at in jobs:
        v = jnp.dot(lhs[rec], w[lax.rem(s[S_X] + r, 4)], preferred_element_type=F32)
        if adds:
            v = v + plus[to][0:half, :].astype(F32)
        outs[to][at * half : (at + 1) * half, :] = v.astype(BF16)


def blocks(s, lhs, w4, jobs, plus=()):
    recs, half, depth = lhs.shape
    n = w4.shape[2]
    each = len(jobs) // 2
    return pl.pallas_call(
        functools.partial(blocks_body, jobs=jobs, adds=len(plus)),
        in_specs=[SMEM] + [VMEM] * (2 + len(plus)),
        out_specs=[VMEM] * 2,
        out_shape=[sds((each * half, n), BF16)] * 2,
        compiler_params=LIMIT,
        cost_estimate=cost(2 * half * depth * n * len(jobs), 4 * half * depth + 8 * n * depth),
        name="blocks",
    )(s, lhs, w4, *plus)


def finish_body(s, lhs, w, up, down, last_a, last_b, keep, give):
    half = lhs.shape[1]
    n = w.shape[2] // 2
    first = s[S_YL] == 0
    for rec, (one, two) in enumerate(((last_a, down), (last_b, up))):
        v = jnp.dot(lhs[rec], w[s[S_X]], preferred_element_type=F32)
        v = v + one[...].astype(F32) + two[half:, :].astype(F32)
        low, high = v[:, :n], v[:, n:]
        keep[:, rec * n : (rec + 1) * n] = jnp.where(first, low, high)
        give[:, rec * n : (rec + 1) * n] = jnp.where(first, high, low).astype(BF16)


def finish(s, lhs, w4, parts, estimate):
    recs, half, depth = lhs.shape
    n = w4.shape[2] // 2
    return pl.pallas_call(
        finish_body,
        in_specs=[SMEM] + [VMEM] * 6,
        out_specs=[VMEM] * 2,
        out_shape=[sds((half, recs * n), F32), sds((half, recs * n), BF16)],
        compiler_params=LIMIT,
        cost_estimate=estimate,
        name="finish",
    )(s, lhs, w4, *parts)


def hop(v, axis, by):
    n = lax.axis_size(axis)
    return lax.ppermute(v, axis, [(i, (i + by) % n) for i in range(n)])


def sum_start(s, lhs, w8):
    sent = blocks(s, lhs, w8, ((0, 2, 0, 0), (1, 2, 1, 0), (1, 1, 0, 1), (0, 3, 1, 1)))
    return (hop(sent[0], "x", 1), hop(sent[1], "x", -1)), sent[0]


def sum_middle(s, lhs, w8, got):
    sent = blocks(s, lhs, w8, ((0, 1, 0, 0), (1, 3, 1, 0)), got)
    return (hop(sent[0], "x", 1), hop(sent[1], "x", -1)), sent[0]


def sum_end(s, lhs, w8, got, last, estimate):
    keep, give = finish(s, lhs, w8, (*got, *last), estimate)
    return keep, hop(give, "yl", 1)


def after(values, *first):
    return lax.optimization_barrier((*values, *first))[: len(values)]


def pick(block, odd):
    n = block.shape[1] // 2
    return jnp.where(odd == 1, block[:, n:].astype(F32), block[:, :n].astype(F32))


def halves(s, keep, got):
    n = keep.shape[1] // 2
    early = pl.program_id(0) == 0
    mine = jnp.where(early, keep[:, :n], keep[:, n:])
    theirs = jnp.where(early, got[:, :n].astype(F32), got[:, n:].astype(F32))
    first = s[S_YL] == 0
    return jnp.where(first, mine, theirs), jnp.where(first, theirs, mine)


def out_body(s, keep, got, fr, out):
    half = keep.shape[0]
    for h, v in enumerate(halves(s, keep, got)):
        rows = slice(h * half, h * half + half)
        out[0, :, rows] = (pick(fr[0, rows, :], s[S_ODD]) + v).T.astype(BF16)


def frames_body(s, keep, got, fr, go, stat, rs, gain, out):
    half = keep.shape[0]
    width = 8 * out.shape[1]
    for h, v in enumerate(halves(s, keep, got)):
        rows = slice(h * half, h * half + half)
        g = v * gain[...]
        mean, rstd = stat[0, rows, 0:1], stat[0, rows, 1:2]
        first, second = rs[h, 0, :, 0:1], rs[h, 0, :, 1:2]
        hat = (pick(fr[0, rows, :], s[S_ODD]) - mean) * rstd
        v = rstd * (g - first / width - hat * (second / width)) + pick(go[0, rows, :], s[S_ODD])
        out[0, :, rows] = v.T.astype(BF16)


def last_call(body, s, keep, got, wide, extra, extra_specs, name):
    recs, length, _ = wide[0].shape
    half, n = length // 2, keep.shape[1] // 2
    cols = pl.BlockSpec((1, 2 * half, 2 * n), lambda b, s: (b, 0, s[S_PAIR]))
    return pl.pallas_call(
        body,
        grid_spec=pltpu.PrefetchScalarGridSpec(
            num_scalar_prefetch=1,
            grid=(recs,),
            in_specs=[
                pl.BlockSpec((half, recs * n), lambda b, s: (0, 0)),
                pl.BlockSpec((half, recs * n), lambda b, s: (0, 0)),
            ]
            + [cols] * len(wide)
            + extra_specs,
            out_specs=pl.BlockSpec((1, n, 2 * half), lambda b, s: (b, 0, 0)),
        ),
        out_shape=sds((recs, n, 2 * half), BF16),
        compiler_params=LIMIT,
        cost_estimate=cost(recs * half * n * 20, recs * half * n * 20),
        name=name,
    )(s, keep, got, *wide, *extra).transpose(0, 2, 1)


def spread(v, axes):
    n = lax.axis_size(axes)
    return lax.all_to_all(jnp.broadcast_to(v[None], (n, *v.shape)), axes, 0, 0, tiled=True)


def on_device(frames, ln_gain, ln_bias, w_in, w_depth, bn_gain, bn_bias, w_out, lengths, grad_out):
    recs, length, width = frames.shape
    shard, _, own = w_in.shape
    half = length // 2
    chans = 2 * own
    yh, z, c, yl, x = (lax.axis_index(a) for a in ("yh", "z", "c", "yl", "x"))
    ctx = (yh * 4 + z) * 2 + c
    chan = yl * 4 + x
    time = ctx * 2 + yl
    s = jnp.stack([yl, x, chan // 2, chan % 2, time * half, lengths[0], lengths[1], z, c, yh]).astype(jnp.int32)

    w3 = jnp.concatenate([w_in.reshape(shard, 2 * own), w_out], axis=1)
    w_yl = hop(w3, "yl", 1)
    w_yh = hop(w3, "yh", 1)
    w_xx = lax.ppermute(w3, ("yh", "yl"), [(i, 3 - i) for i in range(4)])

    def paired(a, b, g0, g1):
        lo, hi = jnp.where(yl == 0, a, b), jnp.where(yl == 0, b, a)
        cols = []
        for g in range(g0, g1):
            cols += [lo[:, g * own : (g + 1) * own], hi[:, g * own : (g + 1) * own]]
        return jnp.concatenate(cols, axis=1)

    def rows_two(g0, g1):
        same, other = paired(w3, w_yl, g0, g1), paired(w_yh, w_xx, g0, g1)
        return jnp.where(yh == 0, jnp.stack([same, other]), jnp.stack([other, same]))

    def gathered(v, first):
        pieces = []
        for r in range(4):
            p = v if r == 0 else hop(v, "z", -r)
            if first is not None:
                (p,) = after([p], first)
            pieces += [p, hop(p, "c", 1)]
        return pieces

    prm1 = jnp.concatenate([w_depth, bn_gain[None], bn_bias[None], jnp.zeros((7, own), F32)], axis=0)
    prm2 = hop(prm1, "yl", 1)
    prm = jnp.where(yl == 0, jnp.concatenate([prm1, prm2], axis=1), jnp.concatenate([prm2, prm1], axis=1))
    (in_two,) = after([rows_two(0, 2)], prm2)
    normed, stat = layer_norm(s, *after([frames, ln_gain, ln_bias], in_two))
    in_pieces = gathered(in_two, normed)
    out_pieces = gathered(*after([rows_two(2, 3)], *in_pieces), None)
    proj, glu, w_in_all = project(s, normed, in_pieces, half)
    glu = glu.reshape(recs, half, chans)
    proj = proj.reshape(recs, half, 2 * chans)
    devices = lax.axis_size(TIME)
    up = [(i, i + 1) for i in range(devices - 1)]
    down = [(i + 1, i) for i in range(devices - 1)]
    g_lo = lax.ppermute(glu[:, half - EDGE :], TIME, up)
    g_hi = lax.ppermute(glu[:, :EDGE], TIME, down)
    gact, w_out_all = grad_act(s, grad_out, out_pieces)
    (glu_c,) = after([glu], gact)
    depth, bn_own = conv(s, glu_c, g_lo, g_hi, prm)
    bn_all = spread(bn_own, TIME).reshape(devices, 2 * chans)
    w_out_4 = turned(*after([w_out_all], bn_own))
    w_in_4 = turned(*after([w_in_all], bn_own))
    g_w = through(*after([ln_gain, ln_bias, w_in_all], bn_own))
    (gact,) = after([gact], w_out_4, w_in_4, g_w)
    act, gbo, sums_own, bn = activate(s, depth, gact, bn_all, prm)
    sums = spread(sums_own, TIME).reshape(devices, 2 * chans)
    e_lo = lax.ppermute(jnp.stack([depth[:, half - EDGE :], gbo[:, half - EDGE :]]), TIME, up)
    e_hi = lax.ppermute(jnp.stack([depth[:, :EDGE], gbo[:, :EDGE]]), TIME, down)

    out_first, sent = sum_start(s, act, w_out_4)
    depth, gbo = after([depth, gbo], sent)
    gd, gp = backward(s, depth, gbo, e_lo, e_hi, sums, bn, prm, proj)
    gn_first, sent = sum_start(s, gp, w_in_4)
    (act_m,) = after([act], sent)
    out_last, sent = sum_middle(s, act_m, w_out_4, out_first)
    (gp_r,) = after([gp], sent)
    rs = row_sums(gp_r, proj, g_w)
    (gp_w,) = after([gp], rs)
    mine, theirs, tu = weight_grads(
        s,
        normed,
        gp_w.reshape(recs * half, 2 * chans),
        grad_out,
        act.reshape(recs * half, chans),
        w_in_all,
    )
    (gp_m,) = after([gp], mine)
    gn_last, sent = sum_middle(s, gp_m, w_in_4, gn_first)
    mine, theirs = after([mine, theirs], sent)
    parts = core_sum(s, mine, hop(theirs, "c", 1))
    (gp_e,) = after([gp], parts[0])
    gn_keep, gn_got = sum_end(s, gp_e, w_in_4, gn_first, gn_last, cost(0, 0))
    gd, glu = after([gd, glu], gn_keep)
    gwd = taps_grad(gd, glu, g_lo, g_hi)
    (act_e,) = after([act], gwd)
    out_keep, out_got = sum_end(s, act_e, w_out_4, out_first, out_last, cost(0, 0))

    tu = tu.T.reshape(2, 2, 4, own).transpose(1, 2, 0, 3)
    mine_x = (jnp.arange(4) == x).astype(F32)[None, :, None, None]
    taps4 = gwd[:TAPS].reshape(TAPS, 2, own).transpose(1, 0, 2)[:, None] * mine_x
    rs_rows = recs * 2 * half // own
    rs8 = jnp.broadcast_to(rs.transpose(2, 0, 1).reshape(1, 1, rs_rows, own), (2, 4, rs_rows, own))
    small = jnp.concatenate([taps4, tu, rs8], axis=2).reshape(8, TAPS + 2 + rs_rows, own)
    small = lax.all_to_all(small, CHAN, 0, 0, tiled=True)
    rs_all = jnp.sum(small[:, TAPS + 2 :].reshape(2, 4, 2, recs, half), axis=1).transpose(0, 2, 3, 1)
    small = jnp.sum(small[:, : TAPS + 2], axis=0)
    block_out = last_call(out_body, s, out_keep, out_got, [frames], [], [], "block_out")
    small = jnp.sum(spread(small, CTX), axis=0)

    own_gain = lax.dynamic_slice_in_dim(ln_gain, chan * own, own, 0)
    own_bias = lax.dynamic_slice_in_dim(ln_bias, chan * own, own, 0)
    grad_frames = last_call(
        frames_body,
        s,
        gn_keep,
        gn_got,
        [frames, grad_out],
        [stat, rs_all, own_gain[None]],
        [
            pl.BlockSpec((1, length, 2), lambda b, s: (b, 0, 0)),
            pl.BlockSpec((2, 1, half, 2), lambda b, s: (0, b, 0, 0)),
            pl.BlockSpec((1, own), lambda b, s: (0, 0)),
        ],
        "grad_frames",
    )

    parts = [parts[0]] + [hop(parts[r], "z", r) for r in range(1, 4)]
    g_fin, to_yl, to_yh, to_xx = ring_sum(s, parts)
    g_fin = g_fin + hop(to_yl, "yl", 1).astype(F32) + hop(to_yh, "yh", 1).astype(F32)
    g_fin = g_fin + lax.ppermute(to_xx, ("yh", "yl"), [(i, 3 - i) for i in range(4)]).astype(F32)
    grad_w_in = g_fin[:, : 2 * own].reshape(shard, 2, own)
    grad_w_out = g_fin[:, 2 * own :]

    grad_w_depth = small[:TAPS]
    t, u = small[TAPS], small[TAPS + 1]
    grad_ln = jnp.stack([(t - own_bias * u) / own_gain, u])
    grad_bn = lax.dynamic_index_in_dim(jnp.sum(sums, axis=0).reshape(2, 2, own), yl, 1, False)
    return (block_out, grad_frames, grad_w_in, grad_w_out, grad_w_depth, grad_bn, grad_ln)


def solution(mesh):
    split = Mesh(mesh.devices.reshape(2, 4, 2, 2, 4), ("yh", "z", "c", "yl", "x"))
    placed = (
        P(None, CTX, None),
        P(),
        P(),
        P(CTX, None, CHAN),
        P(None, CHAN),
        P(CHAN),
        P(CHAN),
        P(CTX, CHAN),
        P(),
        P(None, CTX, None),
    )
    return jax.shard_map(
        on_device,
        mesh=split,
        in_specs=placed,
        out_specs=(
            P(None, CTX, CHAN),
            P(None, CTX, CHAN),
            P(CTX, None, CHAN),
            P(CTX, CHAN),
            P(None, CHAN),
            P(None, CHAN),
            P(None, CHAN),
        ),
        check_vma=False,
    )
```

```python
import functools

import jax
import jax.numpy as jnp
from jax import lax
from jax.experimental import pallas as pl
from jax.experimental.pallas import tpu as pltpu
from jax.sharding import Mesh
from jax.sharding import PartitionSpec as P

F32 = jnp.float32
BF16 = jnp.bfloat16
CTX = ("yh", "z", "c")
CHAN = ("yl", "x")
TIME = ("yh", "z", "c", "yl")
EPS = 1e-05
TAPS = 31
EDGE = 16
LIMIT = pltpu.CompilerParams(vmem_limit_bytes=50 * 1024 * 1024)

S_YL, S_X, S_PAIR, S_ODD, S_POS, S_LEN, S_Z, S_C, S_YH = 0, 1, 2, 3, 4, 5, 7, 8, 9

SMEM = pl.BlockSpec(memory_space=pltpu.SMEM)
VMEM = pl.BlockSpec(memory_space=pltpu.VMEM)
ANY = pl.BlockSpec(memory_space=pl.ANY)


def cost(flops, nbytes):
    return pl.CostEstimate(flops=flops // 50, bytes_accessed=nbytes // 50, transcendentals=0)


LONG = pl.CostEstimate(flops=0, bytes_accessed=100 * 1024 * 1024, transcendentals=0)


def sds(shape, dtype):
    return jax.ShapeDtypeStruct(shape, dtype)


def nt(a, b):
    return lax.dot_general(a, b, (((1,), (1,)), ((), ())), preferred_element_type=F32)


def ln_body(s, fr, gain, bias, normed, stat):
    v = fr[0].astype(F32)
    mean = jnp.mean(v, axis=-1, keepdims=True)
    cen = v - mean
    rstd = lax.rsqrt(jnp.mean(cen * cen, axis=-1, keepdims=True) + EPS)
    stat[0, :, 0:1] = mean
    stat[0, :, 1:2] = rstd

    @pl.when(pl.program_id(0) == 0)
    def _():
        normed[...] = (cen * rstd * gain[...] + bias[...]).astype(BF16)


def layer_norm(s, frames, gain, bias):
    recs, length, width = frames.shape
    blk = length // 4

    def rows(h, b, i, s):
        return (b, jnp.where(h == 0, s[S_YL], 1 - s[S_YL]) * 2 + i, 0)

    return pl.pallas_call(
        ln_body,
        grid_spec=pltpu.PrefetchScalarGridSpec(
            num_scalar_prefetch=1,
            grid=(2, recs, 2),
            in_specs=[
                pl.BlockSpec((1, blk, width), rows),
                pl.BlockSpec((1, width), lambda h, b, i, s: (0, 0)),
                pl.BlockSpec((1, width), lambda h, b, i, s: (0, 0)),
            ],
            out_specs=[
                pl.BlockSpec((blk, width), lambda h, b, i, s: (jnp.where(h == 0, b * 2 + i, 2 * recs - 1), 0)),
                pl.BlockSpec((1, blk, 2), rows),
            ],
        ),
        out_shape=[sds((recs * length // 2, width), BF16), sds((recs, length, 2), F32)],
        compiler_params=LIMIT,
        cost_estimate=cost(recs * length * width * 10, 4 * recs * length * width),
        name="layer_norm",
    )(s, frames, gain[None], bias[None])


def place(s, pieces, out):
    z, c = s[S_Z], s[S_C]
    n = pieces[0].shape[1]
    for r in range(4):
        for k in range(2):
            for h in range(2):
                row = (h * 4 + lax.rem(z + r, 4)) * 2 + (c if k == 0 else 1 - c)
                out[pl.ds(pl.multiple_of(row * n, n), n), :] = pieces[2 * r + k][h]


def proj_body(s, normed, *refs, blk, half):
    pieces, (proj, glu, w) = refs[:8], refs[8:]
    i = pl.program_id(0)

    @pl.when(i == 0)
    def _():
        place(s, pieces, w)

    p = jnp.dot(normed[...], w[...], preferred_element_type=F32)
    proj[...] = p
    n = p.shape[1] // 2
    b = i // (half // blk)
    t = s[S_POS] + (i % (half // blk)) * blk + lax.broadcasted_iota(jnp.int32, (blk, 1), 0)
    valid = (t < s[S_LEN + b]).astype(F32)
    glu[...] = (p[:, :n] * jax.nn.sigmoid(p[:, n:]) * valid).astype(BF16)


def project(s, normed, pieces, half):
    rows, width = normed.shape
    _, shard, n2 = pieces[0].shape
    blk = half
    return pl.pallas_call(
        functools.partial(proj_body, blk=blk, half=half),
        grid_spec=pltpu.PrefetchScalarGridSpec(
            num_scalar_prefetch=1,
            grid=(rows // blk,),
            in_specs=[pl.BlockSpec((blk, width), lambda i, s: (i, 0))] + [VMEM] * 8,
            out_specs=[
                pl.BlockSpec((blk, n2), lambda i, s: (i, 0)),
                pl.BlockSpec((blk, n2 // 2), lambda i, s: (i, 0)),
                pl.BlockSpec((16 * shard, n2), lambda i, s: (0, 0)),
            ],
        ),
        out_shape=[sds((rows, n2), F32), sds((rows, n2 // 2), BF16), sds((16 * shard, n2), BF16)],
        compiler_params=LIMIT,
        cost_estimate=cost(2 * rows * width * n2, 2 * rows * width + 5 * rows * n2),
        name="project",
    )(s, normed, *pieces)


def gact_body(s, go, *refs):
    pieces, (out, w) = refs[:8], refs[8:]

    @pl.when((pl.program_id(0) == 0) & (pl.program_id(1) == 0))
    def _():
        place(s, pieces, w)

    out[0] = jnp.dot(go[0], w[...], preferred_element_type=F32)


def grad_act(s, grad_out, pieces):
    recs, length, width = grad_out.shape
    _, shard, n = pieces[0].shape
    blk = length // 2
    return pl.pallas_call(
        gact_body,
        grid_spec=pltpu.PrefetchScalarGridSpec(
            num_scalar_prefetch=1,
            grid=(recs, 1),
            in_specs=[pl.BlockSpec((1, blk, width), lambda b, i, s: (b, s[S_YL] + i, 0))] + [VMEM] * 8,
            out_specs=[
                pl.BlockSpec((1, blk, n), lambda b, i, s: (b, i, 0)),
                pl.BlockSpec((16 * shard, n), lambda b, i, s: (0, 0)),
            ],
        ),
        out_shape=[sds((recs, length // 2, n), F32), sds((16 * shard, n), BF16)],
        compiler_params=LIMIT,
        cost_estimate=cost(recs * length * width * n, recs * length * (width + 2 * n)),
        name="grad_act",
    )(s, grad_out, *pieces)


def tn(a, b):
    return lax.dot_general(a, b, (((0,), (0,)), ((), ())), preferred_element_type=F32)


def wgrad_body(s, normed, gp, go, act, w, mine, theirs, tu, colsum):
    shard = mine.shape[1]
    n2 = gp.shape[1]

    @pl.when(pl.program_id(0) == 0)
    def _():
        colsum[...] = jnp.sum(gp[...].astype(F32), axis=0, keepdims=True)

    g_in = tn(normed[...], gp[...])
    wide = w[...].astype(F32)
    tu[:, 0:1] = jnp.sum(wide * g_in, axis=1, keepdims=True)
    tu[:, 1:2] = jnp.sum(wide * colsum[...], axis=1, keepdims=True)
    g_out = tn(go[...].reshape(-1, go.shape[2]), act[...])
    first = s[S_C] == 0
    for i in range(2):
        r0 = 2 * i * shard
        for g, cols in ((g_in, slice(0, n2)), (g_out, slice(n2, n2 + g_out.shape[1]))):
            top, low = g[r0 : r0 + shard], g[r0 + shard : r0 + 2 * shard]
            mine[i, :, cols] = jnp.where(first, top, low).astype(BF16)
            theirs[i, :, cols] = jnp.where(first, low, top).astype(BF16)


def weight_grads(s, normed, gp, grad_out, act, w):
    rows, width = normed.shape
    n2, n = gp.shape[1], act.shape[1]
    recs, length, _ = grad_out.shape
    blk = width // 4
    shard = width // 16
    part = pl.BlockSpec((2, shard, n2 + n), lambda k, s: (k, 0, 0))
    return pl.pallas_call(
        wgrad_body,
        grid_spec=pltpu.PrefetchScalarGridSpec(
            num_scalar_prefetch=1,
            grid=(4,),
            in_specs=[
                pl.BlockSpec((rows, blk), lambda k, s: (0, k)),
                pl.BlockSpec((rows, n2), lambda k, s: (0, 0)),
                pl.BlockSpec((recs, length // 2, blk), lambda k, s: (0, s[S_YL], k)),
                pl.BlockSpec((rows, n), lambda k, s: (0, 0)),
                pl.BlockSpec((blk, n2), lambda k, s: (k, 0)),
            ],
            out_specs=[part, part, pl.BlockSpec((blk, 2), lambda k, s: (k, 0))],
            scratch_shapes=[pltpu.VMEM((1, n2), F32)],
        ),
        out_shape=[sds((8, shard, n2 + n), BF16)] * 2 + [sds((width, 2), F32)],
        compiler_params=LIMIT,
        cost_estimate=cost(2 * rows * width * (n2 + n), 4 * rows * width),
        name="weight_grads",
    )(s, normed, gp, grad_out, act, w)


def core_body(s, mine, got, *outs):
    for r, out in enumerate(outs):
        q = lax.rem(s[S_Z] + r, 4)
        for h in range(2):
            out[h] = (mine[h * 4 + q].astype(F32) + got[h * 4 + q].astype(F32)).astype(BF16)


def core_sum(s, mine, got):
    _, shard, n = mine.shape
    return pl.pallas_call(
        core_body,
        in_specs=[SMEM, VMEM, VMEM],
        out_specs=[VMEM] * 4,
        out_shape=[sds((2, shard, n), BF16)] * 4,
        compiler_params=LIMIT,
        cost_estimate=cost(16 * shard * n, 48 * shard * n),
        name="core_sum",
    )(s, mine, got)


def ring_body(s, p0, p1, p2, p3, own, to_yl, to_yh, to_xx):
    n = own.shape[1] // 3

    def total(h):
        return p0[h].astype(F32) + p1[h].astype(F32) + p2[h].astype(F32) + p3[h].astype(F32)

    first = s[S_YL] == 0
    for v, here, there in ((total(s[S_YH]), own, to_yl), (total(1 - s[S_YH]), to_yh, to_xx)):
        for g in range(3):
            low, high = v[:, 2 * g * n : (2 * g + 1) * n], v[:, (2 * g + 1) * n : (2 * g + 2) * n]
            cols = slice(g * n, g * n + n)
            here[:, cols] = jnp.where(first, low, high).astype(here.dtype)
            there[:, cols] = jnp.where(first, high, low).astype(there.dtype)


def ring_sum(s, parts):
    _, shard, n = parts[0].shape
    return pl.pallas_call(
        ring_body,
        in_specs=[SMEM] + [VMEM] * 4,
        out_specs=[VMEM] * 4,
        out_shape=[sds((shard, n // 2), F32)] + [sds((shard, n // 2), BF16)] * 3,
        compiler_params=LIMIT,
        cost_estimate=cost(8 * shard * n, 24 * shard * n),
        name="ring_sum",
    )(s, *parts)


def fill(pad, mid, lo, hi):
    recs, half = mid.shape[0], mid.shape[1]
    for b in range(recs):
        for j in range(mid.shape[2] // 128):
            lanes = slice(128 * j, 128 * j + 128)
            pad[b, j, 0:EDGE, :] = lo[b, :, lanes].astype(F32)
            pad[b, j, EDGE : EDGE + half, :] = mid[b, :, lanes].astype(F32)
            pad[b, j, EDGE + half :, :] = hi[b, :, lanes].astype(F32)


def tile_mask(start, rows, length):
    t = start + lax.broadcasted_iota(jnp.int32, (rows, 128), 0)
    return ((t >= 0) & (t < length)).astype(F32)


def local_count(s, half):
    n = jnp.int32(0)
    for b in range(2):
        n = n + jnp.clip(s[S_LEN + b] - s[S_POS], 0, half)
    return jnp.maximum(n, 1).astype(F32)


def fold(v):
    return jnp.sum(v.reshape(-1, 8, v.shape[1]), axis=0)


TILE = 96


def conv_body(s, glu, lo, hi, w, depth, stat, pad):
    recs, half, chans = glu.shape
    fill(pad, glu, lo, hi)
    count = local_count(s, half)
    for j in range(chans // 128):
        lanes = slice(128 * j, 128 * j + 128)
        total = jnp.zeros((8, 128), F32)
        for b in range(recs):

            def step(i, total, b=b):
                r0 = pl.multiple_of(i * TILE, 8)
                acc = jnp.zeros((TILE, 128), F32)
                for o in range(TAPS):
                    acc = acc + pad[b, j, pl.ds(r0 + o + 1, TILE), :] * w[o : o + 1, lanes]
                depth[b, pl.ds(r0, TILE), lanes] = acc
                return total + fold(acc * tile_mask(s[S_POS] + r0, TILE, s[S_LEN + b]))

            total = lax.fori_loop(0, half // TILE, step, total)
        mean = jnp.sum(total, axis=0, keepdims=True) / count
        spread = jnp.zeros((8, 128), F32)
        for b in range(recs):

            def step2(i, spread, b=b):
                r0 = pl.multiple_of(i * TILE, 8)
                d = (depth[b, pl.ds(r0, TILE), lanes] - mean) * tile_mask(s[S_POS] + r0, TILE, s[S_LEN + b])
                return spread + fold(d * d)

            spread = lax.fori_loop(0, half // TILE, step2, spread)
        stat[0:1, lanes] = mean
        stat[0:1, slice(chans + 128 * j, chans + 128 * j + 128)] = jnp.sum(spread, axis=0, keepdims=True)


def conv(s, glu, lo, hi, w):
    recs, half, chans = glu.shape
    return pl.pallas_call(
        conv_body,
        in_specs=[SMEM, VMEM, VMEM, VMEM, VMEM],
        out_specs=[VMEM, VMEM],
        out_shape=[sds((recs, half, chans), F32), sds((1, 2 * chans), F32)],
        scratch_shapes=[pltpu.VMEM((recs, chans // 128, half + 2 * EDGE, 128), F32)],
        compiler_params=LIMIT,
        cost_estimate=cost(recs * half * chans * 62 * 50, recs * half * chans * 6),
        name="conv",
    )(s, glu, lo, hi, w)


def bn_stats(s, got, half, chans):
    dev = got.shape[0]
    start = half * lax.broadcasted_iota(jnp.int32, (dev, 1), 0)
    n = jnp.zeros((dev, 1), jnp.int32)
    for b in range(2):
        n = n + jnp.clip(s[S_LEN + b] - start, 0, half)
    n = n.astype(F32)
    count = (s[S_LEN].astype(F32)) + (s[S_LEN + 1].astype(F32))
    means, spread = got[:, :chans], got[:, chans:]
    mean = jnp.sum(n * means, axis=0, keepdims=True) / count
    var = jnp.sum(spread + n * (means - mean) ** 2, axis=0, keepdims=True) / count
    return mean, lax.rsqrt(var + EPS), count


def act_body(s, depth, gact, got, prm, act, gbo, sums, bn, *, half):
    b = pl.program_id(0)
    i = pl.program_id(1)
    rows, chans = depth.shape[1], depth.shape[2]

    @pl.when((b == 0) & (i == 0))
    def _():
        mean, rstd, _ = bn_stats(s, got, half, chans)
        bn[0:1, :] = mean
        bn[1:2, :] = rstd
        sums[...] = jnp.zeros_like(sums)

    for j in range(chans // 128):
        lanes = slice(128 * j, 128 * j + 128)
        high = slice(chans + 128 * j, chans + 128 * j + 128)
        mean, rstd = bn[0:1, lanes], bn[1:2, lanes]
        gain, bias = prm[31:32, lanes], prm[32:33, lanes]
        one = jnp.zeros((8, 128), F32)
        two = jnp.zeros((8, 128), F32)
        for k in range(rows // TILE):
            r = slice(k * TILE, k * TILE + TILE)
            hat = (depth[0, r, lanes] - mean) * rstd
            out = hat * gain + bias
            g = jax.nn.sigmoid(out)
            m = tile_mask(s[S_POS] + i * rows + k * TILE, TILE, s[S_LEN + b])
            act[0, r, lanes] = (out * g * m).astype(BF16)
            gb = gact[0, r, lanes] * m * (g * (1.0 + out * (1.0 - g)))
            gbo[0, r, lanes] = gb
            one = one + fold(gb * hat)
            two = two + fold(gb)
        sums[0:1, lanes] += jnp.sum(one, axis=0, keepdims=True)
        sums[0:1, high] += jnp.sum(two, axis=0, keepdims=True)


def activate(s, depth, gact, got, prm):
    recs, half, chans = depth.shape
    blk = half // 2
    block = pl.BlockSpec((1, blk, chans), lambda b, i, s: (b, i, 0))
    whole = lambda a: pl.BlockSpec(a.shape, lambda b, i, s: (0, 0))
    return pl.pallas_call(
        functools.partial(act_body, half=half),
        grid_spec=pltpu.PrefetchScalarGridSpec(
            num_scalar_prefetch=1,
            grid=(recs, 2),
            in_specs=[block, block, whole(got), whole(prm)],
            out_specs=[block, block, pl.BlockSpec((1, 2 * chans), lambda b, i, s: (0, 0)), pl.BlockSpec((8, chans), lambda b, i, s: (0, 0))],
        ),
        out_shape=[sds(depth.shape, BF16), sds(depth.shape, F32), sds((1, 2 * chans), F32), sds((8, chans), F32)],
        compiler_params=LIMIT,
        cost_estimate=cost(recs * half * chans * 200, recs * half * chans * 14),
        name="activate",
    )(s, depth, gact, got, prm)


def back_body(s, depth, gbo, lo, hi, sums, bn, prm, proj, gd_out, gp, pad):
    recs, half, chans = depth.shape
    total = jnp.sum(sums[...], axis=0, keepdims=True)
    count = (s[S_LEN].astype(F32)) + (s[S_LEN + 1].astype(F32))
    pos = s[S_POS]
    for j in range(chans // 128):
        lanes = slice(128 * j, 128 * j + 128)
        high = slice(chans + 128 * j, chans + 128 * j + 128)
        gsum, bsum = total[:, lanes], total[:, high]
        mean, rstd = bn[0:1, lanes], bn[1:2, lanes]
        scale = prm[31:32, lanes] * rstd

        def grad(dep, gb, start, length):
            m = tile_mask(start, dep.shape[0], length)
            hat = (dep - mean) * rstd
            return m * scale * (gb - (bsum + hat * gsum) / count)

        for b in range(recs):
            length = s[S_LEN + b]
            pad[b, j, 0:EDGE, :] = grad(lo[0, b, :, lanes], lo[1, b, :, lanes], pos - EDGE, length)
            pad[b, j, EDGE + half :, :] = grad(hi[0, b, :, lanes], hi[1, b, :, lanes], pos + half, length)

            def step(i, _, b=b, length=length):
                r0 = pl.multiple_of(i * TILE, 8)
                v = grad(depth[b, pl.ds(r0, TILE), lanes], gbo[b, pl.ds(r0, TILE), lanes], pos + r0, length)
                pad[b, j, pl.ds(pl.multiple_of(r0 + EDGE, 8), TILE), :] = v
                gd_out[b, pl.ds(r0, TILE), lanes] = v
                return 0

            lax.fori_loop(0, half // TILE, step, 0)

            def step2(i, _, b=b, length=length):
                r0 = pl.multiple_of(i * TILE, 16)
                acc = jnp.zeros((TILE, 128), F32)
                for o in range(TAPS):
                    acc = acc + pad[b, j, pl.ds(r0 + TAPS - o, TILE), :] * prm[o : o + 1, lanes]
                acc = acc * tile_mask(pos + r0, TILE, length)
                val = proj[b, pl.ds(r0, TILE), lanes]
                g = jax.nn.sigmoid(proj[b, pl.ds(r0, TILE), high])
                gp[b, pl.ds(r0, TILE), lanes] = (acc * g).astype(BF16)
                gp[b, pl.ds(r0, TILE), high] = (acc * val * g * (1.0 - g)).astype(BF16)
                return 0

            lax.fori_loop(0, half // TILE, step2, 0)


def backward(s, depth, gbo, lo, hi, sums, bn, prm, proj):
    recs, half, chans = depth.shape
    return pl.pallas_call(
        back_body,
        in_specs=[SMEM] + [VMEM] * 8,
        out_specs=[VMEM, VMEM],
        out_shape=[sds(depth.shape, F32), sds((recs, half, 2 * chans), BF16)],
        scratch_shapes=[pltpu.VMEM((recs, chans // 128, half + 2 * EDGE, 128), F32)],
        compiler_params=LIMIT,
        cost_estimate=LONG,
        name="backward",
    )(s, depth, gbo, lo, hi, sums, bn, prm, proj)


def taps_body(gd, glu, lo, hi, gwd, pad):
    recs, half, chans = glu.shape
    fill(pad, glu, lo, hi)
    gwd[...] = jnp.zeros_like(gwd)
    for j in range(chans // 128):
        lanes = slice(128 * j, 128 * j + 128)
        accs = tuple(jnp.zeros((8, 128), F32) for _ in range(TAPS))
        for b in range(recs):

            def step(i, accs, b=b):
                r0 = pl.multiple_of(i * 16, 16)
                new = list(accs)
                for k in range(2):
                    g = gd[b, pl.ds(r0 + 8 * k, 8), lanes]
                    for o in range(TAPS):
                        new[o] = new[o] + g * pad[b, j, pl.ds(r0 + 8 * k + o + 1, 8), :]
                return tuple(new)

            accs = lax.fori_loop(0, half // 16, step, accs)
        for o in range(TAPS):
            gwd[o : o + 1, lanes] = jnp.sum(accs[o], axis=0, keepdims=True)


def taps_grad(gd, glu, lo, hi):
    recs, half, chans = glu.shape
    return pl.pallas_call(
        taps_body,
        in_specs=[VMEM] * 4,
        out_specs=VMEM,
        out_shape=sds((32, chans), F32),
        scratch_shapes=[pltpu.VMEM((recs, chans // 128, half + 2 * EDGE, 128), F32)],
        compiler_params=LIMIT,
        cost_estimate=cost(recs * half * chans * 62 * 50, recs * half * chans * 20),
        name="taps_grad",
    )(gd, glu, lo, hi)


def rows_body(gp, proj, gw, rs):
    recs, half, n2 = gp.shape
    lane = lax.broadcasted_iota(jnp.int32, (n2, 128), 1)
    row = lax.broadcasted_iota(jnp.int32, (16, n2), 0)
    total = gw[0:1, :] + gw[1:2, :]
    top = total.astype(BF16).astype(F32)
    taps = jnp.where(row == 0, top, jnp.where(row == 1, total - top, 0.0)).astype(BF16)
    pick_second = (lane == 1).astype(BF16)
    shift = gw[2:3, :] + gw[3:4, :]
    for b in range(recs):
        g = gp[b]
        one = jnp.sum(nt(g, taps), axis=1, keepdims=True)
        p = g.astype(F32) * (proj[b] - shift)
        top = p.astype(BF16)
        low = (p - top.astype(F32)).astype(BF16)
        two = jnp.dot(top, pick_second, preferred_element_type=F32) + jnp.dot(low, pick_second, preferred_element_type=F32)
        first = lax.broadcasted_iota(jnp.int32, two.shape, 1) == 0
        rs[b] = jnp.where(first, one, two)[:, 0:2]


def row_sums(gp, proj, gw):
    recs, half, n2 = gp.shape
    return pl.pallas_call(
        rows_body,
        in_specs=[VMEM] * 3,
        out_specs=VMEM,
        out_shape=sds((recs, half, 2), F32),
        compiler_params=LIMIT,
        cost_estimate=cost(recs * half * n2 * 8, recs * half * n2 * 6),
        name="row_sums",
    )(gp, proj, gw)


def through_body(gain, bias, w, out):
    def split(v):
        top = v.astype(BF16).astype(F32)
        return top, v - top

    g1, g2 = split(gain[...])
    b1, b2 = split(bias[...])
    row = lax.broadcasted_iota(jnp.int32, (16, gain.shape[1]), 0)
    v = jnp.where(row == 0, g1, jnp.where(row == 1, g2, jnp.where(row == 2, b1, jnp.where(row == 3, b2, 0.0))))
    out[...] = jnp.dot(v.astype(BF16), w[...], preferred_element_type=F32)


def through(gain, bias, w):
    return pl.pallas_call(
        through_body,
        in_specs=[VMEM] * 3,
        out_specs=VMEM,
        out_shape=sds((16, w.shape[1]), F32),
        compiler_params=LIMIT,
        cost_estimate=cost(32 * w.shape[0] * w.shape[1], 2 * w.shape[0] * w.shape[1]),
        name="through",
    )(gain[None], bias[None], w)


def turn_body(w, out, cat):
    n = w.shape[1]
    for d in range(4):
        cat[0:n, :] = w[d]
        cat[n:, :] = w[d + 4]
        out[d] = cat[...].T


def turned(w):
    n, depth = w.shape[0] // 8, w.shape[1]
    return pl.pallas_call(
        turn_body,
        in_specs=[VMEM],
        out_specs=VMEM,
        out_shape=sds((4, depth, 2 * n), BF16),
        scratch_shapes=[pltpu.VMEM((2 * n, depth), BF16)],
        compiler_params=LIMIT,
        cost_estimate=cost(32 * n * depth, 32 * n * depth),
        name="turned",
    )(w.reshape(8, n, depth))


def blocks_body(s, lhs, w, *refs, jobs, adds):
    plus, outs = refs[:adds], refs[adds:]
    half = lhs.shape[1]
    for rec, r, to, at in jobs:
        v = jnp.dot(lhs[rec], w[lax.rem(s[S_X] + r, 4)], preferred_element_type=F32)
        if adds:
            v = v + plus[to][0:half, :].astype(F32)
        outs[to][at * half : (at + 1) * half, :] = v.astype(BF16)


def blocks(s, lhs, w4, jobs, plus=()):
    recs, half, depth = lhs.shape
    n = w4.shape[2]
    each = len(jobs) // 2
    return pl.pallas_call(
        functools.partial(blocks_body, jobs=jobs, adds=len(plus)),
        in_specs=[SMEM] + [VMEM] * (2 + len(plus)),
        out_specs=[VMEM] * 2,
        out_shape=[sds((each * half, n), BF16)] * 2,
        compiler_params=LIMIT,
        cost_estimate=cost(2 * half * depth * n * len(jobs), 4 * half * depth + 8 * n * depth),
        name="blocks",
    )(s, lhs, w4, *plus)


def finish_body(s, lhs, w, up, down, last_a, last_b, keep, give):
    half = lhs.shape[1]
    n = w.shape[2] // 2
    first = s[S_YL] == 0
    for rec, (one, two) in enumerate(((last_a, down), (last_b, up))):
        v = jnp.dot(lhs[rec], w[s[S_X]], preferred_element_type=F32)
        v = v + one[...].astype(F32) + two[half:, :].astype(F32)
        low, high = v[:, :n], v[:, n:]
        keep[:, rec * n : (rec + 1) * n] = jnp.where(first, low, high)
        give[:, rec * n : (rec + 1) * n] = jnp.where(first, high, low).astype(BF16)


def finish(s, lhs, w4, parts, estimate):
    recs, half, depth = lhs.shape
    n = w4.shape[2] // 2
    return pl.pallas_call(
        finish_body,
        in_specs=[SMEM] + [VMEM] * 6,
        out_specs=[VMEM] * 2,
        out_shape=[sds((half, recs * n), F32), sds((half, recs * n), BF16)],
        compiler_params=LIMIT,
        cost_estimate=estimate,
        name="finish",
    )(s, lhs, w4, *parts)


def weights_body(own, one, two, three, g_in, g_out):
    v = own[...] + one[...].astype(F32) + two[...].astype(F32) + three[...].astype(F32)
    n = g_out.shape[1]
    g_in[:, 0, :] = v[:, :n]
    g_in[:, 1, :] = v[:, n : 2 * n]
    g_out[...] = v[:, 2 * n :]


def weights_end(own, *got):
    shard, n3 = own.shape
    return pl.pallas_call(
        weights_body,
        in_specs=[VMEM] * 4,
        out_specs=[VMEM] * 2,
        out_shape=[sds((shard, 2, n3 // 3), F32), sds((shard, n3 // 3), F32)],
        compiler_params=LIMIT,
        cost_estimate=cost(4 * shard * n3, 14 * shard * n3),
        name="weights_end",
    )(own, *got)


def params_body(got, gain, bias, taps, ln):
    v = jnp.sum(got[...], axis=0)
    taps[...] = v[:TAPS]
    t, u = v[TAPS : TAPS + 1], v[TAPS + 1 : TAPS + 2]
    ln[0:1, :] = (t - bias[...] * u) / gain[...]
    ln[1:2, :] = u


def params_end(got, gain, bias):
    n = got.shape[2]
    return pl.pallas_call(
        params_body,
        in_specs=[VMEM] * 3,
        out_specs=[VMEM] * 2,
        out_shape=[sds((TAPS, n), F32), sds((2, n), F32)],
        compiler_params=LIMIT,
        cost_estimate=cost(got.size, 4 * got.size),
        name="params_end",
    )(got, gain[None], bias[None])


def hop(v, axis, by):
    n = lax.axis_size(axis)
    return lax.ppermute(v, axis, [(i, (i + by) % n) for i in range(n)])


def sum_start(s, lhs, w8):
    sent = blocks(s, lhs, w8, ((0, 2, 0, 0), (1, 2, 1, 0), (1, 1, 0, 1), (0, 3, 1, 1)))
    return (hop(sent[0], "x", 1), hop(sent[1], "x", -1)), sent[0]


def sum_middle(s, lhs, w8, got):
    sent = blocks(s, lhs, w8, ((0, 1, 0, 0), (1, 3, 1, 0)), got)
    return (hop(sent[0], "x", 1), hop(sent[1], "x", -1)), sent[0]


def sum_end(s, lhs, w8, got, last):
    keep, give = finish(s, lhs, w8, (*got, *last), cost(0, 0))
    return keep, hop(give, "yl", 1)


def after(values, *first):
    return lax.optimization_barrier((*values, *first))[: len(values)]


def pick(block, odd):
    n = block.shape[1] // 2
    return jnp.where(odd == 1, block[:, n:].astype(F32), block[:, :n].astype(F32))


def halves(s, keep, got):
    n = keep.shape[1] // 2
    early = pl.program_id(0) == 0
    mine = jnp.where(early, keep[:, :n], keep[:, n:])
    theirs = jnp.where(early, got[:, :n].astype(F32), got[:, n:].astype(F32))
    first = s[S_YL] == 0
    return jnp.where(first, mine, theirs), jnp.where(first, theirs, mine)


def out_body(s, keep, got, fr, out):
    half = keep.shape[0]
    for h, v in enumerate(halves(s, keep, got)):
        rows = slice(h * half, h * half + half)
        out[0, :, rows] = (pick(fr[0, rows, :], s[S_ODD]) + v).T.astype(BF16)


def frames_body(s, keep, got, fr, go, stat, rs, gain, out):
    half = keep.shape[0]
    width = 8 * out.shape[1]
    for h, v in enumerate(halves(s, keep, got)):
        rows = slice(h * half, h * half + half)
        g = v * gain[...]
        mean, rstd = stat[0, rows, 0:1], stat[0, rows, 1:2]
        first, second = rs[h, 0, :, 0:1], rs[h, 0, :, 1:2]
        hat = (pick(fr[0, rows, :], s[S_ODD]) - mean) * rstd
        v = rstd * (g - first / width - hat * (second / width)) + pick(go[0, rows, :], s[S_ODD])
        out[0, :, rows] = v.T.astype(BF16)


def last_call(body, s, keep, got, wide, extra, extra_specs, name):
    recs, length, _ = wide[0].shape
    half, n = length // 2, keep.shape[1] // 2
    cols = pl.BlockSpec((1, 2 * half, 2 * n), lambda b, s: (b, 0, s[S_PAIR]))
    return pl.pallas_call(
        body,
        grid_spec=pltpu.PrefetchScalarGridSpec(
            num_scalar_prefetch=1,
            grid=(recs,),
            in_specs=[
                pl.BlockSpec((half, recs * n), lambda b, s: (0, 0)),
                pl.BlockSpec((half, recs * n), lambda b, s: (0, 0)),
            ]
            + [cols] * len(wide)
            + extra_specs,
            out_specs=pl.BlockSpec((1, n, 2 * half), lambda b, s: (b, 0, 0)),
        ),
        out_shape=sds((recs, n, 2 * half), BF16),
        compiler_params=LIMIT,
        cost_estimate=cost(recs * half * n * 20, recs * half * n * 20),
        name=name,
    )(s, keep, got, *wide, *extra).transpose(0, 2, 1)


def spread(v, axes):
    n = lax.axis_size(axes)
    return lax.all_to_all(jnp.broadcast_to(v[None], (n, *v.shape)), axes, 0, 0, tiled=True)


def on_device(frames, ln_gain, ln_bias, w_in, w_depth, bn_gain, bn_bias, w_out, lengths, grad_out):
    recs, length, width = frames.shape
    shard, _, own = w_in.shape
    half = length // 2
    chans = 2 * own
    yh, z, c, yl, x = (lax.axis_index(a) for a in ("yh", "z", "c", "yl", "x"))
    ctx = (yh * 4 + z) * 2 + c
    chan = yl * 4 + x
    time = ctx * 2 + yl
    s = jnp.stack([yl, x, chan // 2, chan % 2, time * half, lengths[0], lengths[1], z, c, yh]).astype(jnp.int32)

    w3 = jnp.concatenate([w_in.reshape(shard, 2 * own), w_out], axis=1)
    w_yl = hop(w3, "yl", 1)
    w_yh = hop(w3, "yh", 1)
    w_xx = lax.ppermute(w3, ("yh", "yl"), [(i, 3 - i) for i in range(4)])

    def paired(a, b, g0, g1):
        lo, hi = jnp.where(yl == 0, a, b), jnp.where(yl == 0, b, a)
        cols = []
        for g in range(g0, g1):
            cols += [lo[:, g * own : (g + 1) * own], hi[:, g * own : (g + 1) * own]]
        return jnp.concatenate(cols, axis=1)

    def rows_two(g0, g1):
        same, other = paired(w3, w_yl, g0, g1), paired(w_yh, w_xx, g0, g1)
        return jnp.where(yh == 0, jnp.stack([same, other]), jnp.stack([other, same]))

    def gathered(v, first):
        pieces = []
        for r in range(4):
            p = v if r == 0 else hop(v, "z", -r)
            if first is not None:
                (p,) = after([p], first)
            pieces += [p, hop(p, "c", 1)]
        return pieces

    prm1 = jnp.concatenate([w_depth, bn_gain[None], bn_bias[None], jnp.zeros((7, own), F32)], axis=0)
    prm2 = hop(prm1, "yl", 1)
    prm = jnp.where(yl == 0, jnp.concatenate([prm1, prm2], axis=1), jnp.concatenate([prm2, prm1], axis=1))
    (in_two,) = after([rows_two(0, 2)], prm2)
    normed, stat = layer_norm(s, *after([frames, ln_gain, ln_bias], in_two))
    in_pieces = gathered(in_two, normed)
    out_pieces = gathered(*after([rows_two(2, 3)], *in_pieces), None)
    proj, glu, w_in_all = project(s, normed, in_pieces, half)
    glu = glu.reshape(recs, half, chans)
    proj = proj.reshape(recs, half, 2 * chans)
    own_gain = lax.dynamic_slice_in_dim(ln_gain, chan * own, own, 0)
    own_bias = lax.dynamic_slice_in_dim(ln_bias, chan * own, own, 0)
    devices = lax.axis_size(TIME)
    up = [(i, i + 1) for i in range(devices - 1)]
    down = [(i + 1, i) for i in range(devices - 1)]
    g_lo = lax.ppermute(glu[:, half - EDGE :], TIME, up)
    g_hi = lax.ppermute(glu[:, :EDGE], TIME, down)
    gact, w_out_all = grad_act(s, grad_out, out_pieces)
    (glu_c,) = after([glu], gact)
    depth, bn_own = conv(s, glu_c, g_lo, g_hi, prm)
    bn_all = spread(bn_own, TIME).reshape(devices, 2 * chans)
    w_out_4 = turned(*after([w_out_all], bn_own))
    w_in_4 = turned(*after([w_in_all], bn_own))
    g_w = through(*after([ln_gain, ln_bias, w_in_all], bn_own))
    (gact,) = after([gact], w_out_4, w_in_4, g_w)
    act, gbo, sums_own, bn = activate(s, depth, gact, bn_all, prm)
    sums = spread(sums_own, TIME).reshape(devices, 2 * chans)
    e_lo = lax.ppermute(jnp.stack([depth[:, half - EDGE :], gbo[:, half - EDGE :]]), TIME, up)
    e_hi = lax.ppermute(jnp.stack([depth[:, :EDGE], gbo[:, :EDGE]]), TIME, down)

    out_first, sent = sum_start(s, act, w_out_4)
    depth, gbo = after([depth, gbo], sent)
    gd, gp = backward(s, depth, gbo, e_lo, e_hi, sums, bn, prm, proj)
    gn_first, sent = sum_start(s, gp, w_in_4)
    (act_m,) = after([act], sent)
    out_last, sent = sum_middle(s, act_m, w_out_4, out_first)
    (gp_r,) = after([gp], sent)
    rs = row_sums(gp_r, proj, g_w)
    (gp_w,) = after([gp], rs)
    mine, theirs, tu = weight_grads(
        s,
        normed,
        gp_w.reshape(recs * half, 2 * chans),
        grad_out,
        act.reshape(recs * half, chans),
        w_in_all,
    )
    (gp_m,) = after([gp], mine)
    gn_last, sent = sum_middle(s, gp_m, w_in_4, gn_first)
    mine, theirs = after([mine, theirs], sent)
    parts = core_sum(s, mine, hop(theirs, "c", 1))
    (gp_e,) = after([gp], parts[0])
    gn_keep, gn_got = sum_end(s, gp_e, w_in_4, gn_first, gn_last)
    gd, glu = after([gd, glu], gn_keep)
    gwd = taps_grad(gd, glu, g_lo, g_hi)
    (act_e,) = after([act], gwd)
    out_keep, out_got = sum_end(s, act_e, w_out_4, out_first, out_last)

    tu = tu.T.reshape(2, 2, 4, own).transpose(1, 2, 0, 3)
    mine_x = (jnp.arange(4) == x).astype(F32)[None, :, None, None]
    taps4 = gwd[:TAPS].reshape(TAPS, 2, own).transpose(1, 0, 2)[:, None] * mine_x
    rs_rows = recs * 2 * half // own
    rs8 = jnp.broadcast_to(rs.transpose(2, 0, 1).reshape(1, 1, rs_rows, own), (2, 4, rs_rows, own))
    small = jnp.concatenate([taps4, tu, rs8], axis=2).reshape(8, TAPS + 2 + rs_rows, own)
    small = lax.all_to_all(small, CHAN, 0, 0, tiled=True)
    rs_all = jnp.sum(small[:, TAPS + 2 :].reshape(2, 4, 2, recs, half), axis=1).transpose(0, 2, 3, 1)
    small = jnp.sum(small[:, : TAPS + 2], axis=0)
    block_out = last_call(out_body, s, out_keep, out_got, [frames], [], [], "block_out")
    grad_w_depth, grad_ln = params_end(spread(small, CTX), own_gain, own_bias)

    grad_frames = last_call(
        frames_body,
        s,
        gn_keep,
        gn_got,
        [frames, grad_out],
        [stat, rs_all, own_gain[None]],
        [
            pl.BlockSpec((1, length, 2), lambda b, s: (b, 0, 0)),
            pl.BlockSpec((2, 1, half, 2), lambda b, s: (0, b, 0, 0)),
            pl.BlockSpec((1, own), lambda b, s: (0, 0)),
        ],
        "grad_frames",
    )

    parts = [parts[0]] + [hop(parts[r], "z", r) for r in range(1, 4)]
    g_fin, to_yl, to_yh, to_xx = ring_sum(s, parts)
    grad_w_in, grad_w_out = weights_end(
        g_fin,
        hop(to_yl, "yl", 1),
        hop(to_yh, "yh", 1),
        lax.ppermute(to_xx, ("yh", "yl"), [(i, 3 - i) for i in range(4)]),
    )

    grad_bn = lax.dynamic_index_in_dim(jnp.sum(sums, axis=0).reshape(2, 2, own), yl, 1, False)
    return (block_out, grad_frames, grad_w_in, grad_w_out, grad_w_depth, grad_bn, grad_ln)


def solution(mesh):
    split = Mesh(mesh.devices.reshape(2, 4, 2, 2, 4), ("yh", "z", "c", "yl", "x"))
    placed = (
        P(None, CTX, None),
        P(),
        P(),
        P(CTX, None, CHAN),
        P(None, CHAN),
        P(CHAN),
        P(CHAN),
        P(CTX, CHAN),
        P(),
        P(None, CTX, None),
    )
    return jax.shard_map(
        on_device,
        mesh=split,
        in_specs=placed,
        out_specs=(
            P(None, CTX, CHAN),
            P(None, CTX, CHAN),
            P(CTX, None, CHAN),
            P(CTX, CHAN),
            P(None, CHAN),
            P(None, CHAN),
            P(None, CHAN),
        ),
        check_vma=False,
    )
```

```python
import functools

import jax
import jax.numpy as jnp
from jax import lax
from jax.experimental import pallas as pl
from jax.experimental.pallas import tpu as pltpu
from jax.sharding import Mesh
from jax.sharding import PartitionSpec as P

F32 = jnp.float32
BF16 = jnp.bfloat16
CTX = ("yh", "z", "c")
CHAN = ("yl", "x")
TIME = ("yh", "z", "c", "yl")
EPS = 1e-05
TAPS = 31
EDGE = 16
LIMIT = pltpu.CompilerParams(vmem_limit_bytes=50 * 1024 * 1024)

S_YL, S_X, S_PAIR, S_ODD, S_POS, S_LEN, S_Z, S_C, S_YH = 0, 1, 2, 3, 4, 5, 7, 8, 9

SMEM = pl.BlockSpec(memory_space=pltpu.SMEM)
VMEM = pl.BlockSpec(memory_space=pltpu.VMEM)
ANY = pl.BlockSpec(memory_space=pl.ANY)


def cost(flops, nbytes):
    return pl.CostEstimate(flops=flops // 50, bytes_accessed=nbytes // 50, transcendentals=0)


LONG = pl.CostEstimate(flops=0, bytes_accessed=100 * 1024 * 1024, transcendentals=0)


def sds(shape, dtype):
    return jax.ShapeDtypeStruct(shape, dtype)


def nt(a, b):
    return lax.dot_general(a, b, (((1,), (1,)), ((), ())), preferred_element_type=F32)


def ln_body(s, fr, gain, bias, normed, stat):
    v = fr[0].astype(F32)
    mean = jnp.mean(v, axis=-1, keepdims=True)
    cen = v - mean
    rstd = lax.rsqrt(jnp.mean(cen * cen, axis=-1, keepdims=True) + EPS)
    stat[0, :, 0:1] = mean
    stat[0, :, 1:2] = rstd

    @pl.when(pl.program_id(0) == 0)
    def _():
        normed[...] = (cen * rstd * gain[...] + bias[...]).astype(BF16)


def layer_norm(s, frames, gain, bias):
    recs, length, width = frames.shape
    blk = length // 4

    def rows(h, b, i, s):
        return (b, jnp.where(h == 0, s[S_YL], 1 - s[S_YL]) * 2 + i, 0)

    return pl.pallas_call(
        ln_body,
        grid_spec=pltpu.PrefetchScalarGridSpec(
            num_scalar_prefetch=1,
            grid=(2, recs, 2),
            in_specs=[
                pl.BlockSpec((1, blk, width), rows),
                pl.BlockSpec((1, width), lambda h, b, i, s: (0, 0)),
                pl.BlockSpec((1, width), lambda h, b, i, s: (0, 0)),
            ],
            out_specs=[
                pl.BlockSpec((blk, width), lambda h, b, i, s: (jnp.where(h == 0, b * 2 + i, 2 * recs - 1), 0)),
                pl.BlockSpec((1, blk, 2), rows),
            ],
        ),
        out_shape=[sds((recs * length // 2, width), BF16), sds((recs, length, 2), F32)],
        compiler_params=LIMIT,
        cost_estimate=cost(recs * length * width * 10, 4 * recs * length * width),
        name="layer_norm",
    )(s, frames, gain[None], bias[None])


def place(s, pieces, out):
    z, c = s[S_Z], s[S_C]
    n = pieces[0].shape[1]
    for r in range(4):
        for k in range(2):
            for h in range(2):
                row = (h * 4 + lax.rem(z + r, 4)) * 2 + (c if k == 0 else 1 - c)
                out[pl.ds(pl.multiple_of(row * n, n), n), :] = pieces[2 * r + k][h]


def proj_body(s, normed, *refs, blk, half):
    pieces, (proj, glu, w) = refs[:8], refs[8:]
    i = pl.program_id(0)

    @pl.when(i == 0)
    def _():
        place(s, pieces, w)

    p = jnp.dot(normed[...], w[...], preferred_element_type=F32)
    proj[...] = p
    n = p.shape[1] // 2
    b = i // (half // blk)
    t = s[S_POS] + (i % (half // blk)) * blk + lax.broadcasted_iota(jnp.int32, (blk, 1), 0)
    valid = (t < s[S_LEN + b]).astype(F32)
    glu[...] = (p[:, :n] * jax.nn.sigmoid(p[:, n:]) * valid).astype(BF16)


def project(s, normed, pieces, half):
    rows, width = normed.shape
    _, shard, n2 = pieces[0].shape
    blk = half
    return pl.pallas_call(
        functools.partial(proj_body, blk=blk, half=half),
        grid_spec=pltpu.PrefetchScalarGridSpec(
            num_scalar_prefetch=1,
            grid=(rows // blk,),
            in_specs=[pl.BlockSpec((blk, width), lambda i, s: (i, 0))] + [VMEM] * 8,
            out_specs=[
                pl.BlockSpec((blk, n2), lambda i, s: (i, 0)),
                pl.BlockSpec((blk, n2 // 2), lambda i, s: (i, 0)),
                pl.BlockSpec((16 * shard, n2), lambda i, s: (0, 0)),
            ],
        ),
        out_shape=[sds((rows, n2), F32), sds((rows, n2 // 2), BF16), sds((16 * shard, n2), BF16)],
        compiler_params=LIMIT,
        cost_estimate=cost(2 * rows * width * n2, 2 * rows * width + 5 * rows * n2),
        name="project",
    )(s, normed, *pieces)


def gact_body(s, go, *refs):
    pieces, (out, w) = refs[:8], refs[8:]

    @pl.when((pl.program_id(0) == 0) & (pl.program_id(1) == 0))
    def _():
        place(s, pieces, w)

    out[0] = jnp.dot(go[0], w[...], preferred_element_type=F32)


def grad_act(s, grad_out, pieces):
    recs, length, width = grad_out.shape
    _, shard, n = pieces[0].shape
    blk = length // 2
    return pl.pallas_call(
        gact_body,
        grid_spec=pltpu.PrefetchScalarGridSpec(
            num_scalar_prefetch=1,
            grid=(recs, 1),
            in_specs=[pl.BlockSpec((1, blk, width), lambda b, i, s: (b, s[S_YL] + i, 0))] + [VMEM] * 8,
            out_specs=[
                pl.BlockSpec((1, blk, n), lambda b, i, s: (b, i, 0)),
                pl.BlockSpec((16 * shard, n), lambda b, i, s: (0, 0)),
            ],
        ),
        out_shape=[sds((recs, length // 2, n), F32), sds((16 * shard, n), BF16)],
        compiler_params=LIMIT,
        cost_estimate=cost(recs * length * width * n, recs * length * (width + 2 * n)),
        name="grad_act",
    )(s, grad_out, *pieces)


def tn(a, b):
    return lax.dot_general(a, b, (((0,), (0,)), ((), ())), preferred_element_type=F32)


def wgrad_body(s, normed, gp, go, act, w, mine, theirs, tu, colsum):
    shard = mine.shape[1]
    n2 = gp.shape[1]

    @pl.when(pl.program_id(0) == 0)
    def _():
        colsum[...] = jnp.sum(gp[...].astype(F32), axis=0, keepdims=True)

    g_in = tn(normed[...], gp[...])
    wide = w[...].astype(F32)
    tu[:, 0:1] = jnp.sum(wide * g_in, axis=1, keepdims=True)
    tu[:, 1:2] = jnp.sum(wide * colsum[...], axis=1, keepdims=True)
    g_out = tn(go[...].reshape(-1, go.shape[2]), act[...])
    first = s[S_C] == 0
    for i in range(2):
        r0 = 2 * i * shard
        for g, cols in ((g_in, slice(0, n2)), (g_out, slice(n2, n2 + g_out.shape[1]))):
            top, low = g[r0 : r0 + shard], g[r0 + shard : r0 + 2 * shard]
            mine[i, :, cols] = jnp.where(first, top, low).astype(BF16)
            theirs[i, :, cols] = jnp.where(first, low, top).astype(BF16)


def weight_grads(s, normed, gp, grad_out, act, w):
    rows, width = normed.shape
    n2, n = gp.shape[1], act.shape[1]
    recs, length, _ = grad_out.shape
    blk = width // 4
    shard = width // 16
    part = pl.BlockSpec((2, shard, n2 + n), lambda k, s: (k, 0, 0))
    return pl.pallas_call(
        wgrad_body,
        grid_spec=pltpu.PrefetchScalarGridSpec(
            num_scalar_prefetch=1,
            grid=(4,),
            in_specs=[
                pl.BlockSpec((rows, blk), lambda k, s: (0, k)),
                pl.BlockSpec((rows, n2), lambda k, s: (0, 0)),
                pl.BlockSpec((recs, length // 2, blk), lambda k, s: (0, s[S_YL], k)),
                pl.BlockSpec((rows, n), lambda k, s: (0, 0)),
                pl.BlockSpec((blk, n2), lambda k, s: (k, 0)),
            ],
            out_specs=[part, part, pl.BlockSpec((blk, 2), lambda k, s: (k, 0))],
            scratch_shapes=[pltpu.VMEM((1, n2), F32)],
        ),
        out_shape=[sds((8, shard, n2 + n), BF16)] * 2 + [sds((width, 2), F32)],
        compiler_params=LIMIT,
        cost_estimate=cost(2 * rows * width * (n2 + n), 4 * rows * width),
        name="weight_grads",
    )(s, normed, gp, grad_out, act, w)


def core_body(s, mine, got, *outs):
    for r, out in enumerate(outs):
        q = lax.rem(s[S_Z] + r, 4)
        for h in range(2):
            out[h] = (mine[h * 4 + q].astype(F32) + got[h * 4 + q].astype(F32)).astype(BF16)


def core_sum(s, mine, got):
    _, shard, n = mine.shape
    return pl.pallas_call(
        core_body,
        in_specs=[SMEM, VMEM, VMEM],
        out_specs=[VMEM] * 4,
        out_shape=[sds((2, shard, n), BF16)] * 4,
        compiler_params=LIMIT,
        cost_estimate=cost(16 * shard * n, 48 * shard * n),
        name="core_sum",
    )(s, mine, got)


def ring_body(s, p0, p1, p2, p3, own, to_yl, to_yh, to_xx):
    n = own.shape[1] // 3

    def total(h):
        return p0[h].astype(F32) + p1[h].astype(F32) + p2[h].astype(F32) + p3[h].astype(F32)

    first = s[S_YL] == 0
    for v, here, there in ((total(s[S_YH]), own, to_yl), (total(1 - s[S_YH]), to_yh, to_xx)):
        for g in range(3):
            low, high = v[:, 2 * g * n : (2 * g + 1) * n], v[:, (2 * g + 1) * n : (2 * g + 2) * n]
            cols = slice(g * n, g * n + n)
            here[:, cols] = jnp.where(first, low, high).astype(here.dtype)
            there[:, cols] = jnp.where(first, high, low).astype(there.dtype)


def ring_sum(s, parts):
    _, shard, n = parts[0].shape
    return pl.pallas_call(
        ring_body,
        in_specs=[SMEM] + [VMEM] * 4,
        out_specs=[VMEM] * 4,
        out_shape=[sds((shard, n // 2), F32)] + [sds((shard, n // 2), BF16)] * 3,
        compiler_params=LIMIT,
        cost_estimate=cost(8 * shard * n, 24 * shard * n),
        name="ring_sum",
    )(s, *parts)


def fill(pad, mid, lo, hi):
    recs, half = mid.shape[0], mid.shape[1]
    for b in range(recs):
        for j in range(mid.shape[2] // 128):
            lanes = slice(128 * j, 128 * j + 128)
            pad[b, j, 0:EDGE, :] = lo[b, :, lanes].astype(F32)
            pad[b, j, EDGE : EDGE + half, :] = mid[b, :, lanes].astype(F32)
            pad[b, j, EDGE + half :, :] = hi[b, :, lanes].astype(F32)


def tile_mask(start, rows, length):
    t = start + lax.broadcasted_iota(jnp.int32, (rows, 128), 0)
    return ((t >= 0) & (t < length)).astype(F32)


def local_count(s, half):
    n = jnp.int32(0)
    for b in range(2):
        n = n + jnp.clip(s[S_LEN + b] - s[S_POS], 0, half)
    return jnp.maximum(n, 1).astype(F32)


def fold(v):
    return jnp.sum(v.reshape(-1, 8, v.shape[1]), axis=0)


TILE = 96


def conv_body(s, glu, lo, hi, w, depth, stat, pad):
    recs, half, chans = glu.shape
    fill(pad, glu, lo, hi)
    count = local_count(s, half)
    for j in range(chans // 128):
        lanes = slice(128 * j, 128 * j + 128)
        total = jnp.zeros((8, 128), F32)
        for b in range(recs):

            def step(i, total, b=b):
                r0 = pl.multiple_of(i * TILE, 8)
                acc = jnp.zeros((TILE, 128), F32)
                for o in range(TAPS):
                    acc = acc + pad[b, j, pl.ds(r0 + o + 1, TILE), :] * w[o : o + 1, lanes]
                depth[b, pl.ds(r0, TILE), lanes] = acc
                return total + fold(acc * tile_mask(s[S_POS] + r0, TILE, s[S_LEN + b]))

            total = lax.fori_loop(0, half // TILE, step, total)
        mean = jnp.sum(total, axis=0, keepdims=True) / count
        spread = jnp.zeros((8, 128), F32)
        for b in range(recs):

            def step2(i, spread, b=b):
                r0 = pl.multiple_of(i * TILE, 8)
                d = (depth[b, pl.ds(r0, TILE), lanes] - mean) * tile_mask(s[S_POS] + r0, TILE, s[S_LEN + b])
                return spread + fold(d * d)

            spread = lax.fori_loop(0, half // TILE, step2, spread)
        stat[0:1, lanes] = mean
        stat[0:1, slice(chans + 128 * j, chans + 128 * j + 128)] = jnp.sum(spread, axis=0, keepdims=True)


def conv(s, glu, lo, hi, w):
    recs, half, chans = glu.shape
    return pl.pallas_call(
        conv_body,
        in_specs=[SMEM, VMEM, VMEM, VMEM, VMEM],
        out_specs=[VMEM, VMEM],
        out_shape=[sds((recs, half, chans), F32), sds((1, 2 * chans), F32)],
        scratch_shapes=[pltpu.VMEM((recs, chans // 128, half + 2 * EDGE, 128), F32)],
        compiler_params=LIMIT,
        cost_estimate=cost(recs * half * chans * 62 * 50, recs * half * chans * 6),
        name="conv",
    )(s, glu, lo, hi, w)


def bn_stats(s, got, half, chans):
    dev = got.shape[0]
    start = half * lax.broadcasted_iota(jnp.int32, (dev, 1), 0)
    n = jnp.zeros((dev, 1), jnp.int32)
    for b in range(2):
        n = n + jnp.clip(s[S_LEN + b] - start, 0, half)
    n = n.astype(F32)
    count = (s[S_LEN].astype(F32)) + (s[S_LEN + 1].astype(F32))
    means, spread = got[:, :chans], got[:, chans:]
    mean = jnp.sum(n * means, axis=0, keepdims=True) / count
    var = jnp.sum(spread + n * (means - mean) ** 2, axis=0, keepdims=True) / count
    return mean, lax.rsqrt(var + EPS), count


def act_body(s, depth, gact, got, prm, act, gbo, sums, bn, *, half):
    b = pl.program_id(0)
    i = pl.program_id(1)
    rows, chans = depth.shape[1], depth.shape[2]

    @pl.when((b == 0) & (i == 0))
    def _():
        mean, rstd, _ = bn_stats(s, got, half, chans)
        bn[0:1, :] = mean
        bn[1:2, :] = rstd
        sums[...] = jnp.zeros_like(sums)

    for j in range(chans // 128):
        lanes = slice(128 * j, 128 * j + 128)
        high = slice(chans + 128 * j, chans + 128 * j + 128)
        mean, rstd = bn[0:1, lanes], bn[1:2, lanes]
        gain, bias = prm[31:32, lanes], prm[32:33, lanes]
        one = jnp.zeros((8, 128), F32)
        two = jnp.zeros((8, 128), F32)
        for k in range(rows // TILE):
            r = slice(k * TILE, k * TILE + TILE)
            hat = (depth[0, r, lanes] - mean) * rstd
            out = hat * gain + bias
            g = jax.nn.sigmoid(out)
            m = tile_mask(s[S_POS] + i * rows + k * TILE, TILE, s[S_LEN + b])
            act[0, r, lanes] = (out * g * m).astype(BF16)
            gb = gact[0, r, lanes] * m * (g * (1.0 + out * (1.0 - g)))
            gbo[0, r, lanes] = gb
            one = one + fold(gb * hat)
            two = two + fold(gb)
        sums[0:1, lanes] += jnp.sum(one, axis=0, keepdims=True)
        sums[0:1, high] += jnp.sum(two, axis=0, keepdims=True)


def activate(s, depth, gact, got, prm):
    recs, half, chans = depth.shape
    blk = half // 2
    block = pl.BlockSpec((1, blk, chans), lambda b, i, s: (b, i, 0))
    whole = lambda a: pl.BlockSpec(a.shape, lambda b, i, s: (0, 0))
    return pl.pallas_call(
        functools.partial(act_body, half=half),
        grid_spec=pltpu.PrefetchScalarGridSpec(
            num_scalar_prefetch=1,
            grid=(recs, 2),
            in_specs=[block, block, whole(got), whole(prm)],
            out_specs=[block, block, pl.BlockSpec((1, 2 * chans), lambda b, i, s: (0, 0)), pl.BlockSpec((8, chans), lambda b, i, s: (0, 0))],
        ),
        out_shape=[sds(depth.shape, BF16), sds(depth.shape, F32), sds((1, 2 * chans), F32), sds((8, chans), F32)],
        compiler_params=LIMIT,
        cost_estimate=cost(recs * half * chans * 200, recs * half * chans * 14),
        name="activate",
    )(s, depth, gact, got, prm)


def back_body(s, depth, gbo, lo, hi, sums, bn, prm, proj, gd_out, gp, pad):
    recs, half, chans = depth.shape
    total = jnp.sum(sums[...], axis=0, keepdims=True)
    count = (s[S_LEN].astype(F32)) + (s[S_LEN + 1].astype(F32))
    pos = s[S_POS]
    for j in range(chans // 128):
        lanes = slice(128 * j, 128 * j + 128)
        high = slice(chans + 128 * j, chans + 128 * j + 128)
        gsum, bsum = total[:, lanes], total[:, high]
        mean, rstd = bn[0:1, lanes], bn[1:2, lanes]
        scale = prm[31:32, lanes] * rstd

        def grad(dep, gb, start, length):
            m = tile_mask(start, dep.shape[0], length)
            hat = (dep - mean) * rstd
            return m * scale * (gb - (bsum + hat * gsum) / count)

        for b in range(recs):
            length = s[S_LEN + b]
            pad[b, j, 0:EDGE, :] = grad(lo[0, b, :, lanes], lo[1, b, :, lanes], pos - EDGE, length)
            pad[b, j, EDGE + half :, :] = grad(hi[0, b, :, lanes], hi[1, b, :, lanes], pos + half, length)

            def step(i, _, b=b, length=length):
                r0 = pl.multiple_of(i * TILE, 8)
                v = grad(depth[b, pl.ds(r0, TILE), lanes], gbo[b, pl.ds(r0, TILE), lanes], pos + r0, length)
                pad[b, j, pl.ds(pl.multiple_of(r0 + EDGE, 8), TILE), :] = v
                gd_out[b, pl.ds(r0, TILE), lanes] = v
                return 0

            lax.fori_loop(0, half // TILE, step, 0)

            def step2(i, _, b=b, length=length):
                r0 = pl.multiple_of(i * TILE, 16)
                acc = jnp.zeros((TILE, 128), F32)
                for o in range(TAPS):
                    acc = acc + pad[b, j, pl.ds(r0 + TAPS - o, TILE), :] * prm[o : o + 1, lanes]
                acc = acc * tile_mask(pos + r0, TILE, length)
                val = proj[b, pl.ds(r0, TILE), lanes]
                g = jax.nn.sigmoid(proj[b, pl.ds(r0, TILE), high])
                gp[b, pl.ds(r0, TILE), lanes] = (acc * g).astype(BF16)
                gp[b, pl.ds(r0, TILE), high] = (acc * val * g * (1.0 - g)).astype(BF16)
                return 0

            lax.fori_loop(0, half // TILE, step2, 0)


def backward(s, depth, gbo, lo, hi, sums, bn, prm, proj):
    recs, half, chans = depth.shape
    return pl.pallas_call(
        back_body,
        in_specs=[SMEM] + [VMEM] * 8,
        out_specs=[VMEM, VMEM],
        out_shape=[sds(depth.shape, F32), sds((recs, half, 2 * chans), BF16)],
        scratch_shapes=[pltpu.VMEM((recs, chans // 128, half + 2 * EDGE, 128), F32)],
        compiler_params=LIMIT,
        cost_estimate=LONG,
        name="backward",
    )(s, depth, gbo, lo, hi, sums, bn, prm, proj)


def taps_body(gd, glu, lo, hi, gwd, pad):
    recs, half, chans = glu.shape
    fill(pad, glu, lo, hi)
    gwd[...] = jnp.zeros_like(gwd)
    for j in range(chans // 128):
        lanes = slice(128 * j, 128 * j + 128)
        accs = tuple(jnp.zeros((8, 128), F32) for _ in range(TAPS))
        for b in range(recs):

            def step(i, accs, b=b):
                r0 = pl.multiple_of(i * 16, 16)
                new = list(accs)
                for k in range(2):
                    g = gd[b, pl.ds(r0 + 8 * k, 8), lanes]
                    for o in range(TAPS):
                        new[o] = new[o] + g * pad[b, j, pl.ds(r0 + 8 * k + o + 1, 8), :]
                return tuple(new)

            accs = lax.fori_loop(0, half // 16, step, accs)
        for o in range(TAPS):
            gwd[o : o + 1, lanes] = jnp.sum(accs[o], axis=0, keepdims=True)


def taps_grad(gd, glu, lo, hi):
    recs, half, chans = glu.shape
    return pl.pallas_call(
        taps_body,
        in_specs=[VMEM] * 4,
        out_specs=VMEM,
        out_shape=sds((32, chans), F32),
        scratch_shapes=[pltpu.VMEM((recs, chans // 128, half + 2 * EDGE, 128), F32)],
        compiler_params=LIMIT,
        cost_estimate=cost(recs * half * chans * 62 * 50, recs * half * chans * 20),
        name="taps_grad",
    )(gd, glu, lo, hi)


def rows_body(gp, proj, gw, rs):
    recs, half, n2 = gp.shape
    lane = lax.broadcasted_iota(jnp.int32, (n2, 128), 1)
    row = lax.broadcasted_iota(jnp.int32, (16, n2), 0)
    total = gw[0:1, :] + gw[1:2, :]
    top = total.astype(BF16).astype(F32)
    taps = jnp.where(row == 0, top, jnp.where(row == 1, total - top, 0.0)).astype(BF16)
    pick_second = (lane == 1).astype(BF16)
    shift = gw[2:3, :] + gw[3:4, :]
    for b in range(recs):
        g = gp[b]
        one = jnp.sum(nt(g, taps), axis=1, keepdims=True)
        p = g.astype(F32) * (proj[b] - shift)
        top = p.astype(BF16)
        low = (p - top.astype(F32)).astype(BF16)
        two = jnp.dot(top, pick_second, preferred_element_type=F32) + jnp.dot(low, pick_second, preferred_element_type=F32)
        first = lax.broadcasted_iota(jnp.int32, two.shape, 1) == 0
        rs[b] = jnp.where(first, one, two)[:, 0:2]


def row_sums(gp, proj, gw):
    recs, half, n2 = gp.shape
    return pl.pallas_call(
        rows_body,
        in_specs=[VMEM] * 3,
        out_specs=VMEM,
        out_shape=sds((recs, half, 2), F32),
        compiler_params=LIMIT,
        cost_estimate=cost(recs * half * n2 * 8, recs * half * n2 * 6),
        name="row_sums",
    )(gp, proj, gw)


def through_body(gain, bias, w, out):
    def split(v):
        top = v.astype(BF16).astype(F32)
        return top, v - top

    g1, g2 = split(gain[...])
    b1, b2 = split(bias[...])
    row = lax.broadcasted_iota(jnp.int32, (16, gain.shape[1]), 0)
    v = jnp.where(row == 0, g1, jnp.where(row == 1, g2, jnp.where(row == 2, b1, jnp.where(row == 3, b2, 0.0))))
    out[...] = jnp.dot(v.astype(BF16), w[...], preferred_element_type=F32)


def through(gain, bias, w):
    return pl.pallas_call(
        through_body,
        in_specs=[VMEM] * 3,
        out_specs=VMEM,
        out_shape=sds((16, w.shape[1]), F32),
        compiler_params=LIMIT,
        cost_estimate=cost(32 * w.shape[0] * w.shape[1], 2 * w.shape[0] * w.shape[1]),
        name="through",
    )(gain[None], bias[None], w)


def turn_body(w, out, cat):
    n = w.shape[1]
    for d in range(4):
        cat[0:n, :] = w[d]
        cat[n:, :] = w[d + 4]
        out[d] = cat[...].T


def turned(w):
    n, depth = w.shape[0] // 8, w.shape[1]
    return pl.pallas_call(
        turn_body,
        in_specs=[VMEM],
        out_specs=VMEM,
        out_shape=sds((4, depth, 2 * n), BF16),
        scratch_shapes=[pltpu.VMEM((2 * n, depth), BF16)],
        compiler_params=LIMIT,
        cost_estimate=cost(32 * n * depth, 32 * n * depth),
        name="turned",
    )(w.reshape(8, n, depth))


def blocks_body(s, lhs, w, *refs, jobs, adds):
    plus, outs = refs[:adds], refs[adds:]
    half = lhs.shape[1]
    for rec, r, to, at in jobs:
        v = jnp.dot(lhs[rec], w[lax.rem(s[S_X] + r, 4)], preferred_element_type=F32)
        if adds:
            v = v + plus[to][0:half, :].astype(F32)
        outs[to][at * half : (at + 1) * half, :] = v.astype(BF16)


def blocks(s, lhs, w4, jobs, plus=()):
    recs, half, depth = lhs.shape
    n = w4.shape[2]
    each = len(jobs) // 2
    return pl.pallas_call(
        functools.partial(blocks_body, jobs=jobs, adds=len(plus)),
        in_specs=[SMEM] + [VMEM] * (2 + len(plus)),
        out_specs=[VMEM] * 2,
        out_shape=[sds((each * half, n), BF16)] * 2,
        compiler_params=LIMIT,
        cost_estimate=cost(2 * half * depth * n * len(jobs), 4 * half * depth + 8 * n * depth),
        name="blocks",
    )(s, lhs, w4, *plus)


def finish_body(s, lhs, w, up, down, last_a, last_b, keep, give):
    half = lhs.shape[1]
    n = w.shape[2] // 2
    first = s[S_YL] == 0
    for rec, (one, two) in enumerate(((last_a, down), (last_b, up))):
        v = jnp.dot(lhs[rec], w[s[S_X]], preferred_element_type=F32)
        v = v + one[...].astype(F32) + two[half:, :].astype(F32)
        low, high = v[:, :n], v[:, n:]
        keep[:, rec * n : (rec + 1) * n] = jnp.where(first, low, high)
        give[:, rec * n : (rec + 1) * n] = jnp.where(first, high, low).astype(BF16)


def finish(s, lhs, w4, parts, estimate):
    recs, half, depth = lhs.shape
    n = w4.shape[2] // 2
    return pl.pallas_call(
        finish_body,
        in_specs=[SMEM] + [VMEM] * 6,
        out_specs=[VMEM] * 2,
        out_shape=[sds((half, recs * n), F32), sds((half, recs * n), BF16)],
        compiler_params=LIMIT,
        cost_estimate=estimate,
        name="finish",
    )(s, lhs, w4, *parts)


def weights_body(own, one, two, three, g_in, g_out):
    v = own[...] + one[...].astype(F32) + two[...].astype(F32) + three[...].astype(F32)
    n = g_out.shape[1]
    g_in[:, 0, :] = v[:, :n]
    g_in[:, 1, :] = v[:, n : 2 * n]
    g_out[...] = v[:, 2 * n :]


def weights_end(own, *got):
    shard, n3 = own.shape
    return pl.pallas_call(
        weights_body,
        in_specs=[VMEM] * 4,
        out_specs=[VMEM] * 2,
        out_shape=[sds((shard, 2, n3 // 3), F32), sds((shard, n3 // 3), F32)],
        compiler_params=LIMIT,
        cost_estimate=cost(4 * shard * n3, 14 * shard * n3),
        name="weights_end",
    )(own, *got)


def params_body(got, gain, bias, taps, ln):
    v = jnp.sum(got[...], axis=0)
    taps[...] = v[:TAPS]
    t, u = v[TAPS : TAPS + 1], v[TAPS + 1 : TAPS + 2]
    ln[0:1, :] = (t - bias[...] * u) / gain[...]
    ln[1:2, :] = u


def params_end(got, gain, bias):
    n = got.shape[2]
    return pl.pallas_call(
        params_body,
        in_specs=[VMEM] * 3,
        out_specs=[VMEM] * 2,
        out_shape=[sds((TAPS, n), F32), sds((2, n), F32)],
        compiler_params=LIMIT,
        cost_estimate=cost(got.size, 4 * got.size),
        name="params_end",
    )(got, gain[None], bias[None])


def hop(v, axis, by):
    n = lax.axis_size(axis)
    return lax.ppermute(v, axis, [(i, (i + by) % n) for i in range(n)])


def sum_start(s, lhs, w8):
    sent = blocks(s, lhs, w8, ((0, 2, 0, 0), (1, 2, 1, 0), (1, 1, 0, 1), (0, 3, 1, 1)))
    return (hop(sent[0], "x", 1), hop(sent[1], "x", -1)), sent[0]


def sum_middle(s, lhs, w8, got):
    sent = blocks(s, lhs, w8, ((0, 1, 0, 0), (1, 3, 1, 0)), got)
    return (hop(sent[0], "x", 1), hop(sent[1], "x", -1)), sent[0]


def sum_end(s, lhs, w8, got, last):
    keep, give = finish(s, lhs, w8, (*got, *last), cost(0, 0))
    return keep, hop(give, "yl", 1)


def after(values, *first):
    return lax.optimization_barrier((*values, *first))[: len(values)]


def pick(block, odd):
    n = block.shape[1] // 2
    return jnp.where(odd == 1, block[:, n:].astype(F32), block[:, :n].astype(F32))


def halves(s, keep, got):
    n = keep.shape[1] // 2
    early = pl.program_id(0) == 0
    mine = jnp.where(early, keep[:, :n], keep[:, n:])
    theirs = jnp.where(early, got[:, :n].astype(F32), got[:, n:].astype(F32))
    first = s[S_YL] == 0
    return jnp.where(first, mine, theirs), jnp.where(first, theirs, mine)


def out_body(s, keep, got, fr, out):
    half = keep.shape[0]
    for h, v in enumerate(halves(s, keep, got)):
        rows = slice(h * half, h * half + half)
        out[0, :, rows] = (pick(fr[0, rows, :], s[S_ODD]) + v).T.astype(BF16)


def frames_body(s, keep, got, fr, go, stat, rs, gain, out):
    half = keep.shape[0]
    width = 8 * out.shape[1]
    for h, v in enumerate(halves(s, keep, got)):
        rows = slice(h * half, h * half + half)
        g = v * gain[...]
        mean, rstd = stat[0, rows, 0:1], stat[0, rows, 1:2]
        first, second = rs[h, 0, :, 0:1], rs[h, 0, :, 1:2]
        hat = (pick(fr[0, rows, :], s[S_ODD]) - mean) * rstd
        v = rstd * (g - first / width - hat * (second / width)) + pick(go[0, rows, :], s[S_ODD])
        out[0, :, rows] = v.T.astype(BF16)


def last_call(body, s, keep, got, wide, extra, extra_specs, name):
    recs, length, _ = wide[0].shape
    half, n = length // 2, keep.shape[1] // 2
    cols = pl.BlockSpec((1, 2 * half, 2 * n), lambda b, s: (b, 0, s[S_PAIR]))
    return pl.pallas_call(
        body,
        grid_spec=pltpu.PrefetchScalarGridSpec(
            num_scalar_prefetch=1,
            grid=(recs,),
            in_specs=[
                pl.BlockSpec((half, recs * n), lambda b, s: (0, 0)),
                pl.BlockSpec((half, recs * n), lambda b, s: (0, 0)),
            ]
            + [cols] * len(wide)
            + extra_specs,
            out_specs=pl.BlockSpec((1, n, 2 * half), lambda b, s: (b, 0, 0)),
        ),
        out_shape=sds((recs, n, 2 * half), BF16),
        compiler_params=LIMIT,
        cost_estimate=cost(recs * half * n * 20, recs * half * n * 20),
        name=name,
    )(s, keep, got, *wide, *extra).transpose(0, 2, 1)


def spread(v, axes):
    n = lax.axis_size(axes)
    return lax.all_to_all(jnp.broadcast_to(v[None], (n, *v.shape)), axes, 0, 0, tiled=True)


def on_device(frames, ln_gain, ln_bias, w_in, w_depth, bn_gain, bn_bias, w_out, lengths, grad_out):
    recs, length, width = frames.shape
    shard, _, own = w_in.shape
    half = length // 2
    chans = 2 * own
    yh, z, c, yl, x = (lax.axis_index(a) for a in ("yh", "z", "c", "yl", "x"))
    ctx = (yh * 4 + z) * 2 + c
    chan = yl * 4 + x
    time = ctx * 2 + yl
    s = jnp.stack([yl, x, chan // 2, chan % 2, time * half, lengths[0], lengths[1], z, c, yh]).astype(jnp.int32)

    w3 = jnp.concatenate([w_in.reshape(shard, 2 * own), w_out], axis=1)
    w_yl = hop(w3, "yl", 1)
    w_yh = hop(w3, "yh", 1)
    w_xx = lax.ppermute(w3, ("yh", "yl"), [(i, 3 - i) for i in range(4)])

    def paired(a, b, g0, g1):
        lo, hi = jnp.where(yl == 0, a, b), jnp.where(yl == 0, b, a)
        cols = []
        for g in range(g0, g1):
            cols += [lo[:, g * own : (g + 1) * own], hi[:, g * own : (g + 1) * own]]
        return jnp.concatenate(cols, axis=1)

    def rows_two(g0, g1):
        same, other = paired(w3, w_yl, g0, g1), paired(w_yh, w_xx, g0, g1)
        return jnp.where(yh == 0, jnp.stack([same, other]), jnp.stack([other, same]))

    def gathered(v, first):
        pieces = []
        for r in range(4):
            p = v if r == 0 else hop(v, "z", -r)
            if first is not None:
                (p,) = after([p], first)
            pieces += [p, hop(p, "c", 1)]
        return pieces

    prm1 = jnp.concatenate([w_depth, bn_gain[None], bn_bias[None], jnp.zeros((7, own), F32)], axis=0)
    prm2 = hop(prm1, "yl", 1)
    prm = jnp.where(yl == 0, jnp.concatenate([prm1, prm2], axis=1), jnp.concatenate([prm2, prm1], axis=1))
    (in_two,) = after([rows_two(0, 2)], prm2)
    normed, stat = layer_norm(s, *after([frames, ln_gain, ln_bias], in_two))
    in_pieces = gathered(in_two, normed)
    out_pieces = gathered(*after([rows_two(2, 3)], *in_pieces), None)
    proj, glu, w_in_all = project(s, normed, in_pieces, half)
    glu = glu.reshape(recs, half, chans)
    proj = proj.reshape(recs, half, 2 * chans)
    own_gain = lax.dynamic_slice_in_dim(ln_gain, chan * own, own, 0)
    own_bias = lax.dynamic_slice_in_dim(ln_bias, chan * own, own, 0)
    devices = lax.axis_size(TIME)
    up = [(i, i + 1) for i in range(devices - 1)]
    down = [(i + 1, i) for i in range(devices - 1)]
    g_lo = lax.ppermute(glu[:, half - EDGE :], TIME, up)
    g_hi = lax.ppermute(glu[:, :EDGE], TIME, down)
    gact, w_out_all = grad_act(s, grad_out, out_pieces)
    (glu_c,) = after([glu], gact)
    depth, bn_own = conv(s, glu_c, g_lo, g_hi, prm)
    bn_all = spread(bn_own, TIME).reshape(devices, 2 * chans)
    w_out_4 = turned(*after([w_out_all], bn_own))
    w_in_4 = turned(*after([w_in_all], bn_own))
    g_w = through(*after([ln_gain, ln_bias, w_in_all], bn_own))
    (gact,) = after([gact], w_out_4, w_in_4, g_w)
    act, gbo, sums_own, bn = activate(s, depth, gact, bn_all, prm)
    sums = spread(sums_own, TIME).reshape(devices, 2 * chans)
    e_lo = lax.ppermute(jnp.stack([depth[:, half - EDGE :], gbo[:, half - EDGE :]]), TIME, up)
    e_hi = lax.ppermute(jnp.stack([depth[:, :EDGE], gbo[:, :EDGE]]), TIME, down)

    out_first, sent = sum_start(s, act, w_out_4)
    depth, gbo = after([depth, gbo], sent)
    gd, gp = backward(s, depth, gbo, e_lo, e_hi, sums, bn, prm, proj)
    gn_first, sent = sum_start(s, gp, w_in_4)
    (act_m,) = after([act], sent)
    out_last, sent = sum_middle(s, act_m, w_out_4, out_first)
    (gp_r,) = after([gp], sent)
    rs = row_sums(gp_r, proj, g_w)
    (gp_w,) = after([gp], rs)
    mine, theirs, tu = weight_grads(
        s,
        normed,
        gp_w.reshape(recs * half, 2 * chans),
        grad_out,
        act.reshape(recs * half, chans),
        w_in_all,
    )
    (gp_m,) = after([gp], mine)
    gn_last, sent = sum_middle(s, gp_m, w_in_4, gn_first)
    mine, theirs = after([mine, theirs], sent)
    parts = core_sum(s, mine, hop(theirs, "c", 1))
    (gp_e,) = after([gp], parts[0])
    gn_keep, gn_got = sum_end(s, gp_e, w_in_4, gn_first, gn_last)
    gd, glu = after([gd, glu], gn_keep)
    gwd = taps_grad(gd, glu, g_lo, g_hi)
    ring = [parts[0]] + [hop(parts[r], "z", r) for r in range(1, 4)]
    g_fin, to_yl, to_yh, to_xx = ring_sum(s, ring)
    (act_e,) = after([act], gwd)
    out_keep, out_got = sum_end(s, act_e, w_out_4, out_first, out_last)

    tu = tu.T.reshape(2, 2, 4, own).transpose(1, 2, 0, 3)
    mine_x = (jnp.arange(4) == x).astype(F32)[None, :, None, None]
    taps4 = gwd[:TAPS].reshape(TAPS, 2, own).transpose(1, 0, 2)[:, None] * mine_x
    rs_rows = recs * 2 * half // own
    rs8 = jnp.broadcast_to(rs.transpose(2, 0, 1).reshape(1, 1, rs_rows, own), (2, 4, rs_rows, own))
    small = jnp.concatenate([taps4, tu, rs8], axis=2).reshape(8, TAPS + 2 + rs_rows, own)
    (small,) = after([small], g_fin)
    small = lax.all_to_all(small, CHAN, 0, 0, tiled=True)
    rs_all = jnp.sum(small[:, TAPS + 2 :].reshape(2, 4, 2, recs, half), axis=1).transpose(0, 2, 3, 1)
    small = jnp.sum(small[:, : TAPS + 2], axis=0)
    block_out = last_call(out_body, s, out_keep, out_got, [frames], [], [], "block_out")
    grad_w_depth, grad_ln = params_end(spread(small, CTX), own_gain, own_bias)

    grad_frames = last_call(
        frames_body,
        s,
        gn_keep,
        gn_got,
        [frames, grad_out],
        [stat, rs_all, own_gain[None]],
        [
            pl.BlockSpec((1, length, 2), lambda b, s: (b, 0, 0)),
            pl.BlockSpec((2, 1, half, 2), lambda b, s: (0, b, 0, 0)),
            pl.BlockSpec((1, own), lambda b, s: (0, 0)),
        ],
        "grad_frames",
    )

    grad_w_in, grad_w_out = weights_end(
        g_fin,
        hop(to_yl, "yl", 1),
        hop(to_yh, "yh", 1),
        lax.ppermute(to_xx, ("yh", "yl"), [(i, 3 - i) for i in range(4)]),
    )

    grad_bn = lax.dynamic_index_in_dim(jnp.sum(sums, axis=0).reshape(2, 2, own), yl, 1, False)
    return (block_out, grad_frames, grad_w_in, grad_w_out, grad_w_depth, grad_bn, grad_ln)


def solution(mesh):
    split = Mesh(mesh.devices.reshape(2, 4, 2, 2, 4), ("yh", "z", "c", "yl", "x"))
    placed = (
        P(None, CTX, None),
        P(),
        P(),
        P(CTX, None, CHAN),
        P(None, CHAN),
        P(CHAN),
        P(CHAN),
        P(CTX, CHAN),
        P(),
        P(None, CTX, None),
    )
    return jax.shard_map(
        on_device,
        mesh=split,
        in_specs=placed,
        out_specs=(
            P(None, CTX, CHAN),
            P(None, CTX, CHAN),
            P(CTX, None, CHAN),
            P(CTX, CHAN),
            P(None, CHAN),
            P(None, CHAN),
            P(None, CHAN),
        ),
        check_vma=False,
    )
```

```python
import functools

import jax
import jax.numpy as jnp
from jax import lax
from jax.experimental import pallas as pl
from jax.experimental.pallas import tpu as pltpu
from jax.sharding import Mesh
from jax.sharding import PartitionSpec as P

F32 = jnp.float32
BF16 = jnp.bfloat16
CTX = ("yh", "z", "c")
CHAN = ("yl", "x")
TIME = ("yh", "z", "c", "yl")
EPS = 1e-05
TAPS = 31
EDGE = 16
LIMIT = pltpu.CompilerParams(vmem_limit_bytes=50 * 1024 * 1024)

S_YL, S_X, S_PAIR, S_ODD, S_POS, S_LEN, S_Z, S_C, S_YH = 0, 1, 2, 3, 4, 5, 7, 8, 9

SMEM = pl.BlockSpec(memory_space=pltpu.SMEM)
VMEM = pl.BlockSpec(memory_space=pltpu.VMEM)
ANY = pl.BlockSpec(memory_space=pl.ANY)


def cost(flops, nbytes):
    return pl.CostEstimate(flops=flops // 50, bytes_accessed=nbytes // 50, transcendentals=0)


LONG = pl.CostEstimate(flops=0, bytes_accessed=100 * 1024 * 1024, transcendentals=0)


def sds(shape, dtype):
    return jax.ShapeDtypeStruct(shape, dtype)


def nt(a, b):
    return lax.dot_general(a, b, (((1,), (1,)), ((), ())), preferred_element_type=F32)


def ln_body(s, fr, gain, bias, normed, stat):
    v = fr[0].astype(F32)
    mean = jnp.mean(v, axis=-1, keepdims=True)
    cen = v - mean
    rstd = lax.rsqrt(jnp.mean(cen * cen, axis=-1, keepdims=True) + EPS)
    stat[0, :, 0:1] = mean
    stat[0, :, 1:2] = rstd

    @pl.when(pl.program_id(0) == 0)
    def _():
        normed[...] = (cen * rstd * gain[...] + bias[...]).astype(BF16)


def layer_norm(s, frames, gain, bias):
    recs, length, width = frames.shape
    blk = length // 4

    def rows(h, b, i, s):
        return (b, jnp.where(h == 0, s[S_YL], 1 - s[S_YL]) * 2 + i, 0)

    return pl.pallas_call(
        ln_body,
        grid_spec=pltpu.PrefetchScalarGridSpec(
            num_scalar_prefetch=1,
            grid=(2, recs, 2),
            in_specs=[
                pl.BlockSpec((1, blk, width), rows),
                pl.BlockSpec((1, width), lambda h, b, i, s: (0, 0)),
                pl.BlockSpec((1, width), lambda h, b, i, s: (0, 0)),
            ],
            out_specs=[
                pl.BlockSpec((blk, width), lambda h, b, i, s: (jnp.where(h == 0, b * 2 + i, 2 * recs - 1), 0)),
                pl.BlockSpec((1, blk, 2), rows),
            ],
        ),
        out_shape=[sds((recs * length // 2, width), BF16), sds((recs, length, 2), F32)],
        compiler_params=LIMIT,
        cost_estimate=cost(recs * length * width * 10, 4 * recs * length * width),
        name="layer_norm",
    )(s, frames, gain[None], bias[None])


def place(s, pieces, out):
    z, c = s[S_Z], s[S_C]
    n = pieces[0].shape[1]
    for r in range(4):
        for k in range(2):
            for h in range(2):
                row = (h * 4 + lax.rem(z + r, 4)) * 2 + (c if k == 0 else 1 - c)
                out[pl.ds(pl.multiple_of(row * n, n), n), :] = pieces[2 * r + k][h]


def proj_body(s, normed, *refs, blk, half):
    pieces, (proj, glu, w) = refs[:8], refs[8:]
    i = pl.program_id(0)

    @pl.when(i == 0)
    def _():
        place(s, pieces, w)

    p = jnp.dot(normed[...], w[...], preferred_element_type=F32)
    proj[...] = p
    n = p.shape[1] // 2
    b = i // (half // blk)
    t = s[S_POS] + (i % (half // blk)) * blk + lax.broadcasted_iota(jnp.int32, (blk, 1), 0)
    valid = (t < s[S_LEN + b]).astype(F32)
    glu[...] = (p[:, :n] * jax.nn.sigmoid(p[:, n:]) * valid).astype(BF16)


def project(s, normed, pieces, half):
    rows, width = normed.shape
    _, shard, n2 = pieces[0].shape
    blk = half
    return pl.pallas_call(
        functools.partial(proj_body, blk=blk, half=half),
        grid_spec=pltpu.PrefetchScalarGridSpec(
            num_scalar_prefetch=1,
            grid=(rows // blk,),
            in_specs=[pl.BlockSpec((blk, width), lambda i, s: (i, 0))] + [VMEM] * 8,
            out_specs=[
                pl.BlockSpec((blk, n2), lambda i, s: (i, 0)),
                pl.BlockSpec((blk, n2 // 2), lambda i, s: (i, 0)),
                pl.BlockSpec((16 * shard, n2), lambda i, s: (0, 0)),
            ],
        ),
        out_shape=[sds((rows, n2), F32), sds((rows, n2 // 2), BF16), sds((16 * shard, n2), BF16)],
        compiler_params=LIMIT,
        cost_estimate=cost(2 * rows * width * n2, 2 * rows * width + 5 * rows * n2),
        name="project",
    )(s, normed, *pieces)


def gact_body(s, go, *refs):
    pieces, (out, w) = refs[:8], refs[8:]

    @pl.when((pl.program_id(0) == 0) & (pl.program_id(1) == 0))
    def _():
        place(s, pieces, w)

    out[0] = jnp.dot(go[0], w[...], preferred_element_type=F32)


def grad_act(s, grad_out, pieces):
    recs, length, width = grad_out.shape
    _, shard, n = pieces[0].shape
    blk = length // 2
    return pl.pallas_call(
        gact_body,
        grid_spec=pltpu.PrefetchScalarGridSpec(
            num_scalar_prefetch=1,
            grid=(recs, 1),
            in_specs=[pl.BlockSpec((1, blk, width), lambda b, i, s: (b, s[S_YL] + i, 0))] + [VMEM] * 8,
            out_specs=[
                pl.BlockSpec((1, blk, n), lambda b, i, s: (b, i, 0)),
                pl.BlockSpec((16 * shard, n), lambda b, i, s: (0, 0)),
            ],
        ),
        out_shape=[sds((recs, length // 2, n), F32), sds((16 * shard, n), BF16)],
        compiler_params=LIMIT,
        cost_estimate=cost(recs * length * width * n, recs * length * (width + 2 * n)),
        name="grad_act",
    )(s, grad_out, *pieces)


def tn(a, b):
    return lax.dot_general(a, b, (((0,), (0,)), ((), ())), preferred_element_type=F32)


def wgrad_body(s, normed, gp, go, act, w, mine, theirs, tu, colsum):
    shard = mine.shape[1]
    n2 = gp.shape[1]

    @pl.when(pl.program_id(0) == 0)
    def _():
        colsum[...] = jnp.sum(gp[...].astype(F32), axis=0, keepdims=True)

    g_in = tn(normed[...], gp[...])
    wide = w[...].astype(F32)
    tu[:, 0:1] = jnp.sum(wide * g_in, axis=1, keepdims=True)
    tu[:, 1:2] = jnp.sum(wide * colsum[...], axis=1, keepdims=True)
    g_out = tn(go[...].reshape(-1, go.shape[2]), act[...])
    first = s[S_C] == 0
    for i in range(2):
        r0 = 2 * i * shard
        for g, cols in ((g_in, slice(0, n2)), (g_out, slice(n2, n2 + g_out.shape[1]))):
            top, low = g[r0 : r0 + shard], g[r0 + shard : r0 + 2 * shard]
            mine[i, :, cols] = jnp.where(first, top, low).astype(BF16)
            theirs[i, :, cols] = jnp.where(first, low, top).astype(BF16)


def weight_grads(s, normed, gp, grad_out, act, w):
    rows, width = normed.shape
    n2, n = gp.shape[1], act.shape[1]
    recs, length, _ = grad_out.shape
    blk = width // 4
    shard = width // 16
    part = pl.BlockSpec((2, shard, n2 + n), lambda k, s: (k, 0, 0))
    return pl.pallas_call(
        wgrad_body,
        grid_spec=pltpu.PrefetchScalarGridSpec(
            num_scalar_prefetch=1,
            grid=(4,),
            in_specs=[
                pl.BlockSpec((rows, blk), lambda k, s: (0, k)),
                pl.BlockSpec((rows, n2), lambda k, s: (0, 0)),
                pl.BlockSpec((recs, length // 2, blk), lambda k, s: (0, s[S_YL], k)),
                pl.BlockSpec((rows, n), lambda k, s: (0, 0)),
                pl.BlockSpec((blk, n2), lambda k, s: (k, 0)),
            ],
            out_specs=[part, part, pl.BlockSpec((blk, 2), lambda k, s: (k, 0))],
            scratch_shapes=[pltpu.VMEM((1, n2), F32)],
        ),
        out_shape=[sds((8, shard, n2 + n), BF16)] * 2 + [sds((width, 2), F32)],
        compiler_params=LIMIT,
        cost_estimate=cost(2 * rows * width * (n2 + n), 4 * rows * width),
        name="weight_grads",
    )(s, normed, gp, grad_out, act, w)


def core_body(s, mine, got, *outs):
    for r, out in enumerate(outs):
        q = lax.rem(s[S_Z] + r, 4)
        for h in range(2):
            out[h] = (mine[h * 4 + q].astype(F32) + got[h * 4 + q].astype(F32)).astype(BF16)


def core_sum(s, mine, got):
    _, shard, n = mine.shape
    return pl.pallas_call(
        core_body,
        in_specs=[SMEM, VMEM, VMEM],
        out_specs=[VMEM] * 4,
        out_shape=[sds((2, shard, n), BF16)] * 4,
        compiler_params=LIMIT,
        cost_estimate=cost(16 * shard * n, 48 * shard * n),
        name="core_sum",
    )(s, mine, got)


def ring_body(s, p0, p1, p2, p3, own, to_yl, to_yh, to_xx):
    n = own.shape[1] // 3

    def total(h):
        return p0[h].astype(F32) + p1[h].astype(F32) + p2[h].astype(F32) + p3[h].astype(F32)

    first = s[S_YL] == 0
    for v, here, there in ((total(s[S_YH]), own, to_yl), (total(1 - s[S_YH]), to_yh, to_xx)):
        for g in range(3):
            low, high = v[:, 2 * g * n : (2 * g + 1) * n], v[:, (2 * g + 1) * n : (2 * g + 2) * n]
            cols = slice(g * n, g * n + n)
            here[:, cols] = jnp.where(first, low, high).astype(here.dtype)
            there[:, cols] = jnp.where(first, high, low).astype(there.dtype)


def ring_sum(s, parts):
    _, shard, n = parts[0].shape
    return pl.pallas_call(
        ring_body,
        in_specs=[SMEM] + [VMEM] * 4,
        out_specs=[VMEM] * 4,
        out_shape=[sds((shard, n // 2), F32)] + [sds((shard, n // 2), BF16)] * 3,
        compiler_params=LIMIT,
        cost_estimate=cost(8 * shard * n, 24 * shard * n),
        name="ring_sum",
    )(s, *parts)


def fill(pad, mid, lo, hi):
    recs, half = mid.shape[0], mid.shape[1]
    for b in range(recs):
        for j in range(mid.shape[2] // 128):
            lanes = slice(128 * j, 128 * j + 128)
            pad[b, j, 0:EDGE, :] = lo[b, :, lanes].astype(F32)
            pad[b, j, EDGE : EDGE + half, :] = mid[b, :, lanes].astype(F32)
            pad[b, j, EDGE + half :, :] = hi[b, :, lanes].astype(F32)


def tile_mask(start, rows, length):
    t = start + lax.broadcasted_iota(jnp.int32, (rows, 128), 0)
    return ((t >= 0) & (t < length)).astype(F32)


def local_count(s, half):
    n = jnp.int32(0)
    for b in range(2):
        n = n + jnp.clip(s[S_LEN + b] - s[S_POS], 0, half)
    return jnp.maximum(n, 1).astype(F32)


def fold(v):
    return jnp.sum(v.reshape(-1, 8, v.shape[1]), axis=0)


TILE = 96


def conv_body(s, glu, lo, hi, w, depth, stat, pad):
    recs, half, chans = glu.shape
    fill(pad, glu, lo, hi)
    count = local_count(s, half)
    for j in range(chans // 128):
        lanes = slice(128 * j, 128 * j + 128)
        total = jnp.zeros((8, 128), F32)
        for b in range(recs):

            def step(i, total, b=b):
                r0 = pl.multiple_of(i * TILE, 8)
                acc = jnp.zeros((TILE, 128), F32)
                for o in range(TAPS):
                    acc = acc + pad[b, j, pl.ds(r0 + o + 1, TILE), :] * w[o : o + 1, lanes]
                depth[b, pl.ds(r0, TILE), lanes] = acc
                return total + fold(acc * tile_mask(s[S_POS] + r0, TILE, s[S_LEN + b]))

            total = lax.fori_loop(0, half // TILE, step, total)
        mean = jnp.sum(total, axis=0, keepdims=True) / count
        spread = jnp.zeros((8, 128), F32)
        for b in range(recs):

            def step2(i, spread, b=b):
                r0 = pl.multiple_of(i * TILE, 8)
                d = (depth[b, pl.ds(r0, TILE), lanes] - mean) * tile_mask(s[S_POS] + r0, TILE, s[S_LEN + b])
                return spread + fold(d * d)

            spread = lax.fori_loop(0, half // TILE, step2, spread)
        stat[0:1, lanes] = mean
        stat[0:1, slice(chans + 128 * j, chans + 128 * j + 128)] = jnp.sum(spread, axis=0, keepdims=True)


def conv(s, glu, lo, hi, w):
    recs, half, chans = glu.shape
    return pl.pallas_call(
        conv_body,
        in_specs=[SMEM, VMEM, VMEM, VMEM, VMEM],
        out_specs=[VMEM, VMEM],
        out_shape=[sds((recs, half, chans), F32), sds((1, 2 * chans), F32)],
        scratch_shapes=[pltpu.VMEM((recs, chans // 128, half + 2 * EDGE, 128), F32)],
        compiler_params=LIMIT,
        cost_estimate=cost(recs * half * chans * 62 * 50, recs * half * chans * 6),
        name="conv",
    )(s, glu, lo, hi, w)


def bn_stats(s, got, half, chans):
    dev = got.shape[0]
    start = half * lax.broadcasted_iota(jnp.int32, (dev, 1), 0)
    n = jnp.zeros((dev, 1), jnp.int32)
    for b in range(2):
        n = n + jnp.clip(s[S_LEN + b] - start, 0, half)
    n = n.astype(F32)
    count = (s[S_LEN].astype(F32)) + (s[S_LEN + 1].astype(F32))
    means, spread = got[:, :chans], got[:, chans:]
    mean = jnp.sum(n * means, axis=0, keepdims=True) / count
    var = jnp.sum(spread + n * (means - mean) ** 2, axis=0, keepdims=True) / count
    return mean, lax.rsqrt(var + EPS), count


def act_body(s, depth, gact, got, prm, act, gbo, sums, bn, *, half):
    b = pl.program_id(0)
    i = pl.program_id(1)
    rows, chans = depth.shape[1], depth.shape[2]

    @pl.when((b == 0) & (i == 0))
    def _():
        mean, rstd, _ = bn_stats(s, got, half, chans)
        bn[0:1, :] = mean
        bn[1:2, :] = rstd
        sums[...] = jnp.zeros_like(sums)

    for j in range(chans // 128):
        lanes = slice(128 * j, 128 * j + 128)
        high = slice(chans + 128 * j, chans + 128 * j + 128)
        mean, rstd = bn[0:1, lanes], bn[1:2, lanes]
        gain, bias = prm[31:32, lanes], prm[32:33, lanes]
        one = jnp.zeros((8, 128), F32)
        two = jnp.zeros((8, 128), F32)
        for k in range(rows // TILE):
            r = slice(k * TILE, k * TILE + TILE)
            hat = (depth[0, r, lanes] - mean) * rstd
            out = hat * gain + bias
            g = jax.nn.sigmoid(out)
            m = tile_mask(s[S_POS] + i * rows + k * TILE, TILE, s[S_LEN + b])
            act[0, r, lanes] = (out * g * m).astype(BF16)
            gb = gact[0, r, lanes] * m * (g * (1.0 + out * (1.0 - g)))
            gbo[0, r, lanes] = gb
            one = one + fold(gb * hat)
            two = two + fold(gb)
        sums[0:1, lanes] += jnp.sum(one, axis=0, keepdims=True)
        sums[0:1, high] += jnp.sum(two, axis=0, keepdims=True)


def activate(s, depth, gact, got, prm):
    recs, half, chans = depth.shape
    blk = half // 2
    block = pl.BlockSpec((1, blk, chans), lambda b, i, s: (b, i, 0))
    whole = lambda a: pl.BlockSpec(a.shape, lambda b, i, s: (0, 0))
    return pl.pallas_call(
        functools.partial(act_body, half=half),
        grid_spec=pltpu.PrefetchScalarGridSpec(
            num_scalar_prefetch=1,
            grid=(recs, 2),
            in_specs=[block, block, whole(got), whole(prm)],
            out_specs=[block, block, pl.BlockSpec((1, 2 * chans), lambda b, i, s: (0, 0)), pl.BlockSpec((8, chans), lambda b, i, s: (0, 0))],
        ),
        out_shape=[sds(depth.shape, BF16), sds(depth.shape, F32), sds((1, 2 * chans), F32), sds((8, chans), F32)],
        compiler_params=LIMIT,
        cost_estimate=cost(recs * half * chans * 200, recs * half * chans * 14),
        name="activate",
    )(s, depth, gact, got, prm)


def back_body(s, depth, gbo, lo, hi, sums, bn, prm, proj, gd_out, gp, pad):
    recs, half, chans = depth.shape
    total = jnp.sum(sums[...], axis=0, keepdims=True)
    count = (s[S_LEN].astype(F32)) + (s[S_LEN + 1].astype(F32))
    pos = s[S_POS]
    for j in range(chans // 128):
        lanes = slice(128 * j, 128 * j + 128)
        high = slice(chans + 128 * j, chans + 128 * j + 128)
        gsum, bsum = total[:, lanes], total[:, high]
        mean, rstd = bn[0:1, lanes], bn[1:2, lanes]
        scale = prm[31:32, lanes] * rstd

        def grad(dep, gb, start, length):
            m = tile_mask(start, dep.shape[0], length)
            hat = (dep - mean) * rstd
            return m * scale * (gb - (bsum + hat * gsum) / count)

        for b in range(recs):
            length = s[S_LEN + b]
            pad[b, j, 0:EDGE, :] = grad(lo[0, b, :, lanes], lo[1, b, :, lanes], pos - EDGE, length)
            pad[b, j, EDGE + half :, :] = grad(hi[0, b, :, lanes], hi[1, b, :, lanes], pos + half, length)

            def step(i, _, b=b, length=length):
                r0 = pl.multiple_of(i * TILE, 8)
                v = grad(depth[b, pl.ds(r0, TILE), lanes], gbo[b, pl.ds(r0, TILE), lanes], pos + r0, length)
                pad[b, j, pl.ds(pl.multiple_of(r0 + EDGE, 8), TILE), :] = v
                gd_out[b, pl.ds(r0, TILE), lanes] = v
                return 0

            lax.fori_loop(0, half // TILE, step, 0)

            def step2(i, _, b=b, length=length):
                r0 = pl.multiple_of(i * TILE, 16)
                acc = jnp.zeros((TILE, 128), F32)
                for o in range(TAPS):
                    acc = acc + pad[b, j, pl.ds(r0 + TAPS - o, TILE), :] * prm[o : o + 1, lanes]
                acc = acc * tile_mask(pos + r0, TILE, length)
                val = proj[b, pl.ds(r0, TILE), lanes]
                g = jax.nn.sigmoid(proj[b, pl.ds(r0, TILE), high])
                gp[b, pl.ds(r0, TILE), lanes] = (acc * g).astype(BF16)
                gp[b, pl.ds(r0, TILE), high] = (acc * val * g * (1.0 - g)).astype(BF16)
                return 0

            lax.fori_loop(0, half // TILE, step2, 0)


def backward(s, depth, gbo, lo, hi, sums, bn, prm, proj):
    recs, half, chans = depth.shape
    return pl.pallas_call(
        back_body,
        in_specs=[SMEM] + [VMEM] * 8,
        out_specs=[VMEM, VMEM],
        out_shape=[sds(depth.shape, F32), sds((recs, half, 2 * chans), BF16)],
        scratch_shapes=[pltpu.VMEM((recs, chans // 128, half + 2 * EDGE, 128), F32)],
        compiler_params=LIMIT,
        cost_estimate=LONG,
        name="backward",
    )(s, depth, gbo, lo, hi, sums, bn, prm, proj)


def taps_body(gd, glu, lo, hi, gwd, pad):
    recs, half, chans = glu.shape
    fill(pad, glu, lo, hi)
    gwd[...] = jnp.zeros_like(gwd)
    for j in range(chans // 128):
        lanes = slice(128 * j, 128 * j + 128)
        accs = tuple(jnp.zeros((8, 128), F32) for _ in range(TAPS))
        for b in range(recs):

            def step(i, accs, b=b):
                r0 = pl.multiple_of(i * 16, 16)
                new = list(accs)
                for k in range(2):
                    g = gd[b, pl.ds(r0 + 8 * k, 8), lanes]
                    for o in range(TAPS):
                        new[o] = new[o] + g * pad[b, j, pl.ds(r0 + 8 * k + o + 1, 8), :]
                return tuple(new)

            accs = lax.fori_loop(0, half // 16, step, accs)
        for o in range(TAPS):
            gwd[o : o + 1, lanes] = jnp.sum(accs[o], axis=0, keepdims=True)


def taps_grad(gd, glu, lo, hi):
    recs, half, chans = glu.shape
    return pl.pallas_call(
        taps_body,
        in_specs=[VMEM] * 4,
        out_specs=VMEM,
        out_shape=sds((32, chans), F32),
        scratch_shapes=[pltpu.VMEM((recs, chans // 128, half + 2 * EDGE, 128), F32)],
        compiler_params=LIMIT,
        cost_estimate=cost(recs * half * chans * 62 * 50, recs * half * chans * 20),
        name="taps_grad",
    )(gd, glu, lo, hi)


def rows_body(gp, proj, gw, rs):
    recs, half, n2 = gp.shape
    lane = lax.broadcasted_iota(jnp.int32, (n2, 128), 1)
    row = lax.broadcasted_iota(jnp.int32, (16, n2), 0)
    total = gw[0:1, :] + gw[1:2, :]
    top = total.astype(BF16).astype(F32)
    taps = jnp.where(row == 0, top, jnp.where(row == 1, total - top, 0.0)).astype(BF16)
    pick_second = (lane == 1).astype(BF16)
    shift = gw[2:3, :] + gw[3:4, :]
    for b in range(recs):
        g = gp[b]
        one = jnp.sum(nt(g, taps), axis=1, keepdims=True)
        p = g.astype(F32) * (proj[b] - shift)
        top = p.astype(BF16)
        low = (p - top.astype(F32)).astype(BF16)
        two = jnp.dot(top, pick_second, preferred_element_type=F32) + jnp.dot(low, pick_second, preferred_element_type=F32)
        first = lax.broadcasted_iota(jnp.int32, two.shape, 1) == 0
        rs[b] = jnp.where(first, one, two)[:, 0:2]


def row_sums(gp, proj, gw):
    recs, half, n2 = gp.shape
    return pl.pallas_call(
        rows_body,
        in_specs=[VMEM] * 3,
        out_specs=VMEM,
        out_shape=sds((recs, half, 2), F32),
        compiler_params=LIMIT,
        cost_estimate=cost(recs * half * n2 * 8, recs * half * n2 * 6),
        name="row_sums",
    )(gp, proj, gw)


def through_body(gain, bias, w, out):
    def split(v):
        top = v.astype(BF16).astype(F32)
        return top, v - top

    g1, g2 = split(gain[...])
    b1, b2 = split(bias[...])
    row = lax.broadcasted_iota(jnp.int32, (16, gain.shape[1]), 0)
    v = jnp.where(row == 0, g1, jnp.where(row == 1, g2, jnp.where(row == 2, b1, jnp.where(row == 3, b2, 0.0))))
    out[...] = jnp.dot(v.astype(BF16), w[...], preferred_element_type=F32)


def through(gain, bias, w):
    return pl.pallas_call(
        through_body,
        in_specs=[VMEM] * 3,
        out_specs=VMEM,
        out_shape=sds((16, w.shape[1]), F32),
        compiler_params=LIMIT,
        cost_estimate=cost(32 * w.shape[0] * w.shape[1], 2 * w.shape[0] * w.shape[1]),
        name="through",
    )(gain[None], bias[None], w)


def turn_body(w, out, cat):
    n = w.shape[1]
    for d in range(4):
        cat[0:n, :] = w[d]
        cat[n:, :] = w[d + 4]
        out[d] = cat[...].T


def turned(w):
    n, depth = w.shape[0] // 8, w.shape[1]
    return pl.pallas_call(
        turn_body,
        in_specs=[VMEM],
        out_specs=VMEM,
        out_shape=sds((4, depth, 2 * n), BF16),
        scratch_shapes=[pltpu.VMEM((2 * n, depth), BF16)],
        compiler_params=LIMIT,
        cost_estimate=cost(32 * n * depth, 32 * n * depth),
        name="turned",
    )(w.reshape(8, n, depth))


def blocks_body(s, lhs, w, *refs, jobs, adds):
    plus, outs = refs[:adds], refs[adds:]
    half = lhs.shape[1]
    for rec, r, to, at in jobs:
        v = jnp.dot(lhs[rec], w[lax.rem(s[S_X] + r, 4)], preferred_element_type=F32)
        if adds:
            v = v + plus[to][0:half, :].astype(F32)
        outs[to][at * half : (at + 1) * half, :] = v.astype(BF16)


def blocks(s, lhs, w4, jobs, plus=()):
    recs, half, depth = lhs.shape
    n = w4.shape[2]
    each = len(jobs) // 2
    return pl.pallas_call(
        functools.partial(blocks_body, jobs=jobs, adds=len(plus)),
        in_specs=[SMEM] + [VMEM] * (2 + len(plus)),
        out_specs=[VMEM] * 2,
        out_shape=[sds((each * half, n), BF16)] * 2,
        compiler_params=LIMIT,
        cost_estimate=cost(2 * half * depth * n * len(jobs), 4 * half * depth + 8 * n * depth),
        name="blocks",
    )(s, lhs, w4, *plus)


def finish_body(s, lhs, w, up, down, last_a, last_b, keep, give):
    half = lhs.shape[1]
    n = w.shape[2] // 2
    first = s[S_YL] == 0
    for rec, (one, two) in enumerate(((last_a, down), (last_b, up))):
        v = jnp.dot(lhs[rec], w[s[S_X]], preferred_element_type=F32)
        v = v + one[...].astype(F32) + two[half:, :].astype(F32)
        low, high = v[:, :n], v[:, n:]
        keep[:, rec * n : (rec + 1) * n] = jnp.where(first, low, high)
        give[:, rec * n : (rec + 1) * n] = jnp.where(first, high, low).astype(BF16)


def finish(s, lhs, w4, parts, estimate):
    recs, half, depth = lhs.shape
    n = w4.shape[2] // 2
    return pl.pallas_call(
        finish_body,
        in_specs=[SMEM] + [VMEM] * 6,
        out_specs=[VMEM] * 2,
        out_shape=[sds((half, recs * n), F32), sds((half, recs * n), BF16)],
        compiler_params=LIMIT,
        cost_estimate=estimate,
        name="finish",
    )(s, lhs, w4, *parts)


def weights_body(own, one, two, three, g_in, g_out):
    v = own[...] + one[...].astype(F32) + two[...].astype(F32) + three[...].astype(F32)
    n = g_out.shape[1]
    g_in[:, 0, :] = v[:, :n]
    g_in[:, 1, :] = v[:, n : 2 * n]
    g_out[...] = v[:, 2 * n :]


def weights_end(own, *got):
    shard, n3 = own.shape
    return pl.pallas_call(
        weights_body,
        in_specs=[VMEM] * 4,
        out_specs=[VMEM] * 2,
        out_shape=[sds((shard, 2, n3 // 3), F32), sds((shard, n3 // 3), F32)],
        compiler_params=LIMIT,
        cost_estimate=cost(4 * shard * n3, 14 * shard * n3),
        name="weights_end",
    )(own, *got)


def params_body(got, gain, bias, taps, ln):
    v = jnp.sum(got[...], axis=0)
    taps[...] = v[:TAPS]
    t, u = v[TAPS : TAPS + 1], v[TAPS + 1 : TAPS + 2]
    ln[0:1, :] = (t - bias[...] * u) / gain[...]
    ln[1:2, :] = u


def params_end(got, gain, bias):
    n = got.shape[2]
    return pl.pallas_call(
        params_body,
        in_specs=[VMEM] * 3,
        out_specs=[VMEM] * 2,
        out_shape=[sds((TAPS, n), F32), sds((2, n), F32)],
        compiler_params=LIMIT,
        cost_estimate=cost(got.size, 4 * got.size),
        name="params_end",
    )(got, gain[None], bias[None])


def hop(v, axis, by):
    n = lax.axis_size(axis)
    return lax.ppermute(v, axis, [(i, (i + by) % n) for i in range(n)])


def sum_start(s, lhs, w8):
    sent = blocks(s, lhs, w8, ((0, 2, 0, 0), (1, 2, 1, 0), (1, 1, 0, 1), (0, 3, 1, 1)))
    return (hop(sent[0], "x", 1), hop(sent[1], "x", -1)), sent[0]


def sum_middle(s, lhs, w8, got):
    sent = blocks(s, lhs, w8, ((0, 1, 0, 0), (1, 3, 1, 0)), got)
    return (hop(sent[0], "x", 1), hop(sent[1], "x", -1)), sent[0]


def sum_end(s, lhs, w8, got, last):
    keep, give = finish(s, lhs, w8, (*got, *last), cost(0, 0))
    return keep, hop(give, "yl", 1)


def after(values, *first):
    return lax.optimization_barrier((*values, *first))[: len(values)]


def pick(block, odd):
    n = block.shape[1] // 2
    return jnp.where(odd == 1, block[:, n:].astype(F32), block[:, :n].astype(F32))


def halves(s, keep, got):
    n = keep.shape[1] // 2
    early = pl.program_id(0) == 0
    mine = jnp.where(early, keep[:, :n], keep[:, n:])
    theirs = jnp.where(early, got[:, :n].astype(F32), got[:, n:].astype(F32))
    first = s[S_YL] == 0
    return jnp.where(first, mine, theirs), jnp.where(first, theirs, mine)


def out_body(s, keep, got, fr, out):
    half = keep.shape[0]
    for h, v in enumerate(halves(s, keep, got)):
        rows = slice(h * half, h * half + half)
        out[0, :, rows] = (pick(fr[0, rows, :], s[S_ODD]) + v).T.astype(BF16)


def frames_body(s, keep, got, fr, go, stat, rs, gain, out):
    half = keep.shape[0]
    width = 8 * out.shape[1]
    for h, v in enumerate(halves(s, keep, got)):
        rows = slice(h * half, h * half + half)
        g = v * gain[...]
        mean, rstd = stat[0, rows, 0:1], stat[0, rows, 1:2]
        first, second = rs[h, 0, :, 0:1], rs[h, 0, :, 1:2]
        hat = (pick(fr[0, rows, :], s[S_ODD]) - mean) * rstd
        v = rstd * (g - first / width - hat * (second / width)) + pick(go[0, rows, :], s[S_ODD])
        out[0, :, rows] = v.T.astype(BF16)


def last_call(body, s, keep, got, wide, extra, extra_specs, name):
    recs, length, _ = wide[0].shape
    half, n = length // 2, keep.shape[1] // 2
    cols = pl.BlockSpec((1, 2 * half, 2 * n), lambda b, s: (b, 0, s[S_PAIR]))
    return pl.pallas_call(
        body,
        grid_spec=pltpu.PrefetchScalarGridSpec(
            num_scalar_prefetch=1,
            grid=(recs,),
            in_specs=[
                pl.BlockSpec((half, recs * n), lambda b, s: (0, 0)),
                pl.BlockSpec((half, recs * n), lambda b, s: (0, 0)),
            ]
            + [cols] * len(wide)
            + extra_specs,
            out_specs=pl.BlockSpec((1, n, 2 * half), lambda b, s: (b, 0, 0)),
        ),
        out_shape=sds((recs, n, 2 * half), BF16),
        compiler_params=LIMIT,
        cost_estimate=cost(recs * half * n * 20, recs * half * n * 20),
        name=name,
    )(s, keep, got, *wide, *extra).transpose(0, 2, 1)


def spread(v, axes):
    n = lax.axis_size(axes)
    return lax.all_to_all(jnp.broadcast_to(v[None], (n, *v.shape)), axes, 0, 0, tiled=True)


def on_device(frames, ln_gain, ln_bias, w_in, w_depth, bn_gain, bn_bias, w_out, lengths, grad_out):
    recs, length, width = frames.shape
    shard, _, own = w_in.shape
    half = length // 2
    chans = 2 * own
    yh, z, c, yl, x = (lax.axis_index(a) for a in ("yh", "z", "c", "yl", "x"))
    ctx = (yh * 4 + z) * 2 + c
    chan = yl * 4 + x
    time = ctx * 2 + yl
    s = jnp.stack([yl, x, chan // 2, chan % 2, time * half, lengths[0], lengths[1], z, c, yh]).astype(jnp.int32)

    w3 = jnp.concatenate([w_in.reshape(shard, 2 * own), w_out], axis=1)
    w_yl = hop(w3, "yl", 1)
    w_yh = hop(w3, "yh", 1)
    w_xx = lax.ppermute(w3, ("yh", "yl"), [(i, 3 - i) for i in range(4)])

    def paired(a, b, g0, g1):
        lo, hi = jnp.where(yl == 0, a, b), jnp.where(yl == 0, b, a)
        cols = []
        for g in range(g0, g1):
            cols += [lo[:, g * own : (g + 1) * own], hi[:, g * own : (g + 1) * own]]
        return jnp.concatenate(cols, axis=1)

    def rows_two(g0, g1):
        same, other = paired(w3, w_yl, g0, g1), paired(w_yh, w_xx, g0, g1)
        return jnp.where(yh == 0, jnp.stack([same, other]), jnp.stack([other, same]))

    def gathered(v, first):
        pieces = []
        for r in range(4):
            p = v if r == 0 else hop(v, "z", -r)
            if first is not None:
                (p,) = after([p], first)
            pieces += [p, hop(p, "c", 1)]
        return pieces

    prm1 = jnp.concatenate([w_depth, bn_gain[None], bn_bias[None], jnp.zeros((7, own), F32)], axis=0)
    prm2 = hop(prm1, "yl", 1)
    prm = jnp.where(yl == 0, jnp.concatenate([prm1, prm2], axis=1), jnp.concatenate([prm2, prm1], axis=1))
    (in_two,) = after([rows_two(0, 2)], prm2)
    normed, stat = layer_norm(s, *after([frames, ln_gain, ln_bias], in_two))
    in_pieces = gathered(in_two, normed)
    out_pieces = gathered(*after([rows_two(2, 3)], *in_pieces), None)
    proj, glu, w_in_all = project(s, normed, in_pieces, half)
    glu = glu.reshape(recs, half, chans)
    proj = proj.reshape(recs, half, 2 * chans)
    own_gain = lax.dynamic_slice_in_dim(ln_gain, chan * own, own, 0)
    own_bias = lax.dynamic_slice_in_dim(ln_bias, chan * own, own, 0)
    devices = lax.axis_size(TIME)
    up = [(i, i + 1) for i in range(devices - 1)]
    down = [(i + 1, i) for i in range(devices - 1)]
    g_lo = lax.ppermute(glu[:, half - EDGE :], TIME, up)
    g_hi = lax.ppermute(glu[:, :EDGE], TIME, down)
    gact, w_out_all = grad_act(s, grad_out, out_pieces)
    (glu_c,) = after([glu], gact)
    depth, bn_own = conv(s, glu_c, g_lo, g_hi, prm)
    bn_all = spread(bn_own, TIME).reshape(devices, 2 * chans)
    w_out_4 = turned(*after([w_out_all], bn_own))
    w_in_4 = turned(*after([w_in_all], bn_own))
    g_w = through(*after([ln_gain, ln_bias, w_in_all], bn_own))
    (gact,) = after([gact], w_out_4, w_in_4, g_w)
    act, gbo, sums_own, bn = activate(s, depth, gact, bn_all, prm)
    sums = spread(sums_own, TIME).reshape(devices, 2 * chans)
    e_lo = lax.ppermute(jnp.stack([depth[:, half - EDGE :], gbo[:, half - EDGE :]]), TIME, up)
    e_hi = lax.ppermute(jnp.stack([depth[:, :EDGE], gbo[:, :EDGE]]), TIME, down)

    out_first, sent = sum_start(s, act, w_out_4)
    depth, gbo = after([depth, gbo], sent)
    gd, gp = backward(s, depth, gbo, e_lo, e_hi, sums, bn, prm, proj)
    gn_first, sent = sum_start(s, gp, w_in_4)
    (act_m,) = after([act], sent)
    out_last, sent = sum_middle(s, act_m, w_out_4, out_first)
    (gp_r,) = after([gp], sent)
    rs = row_sums(gp_r, proj, g_w)
    (gp_w,) = after([gp], rs)
    mine, theirs, tu = weight_grads(
        s,
        normed,
        gp_w.reshape(recs * half, 2 * chans),
        grad_out,
        act.reshape(recs * half, chans),
        w_in_all,
    )
    (gp_m,) = after([gp], mine)
    gn_last, sent = sum_middle(s, gp_m, w_in_4, gn_first)
    mine, theirs = after([mine, theirs], sent)
    parts = core_sum(s, mine, hop(theirs, "c", 1))
    (gp_e,) = after([gp], parts[0])
    gn_keep, gn_got = sum_end(s, gp_e, w_in_4, gn_first, gn_last)
    gd, glu = after([gd, glu], gn_keep)
    gwd = taps_grad(gd, glu, g_lo, g_hi)
    ring = [parts[0]] + [hop(parts[r], "z", r) for r in range(1, 4)]
    g_fin, to_yl, to_yh, to_xx = ring_sum(s, ring)
    (act_e,) = after([act], gwd)
    out_keep, out_got = sum_end(s, act_e, w_out_4, out_first, out_last)

    tu = tu.T.reshape(2, 2, 4, own).transpose(1, 2, 0, 3)
    mine_x = (jnp.arange(4) == x).astype(F32)[None, :, None, None]
    taps4 = gwd[:TAPS].reshape(TAPS, 2, own).transpose(1, 0, 2)[:, None] * mine_x
    rs_rows = recs * 2 * half // own
    rs8 = jnp.broadcast_to(rs.transpose(2, 0, 1).reshape(1, 1, rs_rows, own), (2, 4, rs_rows, own))
    small = jnp.concatenate([taps4, tu, rs8], axis=2).reshape(8, TAPS + 2 + rs_rows, own)
    (small,) = after([small], g_fin)
    small = lax.all_to_all(small, CHAN, 0, 0, tiled=True)
    rs_all = jnp.sum(small[:, TAPS + 2 :].reshape(2, 4, 2, recs, half), axis=1).transpose(0, 2, 3, 1)
    small = jnp.sum(small[:, : TAPS + 2], axis=0)
    block_out = last_call(out_body, s, out_keep, out_got, [frames], [], [], "block_out")
    grad_w_depth, grad_ln = params_end(spread(small, CTX), own_gain, own_bias)

    grad_frames = last_call(
        frames_body,
        s,
        gn_keep,
        gn_got,
        [frames, grad_out],
        [stat, rs_all, own_gain[None]],
        [
            pl.BlockSpec((1, length, 2), lambda b, s: (b, 0, 0)),
            pl.BlockSpec((2, 1, half, 2), lambda b, s: (0, b, 0, 0)),
            pl.BlockSpec((1, own), lambda b, s: (0, 0)),
        ],
        "grad_frames",
    )

    grad_w_in, grad_w_out = weights_end(
        *after([g_fin], grad_frames),
        hop(to_yl, "yl", 1),
        hop(to_yh, "yh", 1),
        lax.ppermute(to_xx, ("yh", "yl"), [(i, 3 - i) for i in range(4)]),
    )

    grad_bn = lax.dynamic_index_in_dim(jnp.sum(sums, axis=0).reshape(2, 2, own), yl, 1, False)
    return (block_out, grad_frames, grad_w_in, grad_w_out, grad_w_depth, grad_bn, grad_ln)


def solution(mesh):
    split = Mesh(mesh.devices.reshape(2, 4, 2, 2, 4), ("yh", "z", "c", "yl", "x"))
    placed = (
        P(None, CTX, None),
        P(),
        P(),
        P(CTX, None, CHAN),
        P(None, CHAN),
        P(CHAN),
        P(CHAN),
        P(CTX, CHAN),
        P(),
        P(None, CTX, None),
    )
    return jax.shard_map(
        on_device,
        mesh=split,
        in_specs=placed,
        out_specs=(
            P(None, CTX, CHAN),
            P(None, CTX, CHAN),
            P(CTX, None, CHAN),
            P(CTX, CHAN),
            P(None, CHAN),
            P(None, CHAN),
            P(None, CHAN),
        ),
        check_vma=False,
    )
```
